32 devices in a mesh: dp: 8 (over z, y), mp: 4 (over x, core).
Axes of the slice: x: 2, y: 2, z: 4, core: 2. Of those that a mesh axis runs over, the one named last changes fastest.
Arguments:
- pixels: bfloat16 [64, 1024, 384], P('dp'), may hold values from -6 to 6
- meta: float32 [64, 8], P('dp'), may hold values from -6 to 6
- tags: int32 [64], P('dp'), may hold values from 0 to 6, as said below
- visible: int32 [64, 256], P('dp'), may hold values from 0 to 1023, as said below
- wavelength: float32 [7, 6], replicated, may hold values from 0.4 to 12
- w_hyp: float32 [128, 128], replicated, may hold values from -0.5 to 0.5
- b_hyp: float32 [128], replicated, may hold values from -3 to 3
- w_kernel: bfloat16 [128, 64, 768], P(None, 'dp', 'mp'), may hold values from -0.0390625 to 0.0390625
- w_meta: float32 [8, 768], P(None, 'mp'), may hold values from -2 to 2
- cls_token: float32 [768], P('mp'), may hold values from -6 to 6
- ln1_gain: float32 [768], P('mp'), may hold values from 0.5 to 1.5
- ln1_bias: float32 [768], P('mp'), may hold values from -2 to 2
- w_qkv: bfloat16 [768, 3, 768], P(None, None, 'mp'), may hold values from -0.21875 to 0.21875
- b_qv: float32 [2, 768], P(None, 'mp'), may hold values from -2 to 2
- w_out: bfloat16 [768, 768], P('mp'), may hold values from -0.75 to 0.75
- b_out: float32 [768], P('mp'), may hold values from -2 to 2
- ln2_gain: float32 [768], P('mp'), may hold values from 0.5 to 1.5
- ln2_bias: float32 [768], P('mp'), may hold values from -2 to 2
- w_up: bfloat16 [768, 3072], P(None, 'mp'), may hold values from -0.21875 to 0.21875
- b_up: float32 [3072], P('mp'), may hold values from -3 to 3
- w_down: bfloat16 [3072, 768], P('mp'), may hold values from -0.15625 to 0.15625
- b_down: float32 [768], P('mp'), may hold values from -2 to 2
- cotangent: bfloat16 [64, 258, 768], P('dp', None, 'mp'), may hold values from -6 to 6
Outputs:
- encoded: bfloat16 [64, 258, 768], P('dp', None, 'mp')
- pixel_grad: bfloat16 [64, 256, 384], P('dp', None, 'mp')
- grad_w_hyp: float32 [128, 128], replicated
- grad_b_hyp: float32 [128], replicated
- grad_w_kernel: float32 [128, 64, 768], P(None, 'dp', 'mp')
- grad_w_meta: float32 [8, 768], P(None, 'mp')
- grad_cls: float32 [768], P('mp')
- grad_ln1_gain: float32 [768], P('mp')
- grad_ln1_bias: float32 [768], P('mp')
- grad_w_qkv: float32 [768, 3, 768], P(None, None, 'mp')
- grad_b_qv: float32 [2, 768], P(None, 'mp')
- grad_w_out: float32 [768, 768], P('mp')
- grad_b_out: float32 [768], P('mp')
- grad_ln2_gain: float32 [768], P('mp')
- grad_ln2_bias: float32 [768], P('mp')
- grad_w_up: float32 [768, 3072], P(None, 'mp')
- grad_b_up: float32 [3072], P('mp')
- grad_w_down: float32 [3072, 768], P('mp')
- grad_b_down: float32 [768], P('mp')
The draws below stay inside these ranges and needn't reach their ends.
Inputs may be any that keep to these rules, and one draw needn't show every extreme that they name: tags never fall from one chip to the next; every sensor has at least one chip. `visible`: each chip's indices are distinct and increasing.
All inputs are finite; a program needn't handle non-finite values.
Results may differ from the reference program's by a relative error of at most 0.025.
Values may be sent and summed in bfloat16 or wider, within the bound.
A program may use at most 192 MiB of HBM per device.

```python
import math
import jax
import jax.numpy as jnp
from jax import lax

D = 768
HEADS = 12
HD = 64
FF = 3072
HYP = 128
PIX = 64
BANDS = 6
NSENS = 7
NPATCH = 1024
VIS = 256
MET = 8
CHIPS_DEV = 8
CHIPS = 64
N_DP = 8


def draw_tags(key, part):
    key = jax.random.fold_in(key, 11)
    dice_rolls = jax.random.randint(key, (CHIPS,), 0, NSENS * NSENS)
    levels = jnp.arange(1, NSENS, dtype=jnp.int32)
    sensor_tag = jnp.sum((dice_rolls[:, None] >= levels[None, :] * levels[None, :]).astype(jnp.int32), axis=1)
    sensor_tag = sensor_tag.at[:NSENS].set(jnp.arange(NSENS, dtype=jnp.int32))
    return jnp.sort(sensor_tag).astype(jnp.int32)


def draw_visible(key, part):
    key = jax.random.fold_in(key, 23)
    chip_keys = jax.random.split(key, CHIPS)

    def draw_chip(chip_key):
        return jnp.sort(jax.random.permutation(chip_key, NPATCH)[:VIS]).astype(jnp.int32)
    picked = jax.vmap(draw_chip)(chip_keys)
    picked = picked.at[0, 0].set(0)
    picked = picked.at[0, VIS - 1].set(NPATCH - 1)
    return picked.astype(jnp.int32)


def level_of(stream_key, shape, pieces, smallest, top_value):
    def one(axis_at, shards_of):
        steps = jax.random.uniform(jax.random.fold_in(jax.random.fold_in(stream_key, 6), axis_at), (shards_of,), jnp.float32, smallest / len(pieces), top_value / len(pieces))
        return jnp.repeat(jnp.exp(steps), shape[axis_at] // shards_of).reshape((-1,) + (1,) * (len(shape) - axis_at - 1))

    gain = one(*pieces[0])
    for cut in pieces[1:]:
        gain = gain * one(*cut)
    return gain


def centred(key, extent, scale, reach, shards=(), kind=jnp.bfloat16):
    factor_of = level_of(key, extent, shards, -0.22, 0.18) if shards else 1.0
    drawn = jax.random.normal(key, extent, jnp.float32) * scale * factor_of
    return jnp.minimum(jnp.maximum(drawn, -reach), reach).astype(kind)


def setup_inputs(seed: int = 0) -> dict:
    seeds = jax.random.split(jax.random.key(seed), 24)
    pixels = centred(seeds[0], (CHIPS, NPATCH, BANDS * PIX), 1.0, 6.0, ((0, 8),))
    meta = centred(seeds[1], (CHIPS, MET), 1.0, 6.0, ((0, 8),), jnp.float32)
    tags = draw_tags(jax.random.fold_in(seeds[23], 71), 0)
    visible = draw_visible(jax.random.fold_in(seeds[23], 71), 0)
    wavelength = jnp.clip(jnp.exp(jax.random.uniform(seeds[4], (NSENS, BANDS), jnp.float32, math.log(0.4), math.log(12.0))), 0.4, 12.0)
    w_hyp = centred(seeds[5], (HYP, HYP), HYP ** -0.5, 0.5, (), jnp.float32)
    b_hyp = centred(seeds[6], (HYP,), 0.5, 3.0, (), jnp.float32)
    w_kernel = centred(seeds[7], (HYP, PIX, D), (HYP * BANDS * PIX // 2) ** -0.5, 0.0390625, ((1, 8), (2, 4)))
    w_meta = centred(seeds[8], (MET, D), MET ** -0.5, 2.0, ((1, 4),), jnp.float32)
    cls_token = centred(seeds[9], (D,), 1.0, 6.0, ((0, 4),), jnp.float32)
    ln1_gain = jnp.clip(1.0 + 0.1 * jax.random.normal(seeds[10], (D,), jnp.float32), 0.5, 1.5)
    ln1_bias = centred(seeds[11], (D,), 0.3, 2.0, ((0, 4),), jnp.float32)
    w_qkv = centred(seeds[12], (D, 3, D), D ** -0.5, 0.21875, ((2, 4),))
    b_qv = centred(seeds[13], (2, D), 0.3, 2.0, ((1, 4),), jnp.float32)
    w_out = centred(seeds[14], (D, D), HD ** -0.5, 0.75, ((0, 4),))
    b_out = centred(seeds[15], (D,), 0.3, 2.0, ((0, 4),), jnp.float32)
    ln2_gain = jnp.clip(1.0 + 0.1 * jax.random.normal(seeds[16], (D,), jnp.float32), 0.5, 1.5)
    ln2_bias = centred(seeds[17], (D,), 0.3, 2.0, ((0, 4),), jnp.float32)
    w_up = centred(seeds[18], (D, FF), D ** -0.5, 0.21875, ((1, 4),))
    b_up = centred(seeds[19], (FF,), 0.5, 3.0, ((0, 4),), jnp.float32)
    w_down = centred(seeds[20], (FF, D), (FF // 2) ** -0.5, 0.15625, ((0, 4),))
    b_down = centred(seeds[21], (D,), 0.3, 2.0, ((0, 4),), jnp.float32)
    cotangent = centred(seeds[22], (CHIPS, VIS + 2, D), 1.0, 6.0, ((0, 8), (2, 4)))
    return dict(pixels=pixels, meta=meta, tags=tags, visible=visible, wavelength=wavelength, w_hyp=w_hyp, b_hyp=b_hyp, w_kernel=w_kernel, w_meta=w_meta, cls_token=cls_token, ln1_gain=ln1_gain, ln1_bias=ln1_bias, w_qkv=w_qkv, b_qv=b_qv, w_out=w_out, b_out=b_out, ln2_gain=ln2_gain, ln2_bias=ln2_bias, w_up=w_up, b_up=b_up, w_down=w_down, b_down=b_down, cotangent=cotangent)


@jax.custom_vjp
def low(v):
    return lax.optimization_barrier(v.astype(jnp.bfloat16)).astype(jnp.float32)

@jax.custom_vjp
def low_back(v):
    return v

def low_keep(v):
    return (low(v), None)

def low_pass(kept, grad):
    return (grad,)

def back_keep(v):
    return (v, None)

def back_low(kept, grad):
    return (low(grad),)
low.defvjp(low_keep, low_pass)
low_back.defvjp(back_keep, back_low)
norm_epsilon = 1e-05
highest = lax.Precision.HIGHEST

def wave_code(wavelength):
    half_width = HYP // 2
    ladder = jnp.arange(half_width, dtype=jnp.float32) * (math.log(100.0) / half_width)
    angle_grid = wavelength[..., None] * jnp.exp(ladder)
    return jnp.concatenate([jnp.sin(angle_grid), jnp.cos(angle_grid)], axis=-1)

def pos_code(chip_index, feature):
    rate_grid = jnp.exp((feature // 2).astype(jnp.float32) * (-2.0 * math.log(10000.0) / D))
    angle_grid = chip_index[..., None].astype(jnp.float32) * rate_grid
    return jnp.where(feature % 2 == 0, jnp.sin(angle_grid), jnp.cos(angle_grid))

def layer_norm(field_rows, gain_row, bias_row):
    center = lax.optimization_barrier(jnp.mean(field_rows, axis=-1, keepdims=True))
    square = lax.optimization_barrier(jnp.mean(field_rows * field_rows, axis=-1, keepdims=True))
    scaled = (field_rows - center) * lax.rsqrt(square - center * center + norm_epsilon)
    return scaled * gain_row + bias_row

def pick_rows(chip_pixels, chip_index):
    return chip_pixels[chip_index]

def layer_forward(params, patches, meta_rows, tag_rows, visible_rows, wavelength):
    w_hyp, b_hyp, w_kernel, w_meta, cls_token, ln1_gain, ln1_bias, w_qkv, b_qv, w_out, b_out, ln2_gain, ln2_bias, w_up, b_up, w_down, b_down = params
    chip_count = patches.shape[0]
    wave_hidden = low(jax.nn.gelu(jnp.einsum('sbi,ij->sbj', wave_code(wavelength), w_hyp, precision=highest) + b_hyp))
    kernel = low(jnp.einsum('sbj,jpf->sbpf', wave_hidden, w_kernel, precision=highest))
    kernel = kernel.reshape(NSENS, BANDS * PIX, D)
    select = (tag_rows[:, None] == jnp.arange(NSENS, dtype=jnp.int32)[None, :]).astype(jnp.float32)
    chip_kernel = jnp.einsum('cs,skf->ckf', select, kernel, precision=highest)
    tokens = jnp.einsum('cvk,ckf->cvf', patches, chip_kernel, precision=highest)
    tokens = low_back(tokens + pos_code(visible_rows, jnp.arange(D, dtype=jnp.int32)))
    meta_token = jnp.dot(meta_rows, w_meta, precision=highest)
    first_token = jnp.broadcast_to(cls_token, (chip_count, 1, D))
    start_rows = jnp.concatenate([first_token, meta_token[:, None, :], tokens], axis=1)
    length = start_rows.shape[1]
    normed_one = low(layer_norm(start_rows, ln1_gain, ln1_bias))
    projected = jnp.einsum('cld,dte->clte', normed_one, w_qkv, precision=highest)
    queries = low_back(low(projected[:, :, 0] + b_qv[0]))
    key_rows = low_back(low(projected[:, :, 1]))
    value_rows = low_back(low(projected[:, :, 2] + b_qv[1]))

    def split_heads(field_rows):
        return field_rows.reshape(chip_count, length, HEADS, HD)
    scores = jnp.einsum('cqhe,ckhe->chqk', split_heads(queries), split_heads(key_rows), precision=highest) / math.sqrt(HD)
    scores = low_back(scores)
    weights = low(jax.nn.softmax(scores, axis=-1))
    attended = jnp.einsum('chqk,ckhe->cqhe', weights, split_heads(value_rows), precision=highest)
    attended = low_back(low(attended.reshape(chip_count, length, D)))
    branch = low_back(jnp.einsum('cld,de->cle', attended, w_out, precision=highest) + b_out)
    middle = start_rows + branch
    normed_two = low(layer_norm(middle, ln2_gain, ln2_bias))
    hidden = low_back(jnp.einsum('cld,df->clf', normed_two, w_up, precision=highest) + b_up)
    activated = low(jax.nn.gelu(hidden))
    mlp_out = low_back(jnp.einsum('clf,fd->cld', activated, w_down, precision=highest) + b_down)
    return middle + mlp_out

def reference(pixels, meta, tags, visible, wavelength, w_hyp, b_hyp, w_kernel, w_meta, cls_token, ln1_gain, ln1_bias, w_qkv, b_qv, w_out, b_out, ln2_gain, ln2_bias, w_up, b_up, w_down, b_down, cotangent):
    params = tuple((weight_item.astype(jnp.float32) for weight_item in (w_hyp, b_hyp, w_kernel, w_meta, cls_token, ln1_gain, ln1_bias, w_qkv, b_qv, w_out, b_out, ln2_gain, ln2_bias, w_up, b_up, w_down, b_down)))
    chosen = jax.vmap(pick_rows)(pixels, visible)

    def blocks(field_rows):
        return field_rows.reshape((N_DP, CHIPS_DEV) + field_rows.shape[1:])

    def one_block(running, block_data):
        chip_pixels, chip_meta, chip_tags, chip_visible, chip_cot = block_data

        def forward(param_in, pixel_in):
            return layer_forward(param_in, pixel_in, chip_meta, chip_tags, chip_visible, wavelength)
        output, pullback = jax.vjp(forward, params, chip_pixels.astype(jnp.float32))
        param_grads, pixel_part = pullback(chip_cot.astype(jnp.float32))
        running = jax.tree.map(jnp.add, running, param_grads)
        return (running, (output.astype(jnp.bfloat16), pixel_part.astype(jnp.bfloat16)))
    zero_grads = jax.tree.map(jnp.zeros_like, params)
    running, outputs = lax.scan(one_block, zero_grads, (blocks(chosen), blocks(meta), blocks(tags), blocks(visible), blocks(cotangent)))
    encoded = outputs[0].reshape(CHIPS, VIS + 2, D)
    pixel_grad = outputs[1].reshape(CHIPS, VIS, BANDS * PIX)
    return (encoded, pixel_grad, running[0], running[1], running[2], running[3], running[4], running[5], running[6], running[7], running[8], running[9], running[10], running[11], running[12], running[13], running[14], running[15], running[16])
```

```python
import functools
import itertools
import math

import jax
import jax.numpy as jnp
import numpy as np
from jax import lax
from jax.experimental import pallas as pl
from jax.experimental.pallas import tpu as pltpu
from jax.sharding import PartitionSpec as P

HD = 64
HYP = 128
LANES = 128
TILE = 256
ROW_TILE = 16

norm_epsilon = 1e-05
highest = lax.Precision.HIGHEST
f32 = jnp.float32
bf16 = jnp.bfloat16
VMEM_LIMIT = 58 * 1024 * 1024
MESH = pl.DeviceIdType.MESH

ROW_META = 0
ROW_CLS = 8
ROW_LN1_GAIN = 9
ROW_LN1_BIAS = 10
ROW_BQ = 11
ROW_BV = 12
ROW_B_OUT = 13
ROW_LN2_GAIN = 14
ROW_LN2_BIAS = 15
ROW_B_DOWN = 16
ROW_B_UP = 17
SMALL_ROWS = 24


def wave_code(wavelength):
    half_width = HYP // 2
    ladder = jnp.arange(half_width, dtype=f32) * (math.log(100.0) / half_width)
    angle_grid = wavelength[..., None] * jnp.exp(ladder)
    return jnp.concatenate([jnp.sin(angle_grid), jnp.cos(angle_grid)], axis=-1)


def pos_table(patch_count, width):
    index = np.arange(patch_count, dtype=np.float64)[:, None]
    feature = np.arange(width)[None, :]
    angle = index * np.exp((feature // 2) * (-2.0 * math.log(10000.0) / width))
    table = np.where(feature % 2 == 0, np.sin(angle), np.cos(angle)).astype(np.float32)
    return table.astype(jnp.bfloat16)


def nn_dot(left, right):
    return lax.dot_general(left, right, (((1,), (0,)), ((), ())), preferred_element_type=f32)


def nt_dot(left, right):
    return lax.dot_general(left, right, (((1,), (1,)), ((), ())), preferred_element_type=f32)


def tn_dot(left, right):
    return lax.dot_general(left, right, (((0,), (0,)), ((), ())), preferred_element_type=f32)


def gelu_pair(u):
    c = math.sqrt(2.0 / math.pi)
    square = u * u
    t = jnp.tanh(c * u * (1.0 + 0.044715 * square))
    half = 0.5 * (1.0 + t)
    slope = half + 0.5 * u * (1.0 - t * t) * (c * (1.0 + 3.0 * 0.044715 * square))
    return u * half, slope


def norm_stats(x):
    width = x.shape[1]
    center = jnp.sum(x, axis=1, keepdims=True) * (1.0 / width)
    square = jnp.sum(x * x, axis=1, keepdims=True) * (1.0 / width)
    inverse = lax.rsqrt(square - center * center + norm_epsilon)
    return (x - center) * inverse, inverse


def hot_rows(index, count):
    lane = lax.broadcasted_iota(jnp.int32, (index.shape[0], count), 1)
    return jnp.where(index == lane, 1.0, 0.0).astype(bf16)


def norm_back(grad, gain, scaled, inverse):
    width = grad.shape[1]
    weighted = grad * gain
    first = jnp.sum(weighted, axis=1, keepdims=True) * (1.0 / width)
    second = jnp.sum(weighted * scaled, axis=1, keepdims=True) * (1.0 / width)
    return inverse * (weighted - first - scaled * second)


def column_sum(x):
    return jnp.sum(x, axis=0, keepdims=True)


class Flow:
    def __init__(self, clock, steps, ready):
        self.clock, self.steps, self.next, self.ready = clock, steps, 0, ready

    @property
    def open(self):
        return self.next < len(self.steps)

    def due(self):
        _, link, _ = self.steps[self.next]
        return max(self.ready, self.clock.busy.get(link, 0.0) - self.clock.slack)

    def go(self):
        action, link, cost = self.steps[self.next]
        clock = self.clock
        clock.now = max(clock.now, self.ready)
        action()
        self.next += 1
        clock.now += clock.start
        begin = max(clock.now, clock.busy.get(link, 0.0))
        if link is not None:
            clock.busy[link] = begin + cost
        self.ready = begin + cost + clock.latency


class Clock:
    latency, slack, start = 1.5, 6.0, 0.3

    def __init__(self):
        self.now, self.busy, self.flows = 0.0, {}, []

    def add(self, steps, at=None):
        flow = Flow(self, steps, self.now if at is None else at)
        self.flows.append(flow)
        if at is None:
            flow.go()
        return flow

    def ensure(self, flow, count):
        if not flow.next:
            flow.ready = min(flow.ready, self.now)
        while flow.next < count:
            flow.go()

    def work(self, cost):
        self.now += cost
        self.pump()

    def pump(self):
        while True:
            due = [f for f in self.flows if f.open and f.due() <= self.now]
            if not due:
                return
            min(due, key=Flow.due).go()

    def drain(self):
        while True:
            left = [f for f in self.flows if f.open]
            if not left:
                return
            flow = min(left, key=Flow.due)
            self.now = max(self.now, flow.due())
            flow.go()


class Refs:
    def __init__(self, names, refs):
        self.named = dict(zip(names, refs, strict=True))

    def __getattr__(self, name):
        return self.named[name]

    def __getitem__(self, number):
        return self.named[number]


KERNEL, WIDE, UP = 0, 100, 200
ACROSS = -1


def order_of(dp_bits, late):
    if late:
        return [1, ACROSS, 0, *range(2, dp_bits)]
    return [ACROSS, *range(dp_bits)]


class Bag:
    pass


RATE = 0.05
PAIR_RATE = 0.3
LATE_WIDE, LATE_UP = (), ()
UP_BITS, DOWN_BITS = (0, 1), (0,)
HOLD = 18.0
UP_AT = 8.0
SENSORS_AT = 1
PIXELS_AT = 1
KERNEL_ORDER = (1, 0, 2)
LINK_CORE, LINK_X, LINK_Y, LINK_Z, LINK_SMALL = range(5)


def layer_kernel(names, length, dp_bits, inside, *refs):
    r = Refs(names, refs)
    halves = min(3, dp_bits)
    rows, width = r.index.shape[0], r.start.shape[1]
    chips, patches, depth = r.pixels.shape
    blocks = r.wup.shape[0]
    images = chips // blocks
    block = width // blocks
    tiles = width // TILE
    pairs = width // LANES
    steps_count = images * pairs

    mp, dp = lax.axis_index("mp"), lax.axis_index("dp")
    core_bit, x_bit = mp % 2, mp // 2
    core_mp, x_mp = mp + 1 - 2 * core_bit, mp + 2 - 4 * x_bit
    far_mp = blocks - 1 - mp
    dp_bit = [(dp // (1 << b)) % 2 for b in range(dp_bits)]

    def flip(*bits):
        value = dp
        for b in bits:
            value = value + (1 - 2 * dp_bit[b]) * (1 << b)
        return value

    core, across_x, diagonal = {"mp": core_mp}, {"mp": x_mp}, {"mp": far_mp}
    bit_peer = [{"dp": flip(b)} for b in range(dp_bits)]
    peers = [core, across_x, *bit_peer]
    others = [(core, core_mp), (across_x, x_mp), (diagonal, far_mp)]
    greeted = peers + [diagonal]
    if inside:
        mixed = [{"dp": flip(*bits)} for bits in ((0, 1), (0, 2), (1, 2), (0, 1, 2))]
        greeted += mixed

    barrier = pltpu.get_barrier_semaphore()
    for peer in greeted:
        pl.semaphore_signal(barrier, inc=1, device_id=peer, device_id_type=MESH)
    pl.semaphore_wait(barrier, len(greeted))

    sent, numbers, local_numbers = [], itertools.count(), itertools.count()

    def push(source, target, peer):
        number = next(numbers)
        copy = pltpu.make_async_remote_copy(
            src_ref=source,
            dst_ref=target,
            send_sem=r.send_sems.at[number],
            recv_sem=r.recv_sems.at[number],
            device_id=peer,
            device_id_type=MESH,
        )
        copy.start()
        sent.append(copy)
        return copy

    def left(copy):
        copy.wait_send()
        sent[:] = [c for c in sent if c is not copy]

    def carry_local(source, target):
        copy = pltpu.make_async_copy(source, target, r.local_sems.at[next(local_numbers)])
        copy.start()
        return copy

    def mul16(value):
        return pl.multiple_of(value, ROW_TILE)

    def tile_at(j):
        return pl.ds(pl.multiple_of(j * TILE, TILE), TILE)

    def span_at(i):
        return pl.ds(i * rows, rows)

    def small(row):
        return r.small[row : row + 1, :]

    clock = Clock()

    if inside:
        place = dp // 2
        r.kernels_near[place] = r.piece[...]
        sideways = bit_peer[0]
        direct = push(r.piece, r.kernels_far.at[place], sideways)
        along = []
        for peer, bits in ((bit_peer[1], (1,)), (mixed[2], (1, 2)), (bit_peer[2], (2,))):
            along.append((push(r.piece, r.kernels_near.at[place], peer), flip(*bits) // 2))
        passed = []

        def pass_on(n):
            copy, index = along[n]
            copy.wait_recv()
            passed.append(push(r.kernels_near.at[index], r.kernels_far.at[index], sideways))

        amount = 0.172
        gather_steps = [
            (lambda: None, LINK_Z, amount / RATE),
            (lambda: pass_on(0), LINK_Y, amount * 1.5 / RATE),
            (lambda: pass_on(1), LINK_Y, amount * 1.5 / RATE),
        ]

        def halfway():
            pass_on(2)

        gather_steps.append((halfway, LINK_Y, amount / RATE))

        def gather_end():
            direct.wait_recv()
            for copy in passed:
                copy.wait_recv()

        gather_steps.append((gather_end, None, 0.0))
        gather_flow = clock.add(gather_steps)

    r.narrow[...] = jnp.zeros_like(r.narrow)
    row = 0
    for part in (r.w_meta, r.cls, r.gain_one, r.bias_one, r.b_qv, r.b_out, r.gain_two, r.bias_two):
        r.narrow[row : row + part.shape[0], :] = part[...]
        row += part.shape[0]
    r.narrow[row : row + 1, :] = r.b_down[...]
    r.bias_up[...] = jnp.broadcast_to(r.b_up[...], r.bias_up.shape)
    narrow_copies = []
    for peer, _ in others:
        narrow_copies.append(push(r.narrow, r.narrow_all.at[mp], peer))
        narrow_copies.append(push(r.bias_up, r.bias_all.at[mp], peer))
    r.narrow_all[mp] = r.narrow[...]
    r.bias_all[mp] = r.bias_up[...]

    def weight_flow(shard, full, inner, bits, at=None):
        parts = 1 << len(bits)
        high = block if inner else shard.shape[0]
        lead = (slice(None),) if len(shard.shape) == 3 else ()

        def view(m, first, count):
            place = pl.ds(mul16(first * (high // parts)), count * (high // parts))
            if inner:
                place = pl.ds(
                    mul16(m * block + first * (high // parts)), count * (high // parts)
                )
                return full.at[(*lead, place)]
            return full.at[m, place, :]

        state = Bag()
        first = 0
        for n, b in enumerate(bits):
            first = first + dp_bit[b] * (1 << n)
        state.hands = []

        def begin():
            own = shard.at[(*lead, pl.ds(mul16(first * (high // parts)), high // parts))]
            state.local = carry_local(shard, view(mp, 0, parts))
            state.copy = push(own, view(mp, first, 1), across_x)

        state.hands.append(push(shard, view(mp, 0, parts), core))

        def held(n):
            start = 0
            for k in range(n, len(bits)):
                start = start + dp_bit[bits[k]] * (1 << k)
            return start, 1 << n

        def came(n):
            start, count = held(n)
            if n:
                count //= 2
                start = start + (1 - dp_bit[bits[n - 1]]) * count
            return start, count

        def relay(n):
            state.copy.wait_recv()
            if n < len(bits):
                piece = view(x_mp, *held(n))
                state.next = push(piece, piece, bit_peer[bits[n]])
            piece = view(x_mp, *came(n))
            state.hands.append(push(piece, piece, core))
            if n < len(bits):
                state.copy = state.next

        def end():
            state.local.wait()
            for copy in state.hands:
                copy.wait_recv()

        cost = math.prod(shard.shape) * 2 / parts / 1e6
        steps = [(begin, LINK_X, cost / RATE)]
        for n in range(len(bits)):
            link = LINK_Z if bits[n] else LINK_Y
            steps.append((lambda n=n: relay(n), link, cost * (1 << n) / RATE))
        steps.append((lambda: relay(len(bits)), LINK_CORE, cost * parts / 2 / PAIR_RATE))
        steps.append((end, None, 0.0))
        return clock.add(steps, at=at)

    qkv_flow = weight_flow(r.wqkv_shard, r.wqkv, True, (0,))
    out_flow = weight_flow(r.wout_shard, r.wout, True, (0,))
    up_weight = weight_flow(r.wup_shard, r.wup, False, UP_BITS, at=UP_AT)
    down_weight = weight_flow(r.wdown_shard, r.wdown, False, DOWN_BITS, at=1000.0)
    qkv_flow.ready = out_flow.ready = HOLD

    state = Bag()

    def grad_begin():
        state.grad = [push(r.grad_blocks.at[m], r.grad_recv.at[mp], p) for p, m in others]
        state.grad_own = carry_local(r.grad_blocks.at[mp], r.grad_recv.at[mp])

    def grad_end():
        state.grad_own.wait()
        for copy in state.grad:
            copy.wait_recv()
        for i in range(images):
            r.grad[span_at(i), :] = jnp.concatenate(
                [r.grad_recv[m][:, i * block : (i + 1) * block] for m in range(blocks)], axis=1
            )

    table_copies = []
    for k in range(patches // TILE):
        table_copies.append(
            carry_local(r.table.at[k * TILE : (k + 1) * TILE], r.work_wide.at[0, k // 2, k % 2])
        )

    def pixel_copies(c):
        lanes = slice((c % 2) * depth, (c % 2 + 1) * depth)
        return [
            pltpu.make_async_copy(
                r.pixels.at[c, k * TILE : (k + 1) * TILE],
                r.work_wide.at[1, k // 2, k % 2, :, lanes],
                r.pixel_sems.at[c % 2, k],
            )
            for k in range(patches // TILE)
        ]

    for copy in pixel_copies(0):
        copy.start()
    for c in range(chips):
        if c + 1 < chips:
            for copy in pixel_copies(c + 1):
                copy.start()
        for copy in pixel_copies(c):
            copy.wait()
        hot = hot_rows(r.index[:, c : c + 1], patches)
        lanes = slice((c % 2) * depth, (c % 2 + 1) * depth)
        value = 0.0
        for k in range(patches // TILE):
            value = value + nn_dot(
                hot[:, k * TILE : (k + 1) * TILE], r.work_wide[1, k // 2, k % 2, :, lanes]
            )
        r.chosen[c] = value.astype(bf16)
        clock.work(0.7)

    for copy in narrow_copies:
        copy.wait_recv()
    r.small[...] = jnp.concatenate([r.narrow_all[m] for m in range(blocks)], axis=1)
    for m in range(blocks):
        r.small[ROW_B_UP + m : ROW_B_UP + m + 1, :] = r.bias_all[m, 0:1, :]

    for copy in table_copies:
        copy.wait()
    chip_lane = lax.broadcasted_iota(jnp.int32, (rows, chips), 1)
    index_wide = r.index[...].astype(f32)
    for i in range(images):
        mine = jnp.where(chip_lane == mp * images + i, index_wide, 0.0)
        hot = hot_rows(jnp.sum(mine, axis=1, keepdims=True).astype(jnp.int32), patches)
        value = 0.0
        for k in range(patches // TILE):
            value = value + nn_dot(
                hot[:, k * TILE : (k + 1) * TILE], r.work_wide[0, k // 2, k % 2]
            )
        r.start[span_at(i), :] = value
        token = jnp.zeros((1, width), f32)
        for k in range(r.meta.shape[1]):
            token = token + r.meta[mp * images + i, k] * small(ROW_META + k)
        line = lax.broadcasted_iota(jnp.int32, (8, width), 0)
        r.start[pl.ds(i * rows, 8), :] += jnp.where(
            line == 0, small(ROW_CLS), jnp.where(line == 1, token, 0.0)
        )
        clock.work(1.0)

    clock.ensure(up_weight, 1)
    if inside:
        sensors, piece_rows = r.piece.shape[0], r.piece.shape[1]
        slots = 1 << dp_bits
        pixels_each = r.w_kernel.shape[1]
        bands = piece_rows // pixels_each
        patch_copies = []

        def patch_half(kernels, side):
            for m in range(blocks):
                pair = []
                for i in range(images):
                    tag = r.tags[m * images + i]
                    parts = [kernels[k, tag] for k in range(slots // 2)]
                    pair.append(jnp.concatenate(parts, axis=0))
                r.patch_send[m, side] = jnp.concatenate(pair, axis=1)
            for peer, m in others:
                spot = r.patch_recv.at[mp, side]
                patch_copies.append(push(r.patch_send.at[m, side], spot, peer))
            r.patch_recv[mp, side] = r.patch_send[mp, side]

        def patch_far():
            clock.ensure(gather_flow, 5)
            patch_half(r.kernels_far, 1 - dp_bit[0])

        def patch_end():
            for copy in patch_copies:
                copy.wait_recv()

        clock.ensure(gather_flow, 4)
        patch_flow = clock.add(
            [
                (lambda: patch_half(r.kernels_near, dp_bit[0]), LINK_X, 0.295 / RATE),
                (patch_far, LINK_X, 0.295 / RATE),
                (patch_end, None, 0.0),
            ]
        )
        clock.now += 0.7
        clock.ensure(patch_flow, 2)
        clock.now += 0.7
        clock.ensure(qkv_flow, 2)
        clock.ensure(out_flow, 2)
        clock.ensure(patch_flow, 3)
        for i in range(images):
            side_rows = []
            for side in range(2):
                part = [
                    r.patch_recv[m, side, :, i * block : (i + 1) * block] for m in range(blocks)
                ]
                side_rows.append(jnp.concatenate(part, axis=1).astype(f32))
            strips = []
            for b in range(bands):
                for d in range(slots):
                    first = (d // 2 * bands + b) * pixels_each
                    strips.append(side_rows[d % 2][first : first + pixels_each])
            r.patch[i] = jnp.concatenate(strips, axis=0).astype(bf16)
    clock.ensure(down_weight, 1)
    grad_flow = clock.add(
        [(grad_begin, LINK_X, 0.42 / RATE), (grad_end, None, 0.0)], at=clock.now + 8.0
    )

    for i in range(images):
        value = r.start[span_at(i), :] + nn_dot(r.chosen[mp * images + i], r.patch[i])
        r.start[span_at(i), :] = value
        scaled, _ = norm_stats(value)
        r.normed_one[span_at(i), :] = (
            scaled * small(ROW_LN1_GAIN) + small(ROW_LN1_BIAS)
        ).astype(bf16)
        clock.work(1.0)

    clock.ensure(qkv_flow, 4)
    for t in range(3):

        def project(j, carry, t=t):
            cols = tile_at(j)
            value = nt_dot(r.normed_one[...], r.wqkv[t, cols, :])
            if t == 0:
                value = value + r.small[ROW_BQ : ROW_BQ + 1, cols]
                value = value.astype(bf16).astype(f32) * (1.0 / math.sqrt(HD))
            if t == 2:
                value = value + r.small[ROW_BV : ROW_BV + 1, cols]
            r.qkv[t, :, cols] = value.astype(bf16)
            return carry

        lax.fori_loop(0, tiles, project, 0)
        clock.work(1.5)

    lane = lax.broadcasted_iota(jnp.int32, (1, LANES), 1)
    key_lane = lax.broadcasted_iota(jnp.int32, (1, rows), 1)

    def soft_copy(step, out):
        slot = step % 2
        near, distant = r.soft_slots.at[slot], r.soft.at[step]
        if out:
            return pltpu.make_async_copy(near, distant, r.soft_sems.at[0, slot])
        return pltpu.make_async_copy(distant, near, r.soft_sems.at[1, slot])

    def attend(step, carry):
        image = step // pairs
        pair = step % pairs
        span = pl.ds(mul16(image * rows), rows)
        cols = pl.ds(pl.multiple_of(pair * LANES, LANES), LANES)
        q, k, v = r.qkv[0, span, cols], r.qkv[1, span, cols], r.qkv[2, span, cols]

        @pl.when(step >= 2)
        def _():
            soft_copy(step - 2, True).wait()

        parts = []
        for h in range(2):
            mine = (lane >= HD) if h else (lane < HD)
            scores = nt_dot(jnp.where(mine, q, jnp.zeros_like(q)), k)
            scores = jnp.where(key_lane < length, scores, -1e30)
            top = jnp.max(scores, axis=1, keepdims=True)
            power = jnp.exp(scores - top)
            soft = power * (1.0 / jnp.sum(power, axis=1, keepdims=True))
            soft = soft.astype(bf16)
            r.soft_slots[step % 2, h] = soft
            parts.append(nn_dot(soft, v))
        soft_copy(step, True).start()
        r.attended[span, cols] = jnp.where(lane < HD, parts[0], parts[1]).astype(bf16)
        return carry

    groups = 6
    count = steps_count // groups
    for g in range(groups):
        lax.fori_loop(g * count, (g + 1) * count, attend, 0)
        clock.work(2.0)
    for step in (steps_count - 2, steps_count - 1):
        soft_copy(step, True).wait()
    clock.ensure(out_flow, 4)

    def project_out(j, carry):
        cols = tile_at(j)
        r.middle[:, cols] = (
            r.start[:, cols]
            + nn_dot(r.attended[...], r.wout[:, cols])
            + r.small[ROW_B_OUT : ROW_B_OUT + 1, cols]
        )
        return carry

    lax.fori_loop(0, tiles, project_out, 0)
    clock.work(1.5)

    for i in range(images):
        scaled, _ = norm_stats(r.middle[span_at(i), :])
        r.normed_two[span_at(i), :] = (
            scaled * small(ROW_LN2_GAIN) + small(ROW_LN2_BIAS)
        ).astype(bf16)
        r.total[span_at(i), :] = r.middle[span_at(i), :] + small(ROW_B_DOWN)
    r.normed_flip[...] = r.normed_two[...].T
    r.back[...] = jnp.zeros_like(r.back)
    r.small_sums[0] = jnp.zeros_like(r.small_sums[0])
    clock.work(2.0)
    clock.ensure(grad_flow, 2)
    clock.ensure(up_weight, 3 + len(UP_BITS))
    clock.ensure(down_weight, 3 + len(DOWN_BITS))

    def reduction(work, recv, order, fin):
        state = Bag()
        size = work.shape[2]
        amount = size * work.shape[3] * 2 / 1e6
        split = [b for b in order if b != ACROSS][:halves]

        def half(high, bit):
            return pl.ds(mul16(bit * (high // 2)), high // 2)

        def views(level, stage):
            ref = recv[level]
            if stage == ACROSS:
                return ref.at[x_bit], ref.at[1 - x_bit], across_x
            bit, peer = dp_bit[stage], bit_peer[stage]
            if stage not in split:
                return ref, ref, peer
            lead = (slice(None),) * (len(ref.shape) - 2)
            high = ref.shape[-2]
            return ref.at[(*lead, half(high, bit))], ref.at[(*lead, half(high, 1 - bit))], peer

        def begin():
            state.copy = push(work.at[:, 1 - core_bit], recv[0], core)
            state.work = state.copy

        def step(n):
            state.copy.wait_recv()
            if n == 0:
                recv[0][...] = recv[0][...] + work[:, core_bit]
                left(state.work)
            else:
                keep, _, _ = views(n - 1, order[n - 1])
                recv[n][...] = recv[n][...] + keep[...]
            if n < len(order):
                _, give, peer = views(n, order[n])
                state.copy = push(give, recv[n + 1], peer)

        def corner(count):
            offset = 0
            for n in range(count):
                offset = offset + dp_bit[split[n]] * (size >> (n + 1))
            return pl.ds(mul16(offset), size >> count)

        def last():
            step(len(order))
            source, spot = recv[len(order)], fin(corner(halves))
            state.local = carry_local(source, spot)
            state.copy = push(source, spot, bit_peer[split[halves - 1]])

        def spread(count):
            state.copy.wait_recv()
            if count == halves - 1:
                state.local.wait()
            spot = fin(corner(count))
            state.copy = push(spot, spot, bit_peer[split[count - 1]])

        def end():
            state.copy.wait_recv()

        def link_of(stage):
            return LINK_X if stage == ACROSS else LINK_Z if stage else LINK_Y

        def hops(stage):
            return 2 if stage == 2 else 1

        steps = [(begin, LINK_CORE, amount * 2 / PAIR_RATE)]
        now = amount * 2
        for n, stage in enumerate(order):
            if stage == ACROSS or stage in split:
                now /= 2
            cost = now * hops(stage) / RATE
            steps.append((lambda n=n: step(n), link_of(stage), cost))
        for count in range(halves, 0, -1):
            stage = split[count - 1]
            action = last if count == halves else lambda c=count: spread(c)
            steps.append((action, link_of(stage), (amount / 2**count) * hops(stage) / RATE))
        steps.append((end, None, 0.0))
        return steps

    wide_flows, up_flows = [], []

    def levels_of(base):
        return [r[base + n] for n in range(2 + dp_bits)]

    def wide_flow(chunk):
        work, recv = r.work_wide.at[chunk % 2], levels_of(WIDE + 10 * chunk)
        order = order_of(dp_bits, chunk in LATE_WIDE)
        wide_flows.append(
            clock.add(reduction(work, recv, order, lambda s: r.fin_wide.at[chunk, s]))
        )

    def up_flow(chunk):
        cols = slice(chunk * TILE, (chunk + 1) * TILE)
        work, recv = r.work_up.at[chunk % 2], levels_of(UP + 10 * chunk)
        order = order_of(dp_bits, chunk in LATE_UP)
        up_flows.append(clock.add(reduction(work, recv, order, lambda s: r.fin_up.at[s, cols])))

    order = blocks * tiles

    def fetch(j):
        m, slot = j % blocks, j % 2
        inner = tile_at(j // blocks)
        return (
            pltpu.make_async_copy(
                r.wup.at[m, :, inner], r.up_slots.at[slot], r.slot_sems.at[0, slot]
            ),
            pltpu.make_async_copy(
                r.wdown.at[m, inner, :], r.down_slots.at[slot], r.slot_sems.at[1, slot]
            ),
        )

    for copy in fetch(0):
        copy.start()

    def feed(j, carry):
        m, slot, part = j % blocks, j % 2, (j // blocks) % 2
        inner = tile_at(j // blocks)

        @pl.when(j + 1 < order)
        def _():
            for copy in fetch(j + 1):
                copy.start()

        for copy in fetch(j):
            copy.wait()
        up, down = r.up_slots[slot], r.down_slots[slot]
        hidden = nn_dot(r.normed_two[...], up)
        hidden = hidden + r.small[pl.ds(ROW_B_UP + m, 1), inner]
        value, slope = gelu_pair(hidden)
        value = value.astype(bf16)
        r.total[...] += nn_dot(value, down)
        grad = r.grad[...]
        r.work_wide[part, m // 2, m % 2] = tn_dot(value, grad).astype(bf16)
        hidden_grad = (nt_dot(grad, down) * slope).astype(bf16)
        r.small_sums[0, pl.ds(ROW_B_UP + m, 1), inner] = column_sum(hidden_grad.astype(f32))
        r.work_up[part, m // 2, m % 2] = nn_dot(r.normed_flip[...], hidden_grad).astype(bf16)
        r.back[...] += nt_dot(hidden_grad, up)
        return carry

    for c in range(tiles):
        if c >= 2:
            clock.ensure(wide_flows[c - 2], 2)
            clock.ensure(up_flows[c - 2], 2)
        for half in range(2):
            begin = c * blocks + half * blocks // 2
            lax.fori_loop(begin, begin + blocks // 2, feed, 0)
            clock.work(5.0)
        wide_flow(c)
        up_flow(c)

    def packed(value, m, size):
        lanes = slice(m * size, (m + 1) * size)
        return jnp.concatenate([value[i][:, lanes] for i in range(images)], axis=1)

    total = [r.total[span_at(i), :].astype(bf16) for i in range(images)]
    for m in range(blocks):
        r.encoded_send[m, 0:rows] = packed(total, m, block)
    out_copies = []

    def encoded_begin():
        for peer, m in others:
            out_copies.append(push(r.encoded_send.at[m, 0:rows], r.encoded.at[mp], peer))

    encoded_flow = clock.add([(encoded_begin, LINK_X, 0.42 / RATE)], at=clock.now)
    encoded_own = carry_local(r.encoded_send.at[mp, 0:rows], r.encoded.at[mp])
    clock.work(1.0)

    def add_small(row, value):
        r.small_sums[0, row : row + 1, :] += value

    for i in range(images):
        span = span_at(i)
        scaled, inverse = norm_stats(r.middle[span, :])
        grad = r.back[span, :]
        out = r.grad[span, :].astype(f32)
        add_small(ROW_LN2_GAIN, column_sum(grad * scaled))
        add_small(ROW_LN2_BIAS, column_sum(grad))
        add_small(ROW_B_DOWN, column_sum(out))
        middle_grad = out + norm_back(grad, small(ROW_LN2_GAIN), scaled, inverse)
        r.middle[span, :] = middle_grad
        branch = middle_grad.astype(bf16)
        r.branch[span, :] = branch
        add_small(ROW_B_OUT, column_sum(branch.astype(f32)))
        clock.work(1.0)

    piece = block // 3

    def store_rows(t, j, value):
        for i in range(TILE // piece):
            unit = j * (TILE // piece) + i
            m, place = unit // 3, t * block + (unit % 3) * piece
            chunk, row = tiles + place // TILE, place % TILE
            clock.ensure(wide_flows[chunk - 2], 2)
            r.work_wide[chunk % 2, m // 2, m % 2, row : row + piece, :] = value[
                i * piece : (i + 1) * piece
            ].astype(bf16)

    for j in range(tiles):
        cols = slice(j * TILE, (j + 1) * TILE)
        r.gattended[:, cols] = nt_dot(r.branch[...], r.wout[cols, :]).astype(bf16)
        store_rows(0, j, tn_dot(r.attended[:, cols], r.branch[...]))
        clock.work(1.5)

    def attend_back(step, carry):
        image = step // pairs
        pair = step % pairs
        span = pl.ds(mul16(image * rows), rows)
        cols = pl.ds(pl.multiple_of(pair * LANES, LANES), LANES)

        @pl.when(step + 1 < steps_count)
        def _():
            soft_copy(step + 1, False).start()

        soft_copy(step, False).wait()
        q, k, v = r.qkv[0, span, cols], r.qkv[1, span, cols], r.qkv[2, span, cols]
        ga = r.gattended[span, cols]
        parts = []
        for h in range(2):
            mine = (lane >= HD) if h else (lane < HD)
            soft = r.soft_slots[step % 2, h]
            soft_wide = soft.astype(f32)
            prob = nt_dot(jnp.where(mine, ga, jnp.zeros_like(ga)), v)
            delta = jnp.sum(soft_wide * prob, axis=1, keepdims=True)
            score_grad = (soft_wide * (prob - delta)).astype(bf16)
            parts.append((nn_dot(score_grad, k), tn_dot(score_grad, q), tn_dot(soft, ga)))
        one, two = parts
        gq = jnp.where(lane < HD, one[0], two[0]) * (1.0 / math.sqrt(HD))
        r.qkv[0, span, cols] = gq.astype(bf16)
        r.qkv[1, span, cols] = jnp.where(lane < HD, one[1], two[1]).astype(bf16)
        r.qkv[2, span, cols] = jnp.where(lane < HD, one[2], two[2]).astype(bf16)
        return carry

    soft_copy(0, False).start()
    for g in range(groups):
        lax.fori_loop(g * count, (g + 1) * count, attend_back, 0)
        clock.work(3.0)

    for t, row in ((0, ROW_BQ), (2, ROW_BV)):
        add_small(row, column_sum(r.qkv[t].astype(f32)))

    r.back[...] = jnp.zeros_like(r.back)
    for t in range(3):

        def project_back(j, carry, t=t):
            cols = tile_at(j)
            r.back[...] += nn_dot(r.qkv[t, :, cols], r.wqkv[t, cols, :])
            return carry

        lax.fori_loop(0, tiles, project_back, 0)
        clock.work(1.5)

    tokens = []
    for i in range(images):
        span = span_at(i)
        scaled, inverse = norm_stats(r.start[span, :])
        grad = r.back[span, :]
        add_small(ROW_LN1_GAIN, column_sum(grad * scaled))
        add_small(ROW_LN1_BIAS, column_sum(grad))
        begin = r.middle[span, :] + norm_back(grad, small(ROW_LN1_GAIN), scaled, inverse)
        add_small(ROW_CLS, begin[0:1, :])
        for k in range(r.meta.shape[1]):
            add_small(ROW_META + k, r.meta[mp * images + i, k] * begin[1:2, :])
        tokens.append(begin.astype(bf16))
    clock.ensure(encoded_flow, 1)
    encoded_own.wait()
    for copy in out_copies:
        left(copy)
    for m in range(blocks):
        r.token_send[m, 0:rows] = packed(tokens, m, block)
    token_copies = []

    def token_begin():
        for peer, m in others:
            token_copies.append(push(r.token_send.at[m, 0:rows], r.token_recv.at[mp], peer))
        r.token_recv[mp] = r.token_send[mp, 0:rows]

    def token_end():
        for copy in token_copies:
            copy.wait_recv()

    token_flow = clock.add([(token_begin, LINK_X, 0.42 / RATE), (token_end, None, 0.0)])
    clock.work(2.0)

    def all_sum(levels, out):
        state = Bag()

        def step(level):
            if level:
                state.copy.wait_recv()
                levels[level] = levels[level] + levels[level - 1]
            if level < len(peers):
                state.copy = push(levels.at[level], levels.at[level + 1], peers[level])
            else:
                out(levels[level])

        links = [LINK_CORE, LINK_X, LINK_Y] + [LINK_Z] * (dp_bits - 1) + [None]
        return [(lambda n=n: step(n), link, 1.5) for n, link in enumerate(links)]

    def store_small(value):
        narrow = jnp.zeros(r.gnarrow.shape, f32)
        bias = jnp.zeros(r.gbias.shape, f32)
        for m in range(blocks):
            narrow += jnp.where(mp == m, value[:, m * block : (m + 1) * block], 0.0)
            bias += jnp.where(mp == m, value[ROW_B_UP + m : ROW_B_UP + m + 1, :], 0.0)
        r.gnarrow[...] = narrow
        r.gbias[...] = bias

    def wave_sum():
        copies = []

        def over_mp():
            for peer, _ in others:
                copies.append(push(r.wave_parts.at[mp], r.wave_parts.at[mp], peer))

        def over_dp():
            for copy in copies:
                copy.wait_recv()
            copies.clear()
            r.wave_chips[dp] = sum(r.wave_parts[m] for m in range(blocks))
            for peer in bit_peer + mixed:
                copies.append(push(r.wave_chips.at[dp], r.wave_chips.at[dp], peer))

        def end():
            for copy in copies:
                copy.wait_recv()
            r.gwave[...] = sum(r.wave_chips[d] for d in range(1 << dp_bits))

        return [(over_mp, LINK_SMALL, 1.0), (over_dp, LINK_SMALL, 3.0), (end, None, 0.0)]

    clock.add(all_sum(r.small_sums, store_small))
    def pixel_gradient():
        pixel_back = [nt_dot(tokens[i], r.patch[i]).astype(bf16) for i in range(images)]
        for m in range(blocks):
            r.pixel_send[m] = packed(pixel_back, m, depth // blocks)

        def pixel_begin():
            for peer, m in others:
                out_copies.append(push(r.pixel_send.at[m], r.pixel_grad.at[mp], peer))

        clock.add([(pixel_begin, LINK_X, 0.28 / RATE)], at=clock.now)
        pixel_own = carry_local(r.pixel_send.at[mp], r.pixel_grad.at[mp])
        clock.work(1.5)
        return pixel_own

    def chunks_ready(count):
        while len(wide_flows) < tiles + count:
            wide_flow(len(wide_flows))

    def weight_rows(t, source):
        for j in range(tiles):
            cols = slice(j * TILE, (j + 1) * TILE)
            store_rows(t, j, tn_dot(r.qkv[source, :, cols], r.normed_one[...]))
            clock.work(0.8)
        chunks_ready((t + 1) * block // TILE)

    if inside:
        def sensor_sums():
            r.total[...] = jnp.zeros_like(r.total)
            r.back[...] = jnp.zeros_like(r.back)
            lane_block = lax.broadcasted_iota(jnp.int32, (1, width), 1) // block
            for m in range(blocks):
                for i in range(images):
                    c = m * images + i
                    part = r.token_recv[m, :, i * block : (i + 1) * block]
                    part = tn_dot(r.chosen[c], jnp.concatenate([part] * blocks, axis=1))
                    tag = r.tags[c]
                    r.total[0:depth, :] += jnp.where(lane_block == tag, part, 0.0)
                    r.back[0:depth, :] += jnp.where(lane_block + blocks == tag, part, 0.0)
                    clock.work(0.7)

            for flow in up_flows:
                clock.ensure(flow, 2)

            def slot_of(d):
                return tuple((d >> b) % 2 for b in KERNEL_ORDER)

            for s in range(sensors):
                store = r.total if s < blocks else r.back
                part = store[0:depth, s % blocks * block : (s % blocks + 1) * block]
                for d in range(slots):
                    strips = [
                        part[(b * slots + d) * pixels_each : (b * slots + d + 1) * pixels_each]
                        for b in range(bands)
                    ]
                    line = slice(s * piece_rows, (s + 1) * piece_rows)
                    r.work_up[(*slot_of(d), line, slice(0, block))] = jnp.concatenate(
                        strips, axis=0
                    ).astype(bf16)
            clock.work(1.0)

        cut = 3 * piece_rows

        def kernel_flow(half):
            here = Bag()
            order = KERNEL_ORDER
            lines = slice(cut, sensors * piece_rows) if half else slice(0, cut)

            def source(level):
                if level == 0:
                    return r.work_up.at[:, :, :, lines, :]
                return r[KERNEL + level - 1].at[(slice(None),) * (3 - level) + (lines,)]

            def step(level):
                if level:
                    target = source(level)
                    here.copy.wait_recv()
                    target[...] = target[...] + source(level - 1)[dp_bit[order[level - 1]]]
                if level < 3:
                    give = source(level).at[1 - dp_bit[order[level]]]
                    here.copy = push(give, source(level + 1), bit_peer[order[level]])
                    return
                state.shares.append(half)
                if len(state.shares) == 2:
                    kernel_end()

            steps = []
            for n, b in enumerate(order):
                cost = (0.69, 0.34, 0.17)[n] / 2 * (2 if b == 2 else 1) / RATE
                steps.append((lambda n=n: step(n), LINK_Z if b else LINK_Y, cost))
            return steps + [(lambda: step(3), None, 0.0)]

        def kernel_end():
            flat = r[KERNEL + dp_bits - 1][:, 0:block]
            r.share[...] = flat.astype(f32).reshape(r.share.shape)
            line = lax.broadcasted_iota(jnp.int32, (sensors * piece_rows, HYP), 0)
            wave = jnp.zeros((sensors * piece_rows, HYP), f32)
            for p in range(pixels_each):
                part = nt_dot(flat, r.w_kernel[:, p, :])
                wave = wave + jnp.where(line % pixels_each == p, part, 0.0)
            wave = jnp.sum(wave.reshape(sensors * bands, pixels_each, HYP), axis=1)
            r.wave_parts[mp] = wave
            clock.add(wave_sum())

        def sensor_stage():
            clock.ensure(token_flow, 2)
            sensor_sums()
            state.shares = []
            for half in range(2):
                clock.add(kernel_flow(half))

    else:

        def sensor_stage():
            clock.ensure(token_flow, 2)
            r.token_out[...] = r.token_recv[...]
            r.chosen_out[...] = r.chosen[...]

    for n, (t, source) in enumerate(((1, 2), (2, 0), (3, 1))):
        if PIXELS_AT == n:
            pixel_own = pixel_gradient()
        if SENSORS_AT == n:
            sensor_stage()
        weight_rows(t, source)
    if PIXELS_AT == 3:
        pixel_own = pixel_gradient()
    if SENSORS_AT == 3:
        sensor_stage()

    clock.drain()
    pixel_own.wait()
    for copy in out_copies:
        copy.wait_recv()
    for copy in sent:
        copy.wait_send()


def layer(length, dp_bits, inside, scalars, arrays, distant):
    piece, index, pixels = arrays["piece"], arrays["index"], distant["pixels"]
    rows = index.shape[0]
    chips, patches, depth = pixels.shape
    block, width = distant["wout_shard"].shape
    blocks = width // block
    images = chips // blocks
    total = images * rows
    steps = images * width // LANES
    tiles = width // TILE
    halves = min(3, dp_bits)

    def vmem(*size, kind=bf16):
        return pltpu.VMEM(size, kind)

    anywhere = pl.BlockSpec(memory_space=pl.ANY)
    near = pl.BlockSpec(memory_space=pltpu.VMEM)
    scalar = pl.BlockSpec(memory_space=pltpu.SMEM)
    names, operands, in_specs = list(scalars), list(scalars.values()), [scalar] * len(scalars)
    for group, spec in ((arrays, near), (distant, anywhere)):
        names += list(group)
        operands += list(group.values())
        in_specs += [spec] * len(group)

    outs = dict(
        encoded=((blocks, rows, images * block), bf16, anywhere),
        pixel_grad=((blocks, rows, images * depth // blocks), bf16, anywhere),
        gnarrow=((SMALL_ROWS, block), f32, near),
        gbias=((1, width), f32, near),
        fin_wide=((2 * tiles, TILE, width), bf16, anywhere),
        fin_up=((width, width), bf16, anywhere),
    )
    if inside:
        sensors, piece_rows, _ = piece.shape
        outs.update(share=(piece.shape, f32, near))
        bands = piece_rows // arrays["w_kernel"].shape[1]
        outs.update(gwave=((sensors * bands, HYP), f32, near))
    else:
        outs.update(token_out=((blocks, rows, images * block), bf16, near))
        outs.update(chosen_out=((chips, rows, depth), bf16, near))
    results = list(outs)
    outs.update(wup=((blocks, width, width), bf16, anywhere))
    outs.update(wdown=((blocks, width, width), bf16, anywhere))
    outs.update(soft=((steps, 2, rows, rows), bf16, anywhere))

    scratch = dict(
        narrow=vmem(SMALL_ROWS, block, kind=f32),
        bias_up=vmem(8, width, kind=f32),
        narrow_all=vmem(blocks, SMALL_ROWS, block, kind=f32),
        bias_all=vmem(blocks, 8, width, kind=f32),
        small=vmem(SMALL_ROWS, width, kind=f32),
        grad_recv=vmem(blocks, rows, images * block),
        grad=vmem(total, width),
        chosen=vmem(chips, rows, depth),
        start=vmem(total, width, kind=f32),
        middle=vmem(total, width, kind=f32),
        normed_one=vmem(total, width),
        normed_two=vmem(total, width),
        normed_flip=vmem(width, total),
        qkv=vmem(3, total, width),
        attended=vmem(total, width),
        total=vmem(total, width, kind=f32),
        back=vmem(total, width, kind=f32),
        wqkv=vmem(3, width, width),
        wout=vmem(width, width),
        up_slots=vmem(2, width, TILE),
        down_slots=vmem(2, TILE, width),
        soft_slots=vmem(2, 2, rows, rows),
        small_sums=vmem(3 + dp_bits, SMALL_ROWS, width, kind=f32),
        work_wide=vmem(2, 2, 2, TILE, width),
        work_up=vmem(2, 2, 2, width, TILE),
        token_recv=vmem(blocks, rows, images * block),
        pixel_send=vmem(blocks, rows, images * depth // blocks),
    )
    if inside:
        scratch.update(kernels_near=vmem(1 << (dp_bits - 1), *piece.shape))
        scratch.update(kernels_far=vmem(1 << (dp_bits - 1), *piece.shape))
        for n in range(dp_bits):
            lead = (2,) * (dp_bits - 1 - n)
            scratch[KERNEL + n] = vmem(*lead, sensors * piece_rows, TILE)
        scratch.update(patch_send=vmem(blocks, 2, depth // 2, images * block))
        scratch.update(patch_recv=vmem(blocks, 2, depth // 2, images * block))
        scratch.update(encoded_send=vmem(blocks, rows, images * block))
        scratch.update(patch=vmem(images, depth, width))
        scratch.update(wave_parts=vmem(blocks, sensors * bands, HYP, kind=f32))
        scratch.update(wave_chips=vmem(1 << dp_bits, sensors * bands, HYP, kind=f32))
    else:
        scratch.update(encoded_send=vmem(blocks, rows, images * block))
        scratch.update(token_send=vmem(blocks, rows, images * block))
    for base, amount, high, wide in ((WIDE, 2 * tiles, TILE, width), (UP, tiles, width, TILE)):
        for chunk in range(amount):
            along = order_of(dp_bits, chunk in (LATE_UP if base == UP else LATE_WIDE))
            scratch[base + 10 * chunk] = vmem(2, high, wide)
            lead, now, cut = (2,), high, 0
            for n, stage in enumerate(along):
                if stage == ACROSS:
                    lead = ()
                elif cut < halves:
                    now, cut = now // 2, cut + 1
                scratch[base + 10 * chunk + 1 + n] = vmem(*lead, now, wide)
    copies = 36 + 9 * (2 + dp_bits + halves) + 2 * (2 + dp_bits) + 32 + dp_bits
    dma = pltpu.SemaphoreType.DMA
    scratch.update(local_sems=dma((24,)))
    scratch.update(send_sems=dma((copies,)))
    scratch.update(recv_sems=dma((copies,)))
    scratch.update(slot_sems=dma((2, 2)))
    scratch.update(soft_sems=dma((2, 2)))
    scratch.update(pixel_sems=dma((2, patches // TILE)))

    names += [*outs, *scratch]

    def kernel(*refs):
        labels, refs = list(names), list(refs)
        twice = dict(branch="grad", gattended="normed_two")
        if inside:
            twice.update(token_send="encoded_send")
        for second, first in twice.items():
            labels.append(second)
            refs.append(refs[names.index(first)])
        layer_kernel(labels, length, dp_bits, inside, *refs)

    values = pl.pallas_call(
        kernel,
        in_specs=in_specs,
        out_specs=[spec for _, _, spec in outs.values()],
        out_shape=[jax.ShapeDtypeStruct(size, kind) for size, kind, _ in outs.values()],
        scratch_shapes=list(scratch.values()),
        compiler_params=pltpu.CompilerParams(
            vmem_limit_bytes=VMEM_LIMIT, collective_id=0, has_side_effects=True
        ),
        name="layer",
    )(*operands)
    return Refs(outs, values)


def per_device(
    dp_bits,
    pixels,
    meta,
    tags,
    visible,
    wavelength,
    w_hyp,
    b_hyp,
    w_kernel,
    w_meta,
    cls_token,
    ln1_gain,
    ln1_bias,
    w_qkv,
    b_qv,
    w_out,
    b_out,
    ln2_gain,
    ln2_bias,
    w_up,
    b_up,
    w_down,
    b_down,
    cotangent,
):
    width = w_qkv.shape[0]
    block = cls_token.shape[0]
    blocks = width // block
    sensors, bands = wavelength.shape
    chips, patches, depth = pixels.shape
    pixels_each = w_kernel.shape[1]
    length = visible.shape[1] + 2
    rows = -(-length // ROW_TILE) * ROW_TILE
    images = chips // blocks
    inside = dp_bits == 3 and bands * pixels_each % ROW_TILE == 0

    wave_table = wave_code(wavelength)
    wave_pre = jnp.einsum("sbi,ij->sbj", wave_table, w_hyp, precision=highest) + b_hyp
    wave_hidden, wave_back = jax.vjp(jax.nn.gelu, wave_pre)
    wave_low = wave_hidden.astype(bf16)
    kernel = jnp.einsum("sbj,jpf->sbpf", wave_low, w_kernel, preferred_element_type=f32)
    kernel = kernel.astype(bf16)

    scalars = dict(meta=meta, tags=tags)
    arrays = dict(
        piece=kernel.reshape(sensors, bands * pixels_each, block),
        index=jnp.pad(visible, ((0, 0), (2, rows - length)), constant_values=-1).T,
        w_meta=w_meta,
        cls=cls_token[None],
        gain_one=ln1_gain[None],
        bias_one=ln1_bias[None],
        b_qv=b_qv,
        b_out=b_out[None],
        gain_two=ln2_gain[None],
        bias_two=ln2_bias[None],
        b_down=b_down[None],
        b_up=b_up[None],
        w_kernel=w_kernel,
    )
    distant = dict(
        pixels=pixels,
        table=jnp.asarray(pos_table(patches, width)),
        grad_blocks=jnp.pad(
            cotangent.reshape(blocks, images, length, block).transpose(0, 2, 1, 3),
            ((0, 0), (0, rows - length), (0, 0), (0, 0)),
        ).reshape(blocks, rows, images * block),
        wqkv_shard=w_qkv.transpose(1, 2, 0),
        wout_shard=w_out,
        wup_shard=w_up,
        wdown_shard=w_down,
    )
    if not inside:
        kernel = lax.all_gather(kernel, "dp", axis=2, tiled=True)
        kernel = kernel.reshape(sensors, depth, block)
        arrays.update(patch=lax.all_to_all(kernel[tags], "mp", 0, 2, tiled=True))
    got = layer(length, dp_bits, inside, scalars, arrays, distant)

    def unpack(value, size):
        value = value.reshape(blocks, rows, images, size).transpose(0, 2, 1, 3)
        return value.reshape(chips, rows, size)

    encoded = unpack(got.encoded, block)[:, :length]
    pixel_grad = unpack(got.pixel_grad, depth // blocks)[:, 2:length]
    wave_float = wave_low.astype(f32)
    if inside:
        share = got.share.reshape(sensors, bands, pixels_each, block)
        grad_wave = got.gwave.reshape(sensors, bands, HYP)
    else:
        select = (tags[:, None] == jnp.arange(sensors, dtype=jnp.int32)[None, :]).astype(f32)
        token_grad = unpack(got.token_out, block)
        chip_grad = jnp.einsum(
            "cvk,cvf->ckf", got.chosen_out, token_grad, preferred_element_type=f32
        )
        share = jnp.einsum("cs,ckf->skf", select, chip_grad, precision=highest)
        share = share.reshape(sensors, bands, depth // bands, block)
        share = lax.psum_scatter(share, "dp", scatter_dimension=2, tiled=True)
        grad_wave = lax.psum(
            jnp.einsum("sbpf,jpf->sbj", share, w_kernel.astype(f32), precision=highest),
            ("dp", "mp"),
        )
    grad_w_kernel = jnp.einsum("sbj,sbpf->jpf", wave_float, share, precision=highest)
    grad_pre = wave_back(grad_wave)[0]
    grad_w_hyp = jnp.einsum("sbi,sbj->ij", wave_table, grad_pre, precision=highest)
    grad_b_hyp = jnp.sum(grad_pre, axis=(0, 1))

    tiles = width // TILE
    fin_wide = got.fin_wide
    gdown = fin_wide[:tiles].reshape(width, width).astype(f32)
    gup = got.fin_up.astype(f32)
    inner = fin_wide[tiles:].reshape(4, block, width)
    gout = inner[0].astype(f32)
    gqkv = jnp.stack([inner[2], inner[3], inner[1]]).transpose(2, 0, 1).astype(f32)
    gnarrow = got.gnarrow
    return (
        encoded,
        pixel_grad,
        grad_w_hyp,
        grad_b_hyp,
        grad_w_kernel,
        gnarrow[ROW_META : ROW_META + w_meta.shape[0]],
        gnarrow[ROW_CLS],
        gnarrow[ROW_LN1_GAIN],
        gnarrow[ROW_LN1_BIAS],
        gqkv,
        gnarrow[ROW_BQ : ROW_BV + 1],
        gout,
        gnarrow[ROW_B_OUT],
        gnarrow[ROW_LN2_GAIN],
        gnarrow[ROW_LN2_BIAS],
        gup,
        got.gbias[0],
        gdown,
        gnarrow[ROW_B_DOWN],
    )


def solution(mesh):
    dp_bits = mesh.shape["dp"].bit_length() - 1
    return jax.shard_map(
        functools.partial(per_device, dp_bits),
        mesh=mesh,
        in_specs=(
            P("dp", None, None),
            P("dp", None),
            P("dp"),
            P("dp", None),
            P(),
            P(),
            P(),
            P(None, "dp", "mp"),
            P(None, "mp"),
            P("mp"),
            P("mp"),
            P("mp"),
            P(None, None, "mp"),
            P(None, "mp"),
            P("mp", None),
            P("mp"),
            P("mp"),
            P("mp"),
            P(None, "mp"),
            P("mp"),
            P("mp", None),
            P("mp"),
            P("dp", None, "mp"),
        ),
        out_specs=(
            P("dp", None, "mp"),
            P("dp", None, "mp"),
            P(),
            P(),
            P(None, "dp", "mp"),
            P(None, "mp"),
            P("mp"),
            P("mp"),
            P("mp"),
            P(None, None, "mp"),
            P(None, "mp"),
            P("mp", None),
            P("mp"),
            P("mp"),
            P("mp"),
            P(None, "mp"),
            P("mp"),
            P("mp", None),
            P("mp"),
        ),
        check_vma=False,
    )
```

```python
import functools
import itertools
import math

import jax
import jax.numpy as jnp
import numpy as np
from jax import lax
from jax.experimental import pallas as pl
from jax.experimental.pallas import tpu as pltpu
from jax.sharding import PartitionSpec as P

HD = 64
HYP = 128
LANES = 128
TILE = 256
ROW_TILE = 16

norm_epsilon = 1e-05
highest = lax.Precision.HIGHEST
f32 = jnp.float32
bf16 = jnp.bfloat16
VMEM_LIMIT = 58 * 1024 * 1024
MESH = pl.DeviceIdType.MESH

ROW_META = 0
ROW_CLS = 8
ROW_LN1_GAIN = 9
ROW_LN1_BIAS = 10
ROW_BQ = 11
ROW_BV = 12
ROW_B_OUT = 13
ROW_LN2_GAIN = 14
ROW_LN2_BIAS = 15
ROW_B_DOWN = 16
ROW_B_UP = 17
SMALL_ROWS = 24


def wave_code(wavelength):
    half_width = HYP // 2
    ladder = jnp.arange(half_width, dtype=f32) * (math.log(100.0) / half_width)
    angle_grid = wavelength[..., None] * jnp.exp(ladder)
    return jnp.concatenate([jnp.sin(angle_grid), jnp.cos(angle_grid)], axis=-1)


def pos_table(patch_count, width):
    index = np.arange(patch_count, dtype=np.float64)[:, None]
    feature = np.arange(width)[None, :]
    angle = index * np.exp((feature // 2) * (-2.0 * math.log(10000.0) / width))
    table = np.where(feature % 2 == 0, np.sin(angle), np.cos(angle)).astype(np.float32)
    return table.astype(jnp.bfloat16)


def nn_dot(left, right):
    return lax.dot_general(left, right, (((1,), (0,)), ((), ())), preferred_element_type=f32)


def nt_dot(left, right):
    return lax.dot_general(left, right, (((1,), (1,)), ((), ())), preferred_element_type=f32)


def tn_dot(left, right):
    return lax.dot_general(left, right, (((0,), (0,)), ((), ())), preferred_element_type=f32)


def gelu_pair(u):
    c = math.sqrt(2.0 / math.pi)
    square = u * u
    t = jnp.tanh(c * u * (1.0 + 0.044715 * square))
    half = 0.5 * (1.0 + t)
    slope = half + 0.5 * u * (1.0 - t * t) * (c * (1.0 + 3.0 * 0.044715 * square))
    return u * half, slope


def norm_stats(x):
    width = x.shape[1]
    center = jnp.sum(x, axis=1, keepdims=True) * (1.0 / width)
    square = jnp.sum(x * x, axis=1, keepdims=True) * (1.0 / width)
    inverse = lax.rsqrt(square - center * center + norm_epsilon)
    return (x - center) * inverse, inverse


def hot_rows(index, count):
    lane = lax.broadcasted_iota(jnp.int32, (index.shape[0], count), 1)
    return jnp.where(index == lane, 1.0, 0.0).astype(bf16)


def norm_back(grad, gain, scaled, inverse):
    width = grad.shape[1]
    weighted = grad * gain
    first = jnp.sum(weighted, axis=1, keepdims=True) * (1.0 / width)
    second = jnp.sum(weighted * scaled, axis=1, keepdims=True) * (1.0 / width)
    return inverse * (weighted - first - scaled * second)


def column_sum(x):
    return jnp.sum(x, axis=0, keepdims=True)


class Flow:
    def __init__(self, clock, steps, ready):
        self.clock, self.steps, self.next, self.ready = clock, steps, 0, ready

    @property
    def open(self):
        return self.next < len(self.steps)

    def due(self):
        _, link, _ = self.steps[self.next]
        return max(self.ready, self.clock.busy.get(link, 0.0) - self.clock.slack)

    def go(self):
        action, link, cost = self.steps[self.next]
        clock = self.clock
        clock.now = max(clock.now, self.ready)
        action()
        self.next += 1
        clock.now += clock.start
        begin = max(clock.now, clock.busy.get(link, 0.0))
        if link is not None:
            clock.busy[link] = begin + cost
        self.ready = begin + cost + clock.latency


class Clock:
    latency, slack, start = 1.5, 6.0, 0.3

    def __init__(self):
        self.now, self.busy, self.flows = 0.0, {}, []

    def add(self, steps, at=None):
        flow = Flow(self, steps, self.now if at is None else at)
        self.flows.append(flow)
        if at is None:
            flow.go()
        return flow

    def ensure(self, flow, count):
        if not flow.next:
            flow.ready = min(flow.ready, self.now)
        while flow.next < count:
            flow.go()

    def work(self, cost):
        self.now += cost
        self.pump()

    def pump(self):
        while True:
            due = [f for f in self.flows if f.open and f.due() <= self.now]
            if not due:
                return
            min(due, key=Flow.due).go()

    def drain(self):
        while True:
            left = [f for f in self.flows if f.open]
            if not left:
                return
            flow = min(left, key=Flow.due)
            self.now = max(self.now, flow.due())
            flow.go()


class Refs:
    def __init__(self, names, refs):
        self.named = dict(zip(names, refs, strict=True))

    def __getattr__(self, name):
        return self.named[name]

    def __getitem__(self, number):
        return self.named[number]


KERNEL, WIDE, UP = 0, 100, 200
ACROSS = -1


def order_of(dp_bits, late):
    if late:
        return [1, ACROSS, 0, *range(2, dp_bits)]
    return [ACROSS, *range(dp_bits)]


class Bag:
    pass


RATE = 0.05
PAIR_RATE = 0.3
LATE_WIDE, LATE_UP = (), ()
UP_BITS, DOWN_BITS = (0, 1), (0,)
HOLD = 18.0
UP_AT = 8.0
SENSORS_AT = 1
PIXELS_AT = 1
KERNEL_ORDER = (1, 0, 2)
LINK_CORE, LINK_X, LINK_Y, LINK_Z, LINK_SMALL = range(5)


def layer_kernel(names, length, dp_bits, inside, *refs):
    r = Refs(names, refs)
    halves = min(3, dp_bits)
    rows, width = r.index.shape[0], r.start.shape[1]
    chips, patches, depth = r.pixels.shape
    blocks = r.wup.shape[0]
    images = chips // blocks
    block = width // blocks
    tiles = width // TILE
    pairs = width // LANES
    steps_count = images * pairs

    mp, dp = lax.axis_index("mp"), lax.axis_index("dp")
    core_bit, x_bit = mp % 2, mp // 2
    core_mp, x_mp = mp + 1 - 2 * core_bit, mp + 2 - 4 * x_bit
    far_mp = blocks - 1 - mp
    dp_bit = [(dp // (1 << b)) % 2 for b in range(dp_bits)]

    def flip(*bits):
        value = dp
        for b in bits:
            value = value + (1 - 2 * dp_bit[b]) * (1 << b)
        return value

    core, across_x, diagonal = {"mp": core_mp}, {"mp": x_mp}, {"mp": far_mp}
    bit_peer = [{"dp": flip(b)} for b in range(dp_bits)]
    peers = [core, across_x, *bit_peer]
    others = [(core, core_mp), (across_x, x_mp), (diagonal, far_mp)]
    greeted = peers + [diagonal]
    if inside:
        mixed = [{"dp": flip(*bits)} for bits in ((0, 1), (0, 2), (1, 2), (0, 1, 2))]
        greeted += mixed

    barrier = pltpu.get_barrier_semaphore()
    for peer in greeted:
        pl.semaphore_signal(barrier, inc=1, device_id=peer, device_id_type=MESH)
    pl.semaphore_wait(barrier, len(greeted))

    sent, numbers, local_numbers = [], itertools.count(), itertools.count()

    def push(source, target, peer):
        number = next(numbers)
        copy = pltpu.make_async_remote_copy(
            src_ref=source,
            dst_ref=target,
            send_sem=r.send_sems.at[number],
            recv_sem=r.recv_sems.at[number],
            device_id=peer,
            device_id_type=MESH,
        )
        copy.start()
        sent.append(copy)
        return copy

    def left(copy):
        copy.wait_send()
        sent[:] = [c for c in sent if c is not copy]

    def carry_local(source, target):
        copy = pltpu.make_async_copy(source, target, r.local_sems.at[next(local_numbers)])
        copy.start()
        return copy

    def mul16(value):
        return pl.multiple_of(value, ROW_TILE)

    def tile_at(j):
        return pl.ds(pl.multiple_of(j * TILE, TILE), TILE)

    def span_at(i):
        return pl.ds(i * rows, rows)

    def small(row):
        return r.small[row : row + 1, :]

    clock = Clock()

    if inside:
        place = dp // 2
        r.kernels_near[place] = r.piece[...]
        sideways = bit_peer[0]
        direct = push(r.piece, r.kernels_far.at[place], sideways)
        along = []
        for peer, bits in ((bit_peer[1], (1,)), (mixed[2], (1, 2)), (bit_peer[2], (2,))):
            along.append((push(r.piece, r.kernels_near.at[place], peer), flip(*bits) // 2))
        passed = []

        def pass_on(n):
            copy, index = along[n]
            copy.wait_recv()
            passed.append(push(r.kernels_near.at[index], r.kernels_far.at[index], sideways))

        amount = 0.172
        gather_steps = [
            (lambda: None, LINK_Z, amount / RATE),
            (lambda: pass_on(0), LINK_Y, amount * 1.5 / RATE),
            (lambda: pass_on(1), LINK_Y, amount * 1.5 / RATE),
        ]

        def halfway():
            pass_on(2)

        gather_steps.append((halfway, LINK_Y, amount / RATE))

        def gather_end():
            direct.wait_recv()
            for copy in passed:
                copy.wait_recv()

        gather_steps.append((gather_end, None, 0.0))
        gather_flow = clock.add(gather_steps)

    r.narrow[...] = jnp.zeros_like(r.narrow)
    row = 0
    for part in (r.w_meta, r.cls, r.gain_one, r.bias_one, r.b_qv, r.b_out, r.gain_two, r.bias_two):
        r.narrow[row : row + part.shape[0], :] = part[...]
        row += part.shape[0]
    r.narrow[row : row + 1, :] = r.b_down[...]
    r.bias_up[...] = jnp.broadcast_to(r.b_up[...].reshape(1, width), r.bias_up.shape)
    narrow_copies = []
    for peer, _ in others:
        narrow_copies.append(push(r.narrow, r.narrow_all.at[mp], peer))
        narrow_copies.append(push(r.bias_up, r.bias_all.at[mp], peer))
    r.narrow_all[mp] = r.narrow[...]
    r.bias_all[mp] = r.bias_up[...]

    def weight_flow(shard, full, inner, bits, at=None):
        parts = 1 << len(bits)
        high = block if inner else shard.shape[0]
        lead = (slice(None),) if len(shard.shape) == 3 else ()

        def view(m, first, count):
            place = pl.ds(mul16(first * (high // parts)), count * (high // parts))
            if inner:
                place = pl.ds(
                    mul16(m * block + first * (high // parts)), count * (high // parts)
                )
                return full.at[(*lead, place)]
            return full.at[m, place, :]

        state = Bag()
        first = 0
        for n, b in enumerate(bits):
            first = first + dp_bit[b] * (1 << n)
        state.hands = []

        def begin():
            own = shard.at[(*lead, pl.ds(mul16(first * (high // parts)), high // parts))]
            state.local = carry_local(shard, view(mp, 0, parts))
            state.copy = push(own, view(mp, first, 1), across_x)

        state.hands.append(push(shard, view(mp, 0, parts), core))

        def held(n):
            start = 0
            for k in range(n, len(bits)):
                start = start + dp_bit[bits[k]] * (1 << k)
            return start, 1 << n

        def came(n):
            start, count = held(n)
            if n:
                count //= 2
                start = start + (1 - dp_bit[bits[n - 1]]) * count
            return start, count

        def relay(n):
            state.copy.wait_recv()
            if n < len(bits):
                piece = view(x_mp, *held(n))
                state.next = push(piece, piece, bit_peer[bits[n]])
            piece = view(x_mp, *came(n))
            state.hands.append(push(piece, piece, core))
            if n < len(bits):
                state.copy = state.next

        def end():
            state.local.wait()
            for copy in state.hands:
                copy.wait_recv()

        cost = math.prod(shard.shape) * 2 / parts / 1e6
        steps = [(begin, LINK_X, cost / RATE)]
        for n in range(len(bits)):
            link = LINK_Z if bits[n] else LINK_Y
            steps.append((lambda n=n: relay(n), link, cost * (1 << n) / RATE))
        steps.append((lambda: relay(len(bits)), LINK_CORE, cost * parts / 2 / PAIR_RATE))
        steps.append((end, None, 0.0))
        return clock.add(steps, at=at)

    qkv_flow = weight_flow(r.wqkv_shard, r.wqkv, True, (0,))
    out_flow = weight_flow(r.wout_shard, r.wout, True, (0,))
    up_weight = weight_flow(r.wup_shard, r.wup, False, UP_BITS, at=UP_AT)
    down_weight = weight_flow(r.wdown_shard, r.wdown, False, DOWN_BITS, at=1000.0)
    qkv_flow.ready = out_flow.ready = HOLD

    state = Bag()

    def grad_begin():
        state.grad = [push(r.encoded_send.at[m], r.grad_recv.at[mp], p) for p, m in others]
        r.grad_recv[mp] = r.encoded_send[mp]

    def grad_end():
        for copy in state.grad:
            copy.wait_recv()
        for i in range(images):
            r.grad[span_at(i), :] = jnp.concatenate(
                [r.grad_recv[m][:, i * block : (i + 1) * block] for m in range(blocks)], axis=1
            )

    def pack_grad():
        r.encoded_send[...] = jnp.zeros_like(r.encoded_send)
        for m in range(blocks):
            pair = [r.grad_rows[:, m * images + i, :] for i in range(images)]
            r.encoded_send[m, 0:length] = jnp.concatenate(pair, axis=1)

    turned = r.visible[...].astype(f32).T
    none = jnp.full((rows, chips), -1.0, f32)
    turned = jnp.concatenate([none[0:2], turned, none[length:rows]], axis=0)
    r.index[...] = turned.astype(jnp.int32)

    table_copies = []
    for k in range(patches // TILE):
        table_copies.append(
            carry_local(r.table.at[k * TILE : (k + 1) * TILE], r.work_wide.at[0, k // 2, k % 2])
        )

    def pixel_copies(c):
        lanes = slice((c % 2) * depth, (c % 2 + 1) * depth)
        return [
            pltpu.make_async_copy(
                r.pixels.at[c, k * TILE : (k + 1) * TILE],
                r.work_wide.at[1, k // 2, k % 2, :, lanes],
                r.pixel_sems.at[c % 2, k],
            )
            for k in range(patches // TILE)
        ]

    for copy in pixel_copies(0):
        copy.start()
    for c in range(chips):
        if c + 1 < chips:
            for copy in pixel_copies(c + 1):
                copy.start()
        for copy in pixel_copies(c):
            copy.wait()
        hot = hot_rows(r.index[:, c : c + 1], patches)
        lanes = slice((c % 2) * depth, (c % 2 + 1) * depth)
        value = 0.0
        for k in range(patches // TILE):
            value = value + nn_dot(
                hot[:, k * TILE : (k + 1) * TILE], r.work_wide[1, k // 2, k % 2, :, lanes]
            )
        r.chosen[c] = value.astype(bf16)
        clock.work(0.7)

    for copy in narrow_copies:
        copy.wait_recv()
    r.small[...] = jnp.concatenate([r.narrow_all[m] for m in range(blocks)], axis=1)
    for m in range(blocks):
        r.small[ROW_B_UP + m : ROW_B_UP + m + 1, :] = r.bias_all[m, 0:1, :]

    for copy in table_copies:
        copy.wait()
    chip_lane = lax.broadcasted_iota(jnp.int32, (rows, chips), 1)
    index_wide = r.index[...].astype(f32)
    for i in range(images):
        mine = jnp.where(chip_lane == mp * images + i, index_wide, 0.0)
        hot = hot_rows(jnp.sum(mine, axis=1, keepdims=True).astype(jnp.int32), patches)
        value = 0.0
        for k in range(patches // TILE):
            value = value + nn_dot(
                hot[:, k * TILE : (k + 1) * TILE], r.work_wide[0, k // 2, k % 2]
            )
        r.start[span_at(i), :] = value
        token = jnp.zeros((1, width), f32)
        for k in range(r.meta.shape[1]):
            token = token + r.meta[mp * images + i, k] * small(ROW_META + k)
        line = lax.broadcasted_iota(jnp.int32, (8, width), 0)
        r.start[pl.ds(i * rows, 8), :] += jnp.where(
            line == 0, small(ROW_CLS), jnp.where(line == 1, token, 0.0)
        )
        clock.work(1.0)

    pack_grad()
    clock.work(1.5)

    clock.ensure(up_weight, 1)
    if inside:
        sensors, piece_rows = r.piece.shape[0], r.piece.shape[1]
        slots = 1 << dp_bits
        pixels_each = r.w_kernel.shape[0]
        bands = piece_rows // pixels_each
        patch_copies = []

        def patch_half(kernels, side):
            for m in range(blocks):
                pair = []
                for i in range(images):
                    tag = r.tags[m * images + i]
                    parts = [kernels[k, tag] for k in range(slots // 2)]
                    pair.append(jnp.concatenate(parts, axis=0))
                r.patch_send[m, side] = jnp.concatenate(pair, axis=1)
            for peer, m in others:
                spot = r.patch_recv.at[mp, side]
                patch_copies.append(push(r.patch_send.at[m, side], spot, peer))
            r.patch_recv[mp, side] = r.patch_send[mp, side]

        def patch_far():
            clock.ensure(gather_flow, 5)
            patch_half(r.kernels_far, 1 - dp_bit[0])

        def patch_end():
            for copy in patch_copies:
                copy.wait_recv()

        clock.ensure(gather_flow, 4)
        patch_flow = clock.add(
            [
                (lambda: patch_half(r.kernels_near, dp_bit[0]), LINK_X, 0.295 / RATE),
                (patch_far, LINK_X, 0.295 / RATE),
                (patch_end, None, 0.0),
            ]
        )
        clock.now += 0.7
        clock.ensure(patch_flow, 2)
        clock.now += 0.7
        clock.ensure(qkv_flow, 2)
        clock.ensure(out_flow, 2)
        clock.ensure(patch_flow, 3)
        for i in range(images):
            side_rows = []
            for side in range(2):
                part = [
                    r.patch_recv[m, side, :, i * block : (i + 1) * block] for m in range(blocks)
                ]
                side_rows.append(jnp.concatenate(part, axis=1).astype(f32))
            strips = []
            for b in range(bands):
                for d in range(slots):
                    first = (d // 2 * bands + b) * pixels_each
                    strips.append(side_rows[d % 2][first : first + pixels_each])
            r.patch[i] = jnp.concatenate(strips, axis=0).astype(bf16)
    clock.ensure(down_weight, 1)
    grad_flow = clock.add(
        [(grad_begin, LINK_X, 0.42 / RATE), (grad_end, None, 0.0)], at=clock.now + 8.0
    )

    for i in range(images):
        value = r.start[span_at(i), :] + nn_dot(r.chosen[mp * images + i], r.patch[i])
        r.start[span_at(i), :] = value
        scaled, _ = norm_stats(value)
        r.normed_one[span_at(i), :] = (
            scaled * small(ROW_LN1_GAIN) + small(ROW_LN1_BIAS)
        ).astype(bf16)
        clock.work(1.0)

    clock.ensure(qkv_flow, 4)
    for t in range(3):

        def project(j, carry, t=t):
            cols = tile_at(j)
            value = nt_dot(r.normed_one[...], r.wqkv[t, cols, :])
            if t == 0:
                value = value + r.small[ROW_BQ : ROW_BQ + 1, cols]
                value = value.astype(bf16).astype(f32) * (1.0 / math.sqrt(HD))
            if t == 2:
                value = value + r.small[ROW_BV : ROW_BV + 1, cols]
            r.qkv[t, :, cols] = value.astype(bf16)
            return carry

        lax.fori_loop(0, tiles, project, 0)
        clock.work(1.5)

    lane = lax.broadcasted_iota(jnp.int32, (1, LANES), 1)
    key_lane = lax.broadcasted_iota(jnp.int32, (1, rows), 1)

    def soft_copy(step, out):
        slot = step % 2
        near, distant = r.soft_slots.at[slot], r.soft.at[step]
        if out:
            return pltpu.make_async_copy(near, distant, r.soft_sems.at[0, slot])
        return pltpu.make_async_copy(distant, near, r.soft_sems.at[1, slot])

    def attend(step, carry):
        image = step // pairs
        pair = step % pairs
        span = pl.ds(mul16(image * rows), rows)
        cols = pl.ds(pl.multiple_of(pair * LANES, LANES), LANES)
        q, k, v = r.qkv[0, span, cols], r.qkv[1, span, cols], r.qkv[2, span, cols]

        @pl.when(step >= 2)
        def _():
            soft_copy(step - 2, True).wait()

        parts = []
        for h in range(2):
            mine = (lane >= HD) if h else (lane < HD)
            scores = nt_dot(jnp.where(mine, q, jnp.zeros_like(q)), k)
            scores = jnp.where(key_lane < length, scores, -1e30)
            top = jnp.max(scores, axis=1, keepdims=True)
            power = jnp.exp(scores - top)
            soft = power * (1.0 / jnp.sum(power, axis=1, keepdims=True))
            soft = soft.astype(bf16)
            r.soft_slots[step % 2, h] = soft
            parts.append(nn_dot(soft, v))
        soft_copy(step, True).start()
        r.attended[span, cols] = jnp.where(lane < HD, parts[0], parts[1]).astype(bf16)
        return carry

    groups = 6
    count = steps_count // groups
    for g in range(groups):
        lax.fori_loop(g * count, (g + 1) * count, attend, 0)
        clock.work(2.0)
    for step in (steps_count - 2, steps_count - 1):
        soft_copy(step, True).wait()
    clock.ensure(out_flow, 4)

    def project_out(j, carry):
        cols = tile_at(j)
        r.middle[:, cols] = (
            r.start[:, cols]
            + nn_dot(r.attended[...], r.wout[:, cols])
            + r.small[ROW_B_OUT : ROW_B_OUT + 1, cols]
        )
        return carry

    lax.fori_loop(0, tiles, project_out, 0)
    clock.work(1.5)

    for i in range(images):
        scaled, _ = norm_stats(r.middle[span_at(i), :])
        r.normed_two[span_at(i), :] = (
            scaled * small(ROW_LN2_GAIN) + small(ROW_LN2_BIAS)
        ).astype(bf16)
        r.total[span_at(i), :] = r.middle[span_at(i), :] + small(ROW_B_DOWN)
    r.normed_flip[...] = r.normed_two[...].T
    r.back[...] = jnp.zeros_like(r.back)
    r.small_sums[0] = jnp.zeros_like(r.small_sums[0])
    clock.work(2.0)
    clock.ensure(grad_flow, 2)
    clock.ensure(up_weight, 3 + len(UP_BITS))
    clock.ensure(down_weight, 3 + len(DOWN_BITS))

    def reduction(work, recv, order, fin):
        state = Bag()
        size = work.shape[2]
        amount = size * work.shape[3] * 2 / 1e6
        split = [b for b in order if b != ACROSS][:halves]

        def half(high, bit):
            return pl.ds(mul16(bit * (high // 2)), high // 2)

        def views(level, stage):
            ref = recv[level]
            if stage == ACROSS:
                return ref.at[x_bit], ref.at[1 - x_bit], across_x
            bit, peer = dp_bit[stage], bit_peer[stage]
            if stage not in split:
                return ref, ref, peer
            lead = (slice(None),) * (len(ref.shape) - 2)
            high = ref.shape[-2]
            return ref.at[(*lead, half(high, bit))], ref.at[(*lead, half(high, 1 - bit))], peer

        def begin():
            state.copy = push(work.at[:, 1 - core_bit], recv[0], core)
            state.work = state.copy

        def step(n):
            state.copy.wait_recv()
            if n == 0:
                recv[0][...] = recv[0][...] + work[:, core_bit]
                left(state.work)
            else:
                keep, _, _ = views(n - 1, order[n - 1])
                recv[n][...] = recv[n][...] + keep[...]
            if n < len(order):
                _, give, peer = views(n, order[n])
                state.copy = push(give, recv[n + 1], peer)

        def corner(count):
            offset = 0
            for n in range(count):
                offset = offset + dp_bit[split[n]] * (size >> (n + 1))
            return pl.ds(mul16(offset), size >> count)

        def last():
            step(len(order))
            source, spot = recv[len(order)], fin(corner(halves))
            state.local = carry_local(source, spot)
            state.copy = push(source, spot, bit_peer[split[halves - 1]])

        def spread(count):
            state.copy.wait_recv()
            if count == halves - 1:
                state.local.wait()
            spot = fin(corner(count))
            state.copy = push(spot, spot, bit_peer[split[count - 1]])

        def end():
            state.copy.wait_recv()

        def link_of(stage):
            return LINK_X if stage == ACROSS else LINK_Z if stage else LINK_Y

        def hops(stage):
            return 2 if stage == 2 else 1

        steps = [(begin, LINK_CORE, amount * 2 / PAIR_RATE)]
        now = amount * 2
        for n, stage in enumerate(order):
            if stage == ACROSS or stage in split:
                now /= 2
            cost = now * hops(stage) / RATE
            steps.append((lambda n=n: step(n), link_of(stage), cost))
        for count in range(halves, 0, -1):
            stage = split[count - 1]
            action = last if count == halves else lambda c=count: spread(c)
            steps.append((action, link_of(stage), (amount / 2**count) * hops(stage) / RATE))
        steps.append((end, None, 0.0))
        return steps

    wide_flows, up_flows = [], []

    def levels_of(base):
        return [r[base + n] for n in range(2 + dp_bits)]

    def wide_flow(chunk):
        work, recv = r.work_wide.at[chunk % 2], levels_of(WIDE + 10 * chunk)
        order = order_of(dp_bits, chunk in LATE_WIDE)
        fin = r.fin_down if chunk < tiles else r.fin_inner
        wide_flows.append(
            clock.add(reduction(work, recv, order, lambda s: fin.at[chunk % tiles, s]))
        )

    def up_flow(chunk):
        cols = slice(chunk * TILE, (chunk + 1) * TILE)
        work, recv = r.work_up.at[chunk % 2], levels_of(UP + 10 * chunk)
        order = order_of(dp_bits, chunk in LATE_UP)
        up_flows.append(clock.add(reduction(work, recv, order, lambda s: r.fin_up.at[s, cols])))

    order = blocks * tiles

    def fetch(j):
        m, slot = j % blocks, j % 2
        inner = tile_at(j // blocks)
        return (
            pltpu.make_async_copy(
                r.wup.at[m, :, inner], r.up_slots.at[slot], r.slot_sems.at[0, slot]
            ),
            pltpu.make_async_copy(
                r.wdown.at[m, inner, :], r.down_slots.at[slot], r.slot_sems.at[1, slot]
            ),
        )

    for copy in fetch(0):
        copy.start()

    def feed(j, carry):
        m, slot, part = j % blocks, j % 2, (j // blocks) % 2
        inner = tile_at(j // blocks)

        @pl.when(j + 1 < order)
        def _():
            for copy in fetch(j + 1):
                copy.start()

        for copy in fetch(j):
            copy.wait()
        up, down = r.up_slots[slot], r.down_slots[slot]
        hidden = nn_dot(r.normed_two[...], up)
        hidden = hidden + r.small[pl.ds(ROW_B_UP + m, 1), inner]
        value, slope = gelu_pair(hidden)
        value = value.astype(bf16)
        r.total[...] += nn_dot(value, down)
        grad = r.grad[...]
        r.work_wide[part, m // 2, m % 2] = tn_dot(value, grad).astype(bf16)
        hidden_grad = (nt_dot(grad, down) * slope).astype(bf16)
        r.small_sums[0, pl.ds(ROW_B_UP + m, 1), inner] = column_sum(hidden_grad.astype(f32))
        r.work_up[part, m // 2, m % 2] = nn_dot(r.normed_flip[...], hidden_grad).astype(bf16)
        r.back[...] += nt_dot(hidden_grad, up)
        return carry

    for c in range(tiles):
        if c >= 2:
            clock.ensure(wide_flows[c - 2], 2)
            clock.ensure(up_flows[c - 2], 2)
        for half in range(2):
            begin = c * blocks + half * blocks // 2
            lax.fori_loop(begin, begin + blocks // 2, feed, 0)
            clock.work(5.0)
        wide_flow(c)
        up_flow(c)

    def packed(value, m, size):
        lanes = slice(m * size, (m + 1) * size)
        return jnp.concatenate([value[i][:, lanes] for i in range(images)], axis=1)

    for copy in state.grad:
        left(copy)
    total = [r.total[span_at(i), :].astype(bf16) for i in range(images)]
    for m in range(blocks):
        r.encoded_send[m, 0:rows] = packed(total, m, block)
    out_copies = []

    def encoded_begin():
        for peer, m in others:
            out_copies.append(push(r.encoded_send.at[m, 0:rows], r.encoded.at[mp], peer))

    encoded_flow = clock.add([(encoded_begin, LINK_X, 0.42 / RATE)], at=clock.now)
    encoded_own = carry_local(r.encoded_send.at[mp, 0:rows], r.encoded.at[mp])
    clock.work(1.0)

    def add_small(row, value):
        r.small_sums[0, row : row + 1, :] += value

    for i in range(images):
        span = span_at(i)
        scaled, inverse = norm_stats(r.middle[span, :])
        grad = r.back[span, :]
        out = r.grad[span, :].astype(f32)
        add_small(ROW_LN2_GAIN, column_sum(grad * scaled))
        add_small(ROW_LN2_BIAS, column_sum(grad))
        add_small(ROW_B_DOWN, column_sum(out))
        middle_grad = out + norm_back(grad, small(ROW_LN2_GAIN), scaled, inverse)
        r.middle[span, :] = middle_grad
        branch = middle_grad.astype(bf16)
        r.branch[span, :] = branch
        add_small(ROW_B_OUT, column_sum(branch.astype(f32)))
        clock.work(1.0)

    piece = block // 3

    def store_rows(t, j, value):
        for i in range(TILE // piece):
            unit = j * (TILE // piece) + i
            m, place = unit // 3, t * block + (unit % 3) * piece
            chunk, row = tiles + place // TILE, place % TILE
            clock.ensure(wide_flows[chunk - 2], 2)
            r.work_wide[chunk % 2, m // 2, m % 2, row : row + piece, :] = value[
                i * piece : (i + 1) * piece
            ].astype(bf16)

    for j in range(tiles):
        cols = slice(j * TILE, (j + 1) * TILE)
        r.gattended[:, cols] = nt_dot(r.branch[...], r.wout[cols, :]).astype(bf16)
        store_rows(0, j, tn_dot(r.attended[:, cols], r.branch[...]))
        clock.work(1.5)

    def attend_back(step, carry):
        image = step // pairs
        pair = step % pairs
        span = pl.ds(mul16(image * rows), rows)
        cols = pl.ds(pl.multiple_of(pair * LANES, LANES), LANES)

        @pl.when(step + 1 < steps_count)
        def _():
            soft_copy(step + 1, False).start()

        soft_copy(step, False).wait()
        q, k, v = r.qkv[0, span, cols], r.qkv[1, span, cols], r.qkv[2, span, cols]
        ga = r.gattended[span, cols]
        parts = []
        for h in range(2):
            mine = (lane >= HD) if h else (lane < HD)
            soft = r.soft_slots[step % 2, h]
            soft_wide = soft.astype(f32)
            prob = nt_dot(jnp.where(mine, ga, jnp.zeros_like(ga)), v)
            delta = jnp.sum(soft_wide * prob, axis=1, keepdims=True)
            score_grad = (soft_wide * (prob - delta)).astype(bf16)
            parts.append((nn_dot(score_grad, k), tn_dot(score_grad, q), tn_dot(soft, ga)))
        one, two = parts
        gq = jnp.where(lane < HD, one[0], two[0]) * (1.0 / math.sqrt(HD))
        r.qkv[0, span, cols] = gq.astype(bf16)
        r.qkv[1, span, cols] = jnp.where(lane < HD, one[1], two[1]).astype(bf16)
        r.qkv[2, span, cols] = jnp.where(lane < HD, one[2], two[2]).astype(bf16)
        return carry

    soft_copy(0, False).start()
    for g in range(groups):
        lax.fori_loop(g * count, (g + 1) * count, attend_back, 0)
        clock.work(3.0)

    for t, row in ((0, ROW_BQ), (2, ROW_BV)):
        add_small(row, column_sum(r.qkv[t].astype(f32)))

    r.back[...] = jnp.zeros_like(r.back)
    for t in range(3):

        def project_back(j, carry, t=t):
            cols = tile_at(j)
            r.back[...] += nn_dot(r.qkv[t, :, cols], r.wqkv[t, cols, :])
            return carry

        lax.fori_loop(0, tiles, project_back, 0)
        clock.work(1.5)

    tokens = []
    for i in range(images):
        span = span_at(i)
        scaled, inverse = norm_stats(r.start[span, :])
        grad = r.back[span, :]
        add_small(ROW_LN1_GAIN, column_sum(grad * scaled))
        add_small(ROW_LN1_BIAS, column_sum(grad))
        begin = r.middle[span, :] + norm_back(grad, small(ROW_LN1_GAIN), scaled, inverse)
        add_small(ROW_CLS, begin[0:1, :])
        for k in range(r.meta.shape[1]):
            add_small(ROW_META + k, r.meta[mp * images + i, k] * begin[1:2, :])
        tokens.append(begin.astype(bf16))
    clock.ensure(encoded_flow, 1)
    encoded_own.wait()
    for copy in out_copies:
        left(copy)
    for m in range(blocks):
        r.token_send[m, 0:rows] = packed(tokens, m, block)
    token_copies = []

    def token_begin():
        for peer, m in others:
            token_copies.append(push(r.token_send.at[m, 0:rows], r.token_recv.at[mp], peer))
        r.token_recv[mp] = r.token_send[mp, 0:rows]

    def token_end():
        for copy in token_copies:
            copy.wait_recv()

    token_flow = clock.add([(token_begin, LINK_X, 0.42 / RATE), (token_end, None, 0.0)])
    clock.work(2.0)

    def all_sum(levels, out):
        state = Bag()

        def step(level):
            if level:
                state.copy.wait_recv()
                levels[level] = levels[level] + levels[level - 1]
            if level < len(peers):
                state.copy = push(levels.at[level], levels.at[level + 1], peers[level])
            else:
                out(levels[level])

        links = [LINK_CORE, LINK_X, LINK_Y] + [LINK_Z] * (dp_bits - 1) + [None]
        return [(lambda n=n: step(n), link, 1.5) for n, link in enumerate(links)]

    def store_small(value):
        narrow = jnp.zeros(r.gnarrow.shape, f32)
        bias = jnp.zeros(r.gbias.shape, f32)
        for m in range(blocks):
            narrow += jnp.where(mp == m, value[:, m * block : (m + 1) * block], 0.0)
            bias += jnp.where(mp == m, value[ROW_B_UP + m : ROW_B_UP + m + 1, :], 0.0)
        r.gnarrow[...] = narrow
        r.gbias[...] = bias

    def wave_sum():
        copies = []

        def over_mp():
            for peer, _ in others:
                copies.append(push(r.wave_parts.at[mp], r.wave_parts.at[mp], peer))

        def over_dp():
            for copy in copies:
                copy.wait_recv()
            copies.clear()
            r.wave_chips[dp] = sum(r.wave_parts[m] for m in range(blocks))
            for peer in bit_peer + mixed:
                copies.append(push(r.wave_chips.at[dp], r.wave_chips.at[dp], peer))

        def end():
            for copy in copies:
                copy.wait_recv()
            r.gwave[...] = sum(r.wave_chips[d] for d in range(1 << dp_bits))

        return [(over_mp, LINK_SMALL, 1.0), (over_dp, LINK_SMALL, 3.0), (end, None, 0.0)]

    clock.add(all_sum(r.small_sums, store_small))
    def pixel_gradient():
        pixel_back = [nt_dot(tokens[i], r.patch[i]).astype(bf16) for i in range(images)]
        for m in range(blocks):
            r.pixel_send[m] = packed(pixel_back, m, depth // blocks)

        def pixel_begin():
            for peer, m in others:
                out_copies.append(push(r.pixel_send.at[m], r.pixel_grad.at[mp], peer))

        clock.add([(pixel_begin, LINK_X, 0.28 / RATE)], at=clock.now)
        pixel_own = carry_local(r.pixel_send.at[mp], r.pixel_grad.at[mp])
        clock.work(1.5)
        return pixel_own

    def chunks_ready(count):
        while len(wide_flows) < tiles + count:
            wide_flow(len(wide_flows))

    def weight_rows(t, source):
        for j in range(tiles):
            cols = slice(j * TILE, (j + 1) * TILE)
            store_rows(t, j, tn_dot(r.qkv[source, :, cols], r.normed_one[...]))
            clock.work(0.8)
        chunks_ready((t + 1) * block // TILE)

    if inside:
        def sensor_sums():
            r.total[...] = jnp.zeros_like(r.total)
            r.back[...] = jnp.zeros_like(r.back)
            lane_block = lax.broadcasted_iota(jnp.int32, (1, width), 1) // block
            for m in range(blocks):
                for i in range(images):
                    c = m * images + i
                    part = r.token_recv[m, :, i * block : (i + 1) * block]
                    part = tn_dot(r.chosen[c], jnp.concatenate([part] * blocks, axis=1))
                    tag = r.tags[c]
                    r.total[0:depth, :] += jnp.where(lane_block == tag, part, 0.0)
                    r.back[0:depth, :] += jnp.where(lane_block + blocks == tag, part, 0.0)
                    clock.work(0.7)

            for flow in up_flows:
                clock.ensure(flow, 2)

            def slot_of(d):
                return tuple((d >> b) % 2 for b in KERNEL_ORDER)

            for s in range(sensors):
                store = r.total if s < blocks else r.back
                part = store[0:depth, s % blocks * block : (s % blocks + 1) * block]
                for d in range(slots):
                    strips = [
                        part[(b * slots + d) * pixels_each : (b * slots + d + 1) * pixels_each]
                        for b in range(bands)
                    ]
                    line = slice(s * piece_rows, (s + 1) * piece_rows)
                    r.work_up[(*slot_of(d), line, slice(0, block))] = jnp.concatenate(
                        strips, axis=0
                    ).astype(bf16)
            clock.work(1.0)

        cut = 3 * piece_rows

        def kernel_flow(half):
            here = Bag()
            order = KERNEL_ORDER
            lines = slice(cut, sensors * piece_rows) if half else slice(0, cut)

            def source(level):
                if level == 0:
                    return r.work_up.at[:, :, :, lines, :]
                return r[KERNEL + level - 1].at[(slice(None),) * (3 - level) + (lines,)]

            def step(level):
                if level:
                    target = source(level)
                    here.copy.wait_recv()
                    target[...] = target[...] + source(level - 1)[dp_bit[order[level - 1]]]
                if level < 3:
                    give = source(level).at[1 - dp_bit[order[level]]]
                    here.copy = push(give, source(level + 1), bit_peer[order[level]])
                    return
                state.shares.append(half)
                if len(state.shares) == 2:
                    kernel_end()

            steps = []
            for n, b in enumerate(order):
                cost = (0.69, 0.34, 0.17)[n] / 2 * (2 if b == 2 else 1) / RATE
                steps.append((lambda n=n: step(n), LINK_Z if b else LINK_Y, cost))
            return steps + [(lambda: step(3), None, 0.0)]

        def kernel_end():
            flat = r[KERNEL + dp_bits - 1][:, 0:block]
            r.share[...] = flat.astype(f32).reshape(r.share.shape)
            line = lax.broadcasted_iota(jnp.int32, (sensors * piece_rows, HYP), 0)
            wave = jnp.zeros((sensors * piece_rows, HYP), f32)
            for p in range(pixels_each):
                part = nn_dot(flat, r.w_kernel[p])
                wave = wave + jnp.where(line % pixels_each == p, part, 0.0)
            wave = jnp.sum(wave.reshape(sensors * bands, pixels_each, HYP), axis=1)
            r.wave_parts[mp] = wave
            clock.add(wave_sum())

        def sensor_stage():
            clock.ensure(token_flow, 2)
            sensor_sums()
            state.shares = []
            for half in range(2):
                clock.add(kernel_flow(half))

    else:

        def sensor_stage():
            clock.ensure(token_flow, 2)
            r.token_out[...] = r.token_recv[...]
            r.chosen_out[...] = r.chosen[...]

    for n, (t, source) in enumerate(((1, 2), (2, 0), (3, 1))):
        if PIXELS_AT == n:
            pixel_own = pixel_gradient()
        if SENSORS_AT == n:
            sensor_stage()
        weight_rows(t, source)
    if PIXELS_AT == 3:
        pixel_own = pixel_gradient()
    if SENSORS_AT == 3:
        sensor_stage()

    clock.drain()
    pixel_own.wait()
    for copy in out_copies:
        copy.wait_recv()
    for copy in sent:
        copy.wait_send()


def layer(length, dp_bits, inside, scalars, arrays, distant):
    piece, pixels = arrays["piece"], distant["pixels"]
    rows = -(-length // ROW_TILE) * ROW_TILE
    chips, patches, depth = pixels.shape
    block, width = distant["wout_shard"].shape
    blocks = width // block
    images = chips // blocks
    total = images * rows
    steps = images * width // LANES
    tiles = width // TILE
    halves = min(3, dp_bits)

    def vmem(*size, kind=bf16):
        return pltpu.VMEM(size, kind)

    anywhere = pl.BlockSpec(memory_space=pl.ANY)
    near = pl.BlockSpec(memory_space=pltpu.VMEM)
    scalar = pl.BlockSpec(memory_space=pltpu.SMEM)
    names, operands, in_specs = list(scalars), list(scalars.values()), [scalar] * len(scalars)
    for group, spec in ((arrays, near), (distant, anywhere)):
        names += list(group)
        operands += list(group.values())
        in_specs += [spec] * len(group)

    outs = dict(
        encoded=((blocks, rows, images * block), bf16, anywhere),
        pixel_grad=((blocks, rows, images * depth // blocks), bf16, anywhere),
        gnarrow=((SMALL_ROWS, block), f32, near),
        gbias=((1, width), f32, near),
        fin_down=((tiles, TILE, width), bf16, anywhere),
        fin_inner=((tiles, TILE, width), bf16, anywhere),
        fin_up=((width, width), bf16, anywhere),
    )
    if inside:
        sensors, piece_rows, _ = piece.shape
        outs.update(share=(piece.shape, f32, near))
        bands = piece_rows // arrays["w_kernel"].shape[0]
        outs.update(gwave=((sensors * bands, HYP), f32, near))
    else:
        outs.update(token_out=((blocks, rows, images * block), bf16, near))
        outs.update(chosen_out=((chips, rows, depth), bf16, near))
    results = list(outs)
    outs.update(wup=((blocks, width, width), bf16, anywhere))
    outs.update(wdown=((blocks, width, width), bf16, anywhere))
    outs.update(soft=((steps, 2, rows, rows), bf16, anywhere))

    scratch = dict(
        index=vmem(rows, chips, kind=jnp.int32),
        narrow=vmem(SMALL_ROWS, block, kind=f32),
        bias_up=vmem(8, width, kind=f32),
        narrow_all=vmem(blocks, SMALL_ROWS, block, kind=f32),
        bias_all=vmem(blocks, 8, width, kind=f32),
        small=vmem(SMALL_ROWS, width, kind=f32),
        grad_recv=vmem(blocks, rows, images * block),
        grad=vmem(total, width),
        chosen=vmem(chips, rows, depth),
        start=vmem(total, width, kind=f32),
        middle=vmem(total, width, kind=f32),
        normed_one=vmem(total, width),
        normed_two=vmem(total, width),
        normed_flip=vmem(width, total),
        qkv=vmem(3, total, width),
        attended=vmem(total, width),
        total=vmem(total, width, kind=f32),
        back=vmem(total, width, kind=f32),
        wqkv=vmem(3, width, width),
        wout=vmem(width, width),
        up_slots=vmem(2, width, TILE),
        down_slots=vmem(2, TILE, width),
        soft_slots=vmem(2, 2, rows, rows),
        small_sums=vmem(3 + dp_bits, SMALL_ROWS, width, kind=f32),
        work_wide=vmem(2, 2, 2, TILE, width),
        work_up=vmem(2, 2, 2, width, TILE),
        token_recv=vmem(blocks, rows, images * block),
        pixel_send=vmem(blocks, rows, images * depth // blocks),
    )
    if inside:
        scratch.update(kernels_near=vmem(1 << (dp_bits - 1), *piece.shape))
        scratch.update(kernels_far=vmem(1 << (dp_bits - 1), *piece.shape))
        for n in range(dp_bits):
            lead = (2,) * (dp_bits - 1 - n)
            scratch[KERNEL + n] = vmem(*lead, sensors * piece_rows, TILE)
        scratch.update(patch_send=vmem(blocks, 2, depth // 2, images * block))
        scratch.update(patch_recv=vmem(blocks, 2, depth // 2, images * block))
        scratch.update(encoded_send=vmem(blocks, rows, images * block))
        scratch.update(patch=vmem(images, depth, width))
        scratch.update(wave_parts=vmem(blocks, sensors * bands, HYP, kind=f32))
        scratch.update(wave_chips=vmem(1 << dp_bits, sensors * bands, HYP, kind=f32))
    else:
        scratch.update(encoded_send=vmem(blocks, rows, images * block))
        scratch.update(token_send=vmem(blocks, rows, images * block))
    for base, amount, high, wide in ((WIDE, 2 * tiles, TILE, width), (UP, tiles, width, TILE)):
        for chunk in range(amount):
            along = order_of(dp_bits, chunk in (LATE_UP if base == UP else LATE_WIDE))
            scratch[base + 10 * chunk] = vmem(2, high, wide)
            lead, now, cut = (2,), high, 0
            for n, stage in enumerate(along):
                if stage == ACROSS:
                    lead = ()
                elif cut < halves:
                    now, cut = now // 2, cut + 1
                scratch[base + 10 * chunk + 1 + n] = vmem(*lead, now, wide)
    copies = 36 + 9 * (2 + dp_bits + halves) + 2 * (2 + dp_bits) + 32 + dp_bits
    dma = pltpu.SemaphoreType.DMA
    scratch.update(local_sems=dma((24,)))
    scratch.update(send_sems=dma((copies,)))
    scratch.update(recv_sems=dma((copies,)))
    scratch.update(slot_sems=dma((2, 2)))
    scratch.update(soft_sems=dma((2, 2)))
    scratch.update(pixel_sems=dma((2, patches // TILE)))

    names += [*outs, *scratch]

    def kernel(*refs):
        labels, refs = list(names), list(refs)
        twice = dict(branch="grad", gattended="normed_two")
        if inside:
            twice.update(token_send="encoded_send")
        for second, first in twice.items():
            labels.append(second)
            refs.append(refs[names.index(first)])
        layer_kernel(labels, length, dp_bits, inside, *refs)

    values = pl.pallas_call(
        kernel,
        in_specs=in_specs,
        out_specs=[spec for _, _, spec in outs.values()],
        out_shape=[jax.ShapeDtypeStruct(size, kind) for size, kind, _ in outs.values()],
        scratch_shapes=list(scratch.values()),
        compiler_params=pltpu.CompilerParams(
            vmem_limit_bytes=VMEM_LIMIT,
            fuse_transposed_lhs_in_matmul=True,
            collective_id=0,
            has_side_effects=True,
        ),
        name="layer",
    )(*operands)
    return Refs(outs, values)


def per_device(
    dp_bits,
    pixels,
    meta,
    tags,
    visible,
    wavelength,
    w_hyp,
    b_hyp,
    w_kernel,
    w_meta,
    cls_token,
    ln1_gain,
    ln1_bias,
    w_qkv,
    b_qv,
    w_out,
    b_out,
    ln2_gain,
    ln2_bias,
    w_up,
    b_up,
    w_down,
    b_down,
    cotangent,
):
    width = w_qkv.shape[0]
    block = cls_token.shape[0]
    blocks = width // block
    sensors, bands = wavelength.shape
    chips, patches, depth = pixels.shape
    pixels_each = w_kernel.shape[1]
    length = visible.shape[1] + 2
    rows = -(-length // ROW_TILE) * ROW_TILE
    images = chips // blocks
    inside = dp_bits == 3 and bands * pixels_each % ROW_TILE == 0

    wave_table = wave_code(wavelength)
    wave_pre = jnp.einsum("sbi,ij->sbj", wave_table, w_hyp, precision=highest) + b_hyp
    wave_hidden, wave_back = jax.vjp(jax.nn.gelu, wave_pre)
    wave_low = wave_hidden.astype(bf16)
    kernel = jnp.einsum("sbj,jpf->sbpf", wave_low, w_kernel, preferred_element_type=f32)
    kernel = kernel.astype(bf16)

    scalars = dict(meta=meta, tags=tags)
    arrays = dict(
        piece=kernel.reshape(sensors, bands * pixels_each, block),
        w_meta=w_meta,
        cls=cls_token[None],
        gain_one=ln1_gain[None],
        bias_one=ln1_bias[None],
        b_qv=b_qv,
        b_out=b_out[None],
        gain_two=ln2_gain[None],
        bias_two=ln2_bias[None],
        b_down=b_down[None],
        b_up=b_up,
        w_kernel=w_kernel.transpose(1, 2, 0),
        visible=visible,
        grad_rows=cotangent.transpose(1, 0, 2),
    )
    distant = dict(
        pixels=pixels,
        table=jnp.asarray(pos_table(patches, width)),
        wqkv_shard=w_qkv.transpose(1, 2, 0),
        wout_shard=w_out,
        wup_shard=w_up,
        wdown_shard=w_down,
    )
    if not inside:
        kernel = lax.all_gather(kernel, "dp", axis=2, tiled=True)
        kernel = kernel.reshape(sensors, depth, block)
        arrays.update(patch=lax.all_to_all(kernel[tags], "mp", 0, 2, tiled=True))
    got = layer(length, dp_bits, inside, scalars, arrays, distant)

    def unpack(value, size):
        value = value.reshape(blocks, rows, images, size).transpose(0, 2, 1, 3)
        return value.reshape(chips, rows, size)

    encoded = unpack(got.encoded, block)[:, :length]
    pixel_grad = unpack(got.pixel_grad, depth // blocks)[:, 2:length]
    wave_float = wave_low.astype(f32)
    if inside:
        share = got.share.reshape(sensors, bands, pixels_each, block)
        grad_wave = got.gwave.reshape(sensors, bands, HYP)
    else:
        select = (tags[:, None] == jnp.arange(sensors, dtype=jnp.int32)[None, :]).astype(f32)
        token_grad = unpack(got.token_out, block)
        chip_grad = jnp.einsum(
            "cvk,cvf->ckf", got.chosen_out, token_grad, preferred_element_type=f32
        )
        share = jnp.einsum("cs,ckf->skf", select, chip_grad, precision=highest)
        share = share.reshape(sensors, bands, depth // bands, block)
        share = lax.psum_scatter(share, "dp", scatter_dimension=2, tiled=True)
        grad_wave = lax.psum(
            jnp.einsum("sbpf,jpf->sbj", share, w_kernel.astype(f32), precision=highest),
            ("dp", "mp"),
        )
    grad_w_kernel = jnp.einsum("sbj,sbpf->jpf", wave_float, share, precision=highest)
    grad_pre = wave_back(grad_wave)[0]
    grad_w_hyp = jnp.einsum("sbi,sbj->ij", wave_table, grad_pre, precision=highest)
    grad_b_hyp = jnp.sum(grad_pre, axis=(0, 1))

    gdown = got.fin_down.reshape(width, width).astype(f32)
    gup = got.fin_up.astype(f32)
    inner = got.fin_inner.reshape(4, block, width)
    gout = inner[0].astype(f32)
    gqkv = jnp.stack([inner[2], inner[3], inner[1]]).transpose(2, 0, 1).astype(f32)
    gnarrow = got.gnarrow
    return (
        encoded,
        pixel_grad,
        grad_w_hyp,
        grad_b_hyp,
        grad_w_kernel,
        gnarrow[ROW_META : ROW_META + w_meta.shape[0]],
        gnarrow[ROW_CLS],
        gnarrow[ROW_LN1_GAIN],
        gnarrow[ROW_LN1_BIAS],
        gqkv,
        gnarrow[ROW_BQ : ROW_BV + 1],
        gout,
        gnarrow[ROW_B_OUT],
        gnarrow[ROW_LN2_GAIN],
        gnarrow[ROW_LN2_BIAS],
        gup,
        got.gbias[0],
        gdown,
        gnarrow[ROW_B_DOWN],
    )


def solution(mesh):
    dp_bits = mesh.shape["dp"].bit_length() - 1
    return jax.shard_map(
        functools.partial(per_device, dp_bits),
        mesh=mesh,
        in_specs=(
            P("dp", None, None),
            P("dp", None),
            P("dp"),
            P("dp", None),
            P(),
            P(),
            P(),
            P(None, "dp", "mp"),
            P(None, "mp"),
            P("mp"),
            P("mp"),
            P("mp"),
            P(None, None, "mp"),
            P(None, "mp"),
            P("mp", None),
            P("mp"),
            P("mp"),
            P("mp"),
            P(None, "mp"),
            P("mp"),
            P("mp", None),
            P("mp"),
            P("dp", None, "mp"),
        ),
        out_specs=(
            P("dp", None, "mp"),
            P("dp", None, "mp"),
            P(),
            P(),
            P(None, "dp", "mp"),
            P(None, "mp"),
            P("mp"),
            P("mp"),
            P("mp"),
            P(None, None, "mp"),
            P(None, "mp"),
            P("mp", None),
            P("mp"),
            P("mp"),
            P("mp"),
            P(None, "mp"),
            P("mp"),
            P("mp", None),
            P("mp"),
        ),
        check_vma=False,
    )
```

```python
import functools
import itertools
import math

import jax
import jax.numpy as jnp
import numpy as np
from jax import lax
from jax.experimental import pallas as pl
from jax.experimental.pallas import tpu as pltpu
from jax.sharding import PartitionSpec as P

HD = 64
HYP = 128
LANES = 128
TILE = 256
ROW_TILE = 16

norm_epsilon = 1e-05
highest = lax.Precision.HIGHEST
f32 = jnp.float32
bf16 = jnp.bfloat16
VMEM_LIMIT = 62 * 1024 * 1024
MESH = pl.DeviceIdType.MESH

ROW_META = 0
ROW_CLS = 8
ROW_LN1_GAIN = 9
ROW_LN1_BIAS = 10
ROW_BQ = 11
ROW_BV = 12
ROW_B_OUT = 13
ROW_LN2_GAIN = 14
ROW_LN2_BIAS = 15
ROW_B_DOWN = 16
ROW_B_UP = 17
SMALL_ROWS = 24


def wave_code(wavelength):
    half_width = HYP // 2
    ladder = jnp.arange(half_width, dtype=f32) * (math.log(100.0) / half_width)
    angle_grid = wavelength[..., None] * jnp.exp(ladder)
    return jnp.concatenate([jnp.sin(angle_grid), jnp.cos(angle_grid)], axis=-1)


def pos_table(patch_count, width):
    index = np.arange(patch_count, dtype=np.float64)[:, None]
    feature = np.arange(width)[None, :]
    angle = index * np.exp((feature // 2) * (-2.0 * math.log(10000.0) / width))
    table = np.where(feature % 2 == 0, np.sin(angle), np.cos(angle)).astype(np.float32)
    return table.astype(jnp.bfloat16)


def nn_dot(left, right):
    return lax.dot_general(left, right, (((1,), (0,)), ((), ())), preferred_element_type=f32)


def nt_dot(left, right):
    return lax.dot_general(left, right, (((1,), (1,)), ((), ())), preferred_element_type=f32)


def tn_dot(left, right):
    return lax.dot_general(left, right, (((0,), (0,)), ((), ())), preferred_element_type=f32)


def gelu_pair(u):
    c = math.sqrt(2.0 / math.pi)
    square = u * u
    t = jnp.tanh(c * u * (1.0 + 0.044715 * square))
    half = 0.5 * (1.0 + t)
    slope = half + 0.5 * u * (1.0 - t * t) * (c * (1.0 + 3.0 * 0.044715 * square))
    return u * half, slope


def norm_stats(x):
    width = x.shape[1]
    center = jnp.sum(x, axis=1, keepdims=True) * (1.0 / width)
    square = jnp.sum(x * x, axis=1, keepdims=True) * (1.0 / width)
    inverse = lax.rsqrt(square - center * center + norm_epsilon)
    return (x - center) * inverse, inverse


def hot_rows(index, count):
    lane = lax.broadcasted_iota(jnp.int32, (index.shape[0], count), 1)
    return jnp.where(index == lane, 1.0, 0.0).astype(bf16)


def norm_back(grad, gain, scaled, inverse):
    width = grad.shape[1]
    weighted = grad * gain
    first = jnp.sum(weighted, axis=1, keepdims=True) * (1.0 / width)
    second = jnp.sum(weighted * scaled, axis=1, keepdims=True) * (1.0 / width)
    return inverse * (weighted - first - scaled * second)


def column_sum(x):
    return jnp.sum(x, axis=0, keepdims=True)


class Flow:
    def __init__(self, clock, steps, ready):
        self.clock, self.steps, self.next, self.ready = clock, steps, 0, ready

    @property
    def open(self):
        return self.next < len(self.steps)

    def due(self):
        _, link, _ = self.steps[self.next]
        return max(self.ready, self.clock.busy.get(link, 0.0) - self.clock.slack)

    def go(self):
        action, link, cost = self.steps[self.next]
        clock = self.clock
        clock.now = max(clock.now, self.ready)
        action()
        self.next += 1
        clock.now += clock.start
        begin = max(clock.now, clock.busy.get(link, 0.0))
        if link is not None:
            clock.busy[link] = begin + cost
        self.ready = begin + cost + clock.latency


class Clock:
    latency, slack, start = 1.5, 6.0, 0.3

    def __init__(self):
        self.now, self.busy, self.flows = 0.0, {}, []

    def add(self, steps, at=None):
        flow = Flow(self, steps, self.now if at is None else at)
        self.flows.append(flow)
        if at is None:
            flow.go()
        return flow

    def ensure(self, flow, count):
        if not flow.next:
            flow.ready = min(flow.ready, self.now)
        while flow.next < count:
            flow.go()

    def work(self, cost):
        self.now += cost
        self.pump()

    def pump(self):
        while True:
            due = [f for f in self.flows if f.open and f.due() <= self.now]
            if not due:
                return
            min(due, key=Flow.due).go()

    def drain(self):
        while True:
            left = [f for f in self.flows if f.open]
            if not left:
                return
            flow = min(left, key=Flow.due)
            self.now = max(self.now, flow.due())
            flow.go()


class Refs:
    def __init__(self, names, refs):
        self.named = dict(zip(names, refs, strict=True))

    def __getattr__(self, name):
        return self.named[name]

    def __getitem__(self, number):
        return self.named[number]


KERNEL, WIDE, UP = 0, 100, 200
ACROSS = -1


def order_of(dp_bits, late):
    if late:
        return [1, ACROSS, 0, *range(2, dp_bits)]
    return [ACROSS, *range(dp_bits)]


class Bag:
    pass


RATE = 0.05
PAIR_RATE = 0.3
LATE_WIDE, LATE_UP = (), ()
UP_BITS, DOWN_BITS = (0, 1), (0,)
HOLD = 18.0
UP_AT = 8.0
SENSORS_AT = 1
PIXELS_AT = 1
KERNEL_ORDER = (1, 0, 2)
LINK_CORE, LINK_X, LINK_Y, LINK_Z, LINK_SMALL = range(5)


def layer_kernel(names, length, dp_bits, inside, *refs):
    r = Refs(names, refs)
    halves = min(3, dp_bits)
    rows, width = r.index.shape[0], r.start.shape[1]
    chips, patches, depth = r.pixels.shape
    blocks = r.wup.shape[0]
    images = chips // blocks
    block = width // blocks
    tiles = width // TILE
    pairs = width // LANES
    steps_count = images * pairs

    mp, dp = lax.axis_index("mp"), lax.axis_index("dp")
    core_bit, x_bit = mp % 2, mp // 2
    core_mp, x_mp = mp + 1 - 2 * core_bit, mp + 2 - 4 * x_bit
    far_mp = blocks - 1 - mp
    dp_bit = [(dp // (1 << b)) % 2 for b in range(dp_bits)]

    def flip(*bits):
        value = dp
        for b in bits:
            value = value + (1 - 2 * dp_bit[b]) * (1 << b)
        return value

    core, across_x, diagonal = {"mp": core_mp}, {"mp": x_mp}, {"mp": far_mp}
    bit_peer = [{"dp": flip(b)} for b in range(dp_bits)]
    peers = [core, across_x, *bit_peer]
    others = [(core, core_mp), (across_x, x_mp), (diagonal, far_mp)]
    greeted = peers + [diagonal]
    if inside:
        mixed = [{"dp": flip(*bits)} for bits in ((0, 1), (0, 2), (1, 2), (0, 1, 2))]
        greeted += mixed

    barrier = pltpu.get_barrier_semaphore()
    for peer in greeted:
        pl.semaphore_signal(barrier, inc=1, device_id=peer, device_id_type=MESH)
    pl.semaphore_wait(barrier, len(greeted))

    sent, numbers, local_numbers = [], itertools.count(), itertools.count()

    def push(source, target, peer):
        number = next(numbers)
        copy = pltpu.make_async_remote_copy(
            src_ref=source,
            dst_ref=target,
            send_sem=r.send_sems.at[number],
            recv_sem=r.recv_sems.at[number],
            device_id=peer,
            device_id_type=MESH,
        )
        copy.start()
        sent.append(copy)
        return copy

    def left(copy):
        copy.wait_send()
        sent[:] = [c for c in sent if c is not copy]

    def carry_local(source, target):
        copy = pltpu.make_async_copy(source, target, r.local_sems.at[next(local_numbers)])
        copy.start()
        return copy

    def mul16(value):
        return pl.multiple_of(value, ROW_TILE)

    def tile_at(j):
        return pl.ds(pl.multiple_of(j * TILE, TILE), TILE)

    def span_at(i):
        return pl.ds(i * rows, rows)

    def small(row):
        return r.small[row : row + 1, :]

    clock = Clock()

    if inside:
        place = dp // 2
        r.kernels_near[place] = r.piece[...]
        sideways = bit_peer[0]
        direct = push(r.piece, r.kernels_far.at[place], sideways)
        along = []
        for peer, bits in ((bit_peer[1], (1,)), (mixed[2], (1, 2)), (bit_peer[2], (2,))):
            along.append((push(r.piece, r.kernels_near.at[place], peer), flip(*bits) // 2))
        passed = []

        def pass_on(n):
            copy, index = along[n]
            copy.wait_recv()
            passed.append(push(r.kernels_near.at[index], r.kernels_far.at[index], sideways))

        amount = 0.172
        gather_steps = [
            (lambda: None, LINK_Z, amount / RATE),
            (lambda: pass_on(0), LINK_Y, amount * 1.5 / RATE),
            (lambda: pass_on(1), LINK_Y, amount * 1.5 / RATE),
        ]

        def halfway():
            pass_on(2)

        gather_steps.append((halfway, LINK_Y, amount / RATE))

        def gather_end():
            direct.wait_recv()
            for copy in passed:
                copy.wait_recv()

        gather_steps.append((gather_end, None, 0.0))
        gather_flow = clock.add(gather_steps)

    r.narrow[...] = jnp.zeros_like(r.narrow)
    row = 0
    for part in (r.w_meta, r.cls, r.gain_one, r.bias_one, r.b_qv, r.b_out, r.gain_two, r.bias_two):
        r.narrow[row : row + part.shape[0], :] = part[...]
        row += part.shape[0]
    r.narrow[row : row + 1, :] = r.b_down[...]
    r.bias_up[...] = jnp.broadcast_to(r.b_up[...].reshape(1, width), r.bias_up.shape)
    narrow_copies = []
    for peer, _ in others:
        narrow_copies.append(push(r.narrow, r.narrow_all.at[mp], peer))
        narrow_copies.append(push(r.bias_up, r.bias_all.at[mp], peer))
    r.narrow_all[mp] = r.narrow[...]
    r.bias_all[mp] = r.bias_up[...]

    def weight_flow(shard, full, inner, bits, at=None):
        parts = 1 << len(bits)
        high = block if inner else shard.shape[0]
        lead = (slice(None),) if len(shard.shape) == 3 else ()

        def view(m, first, count):
            place = pl.ds(mul16(first * (high // parts)), count * (high // parts))
            if inner:
                place = pl.ds(
                    mul16(m * block + first * (high // parts)), count * (high // parts)
                )
                return full.at[(*lead, place)]
            return full.at[m, place, :]

        state = Bag()
        first = 0
        for n, b in enumerate(bits):
            first = first + dp_bit[b] * (1 << n)
        state.hands = []

        def begin():
            own = shard.at[(*lead, pl.ds(mul16(first * (high // parts)), high // parts))]
            state.local = carry_local(shard, view(mp, 0, parts))
            state.copy = push(own, view(mp, first, 1), across_x)

        state.hands.append(push(shard, view(mp, 0, parts), core))

        def held(n):
            start = 0
            for k in range(n, len(bits)):
                start = start + dp_bit[bits[k]] * (1 << k)
            return start, 1 << n

        def came(n):
            start, count = held(n)
            if n:
                count //= 2
                start = start + (1 - dp_bit[bits[n - 1]]) * count
            return start, count

        def relay(n):
            state.copy.wait_recv()
            if n < len(bits):
                piece = view(x_mp, *held(n))
                state.next = push(piece, piece, bit_peer[bits[n]])
            piece = view(x_mp, *came(n))
            state.hands.append(push(piece, piece, core))
            if n < len(bits):
                state.copy = state.next

        def end():
            state.local.wait()
            for copy in state.hands:
                copy.wait_recv()

        cost = math.prod(shard.shape) * 2 / parts / 1e6
        steps = [(begin, LINK_X, cost / RATE)]
        for n in range(len(bits)):
            link = LINK_Z if bits[n] else LINK_Y
            steps.append((lambda n=n: relay(n), link, cost * (1 << n) / RATE))
        steps.append((lambda: relay(len(bits)), LINK_CORE, cost * parts / 2 / PAIR_RATE))
        steps.append((end, None, 0.0))
        return clock.add(steps, at=at)

    qkv_flow = weight_flow(r.wqkv_shard, r.wqkv, True, (0,))
    out_flow = weight_flow(r.wout_shard, r.wout, True, (0,))
    up_weight = weight_flow(r.wup_shard, r.wup, False, UP_BITS, at=UP_AT)
    down_weight = weight_flow(r.wdown_shard, r.wdown, False, DOWN_BITS, at=1000.0)
    qkv_flow.ready = out_flow.ready = HOLD

    state = Bag()

    def grad_begin():
        state.grad = [push(r.encoded_send.at[m], r.grad_recv.at[mp], p) for p, m in others]
        r.grad_recv[mp] = r.encoded_send[mp]

    def grad_end():
        for copy in state.grad:
            copy.wait_recv()
        for i in range(images):
            r.grad[span_at(i), :] = jnp.concatenate(
                [r.grad_recv[m][:, i * block : (i + 1) * block] for m in range(blocks)], axis=1
            )

    def pack_grad():
        r.encoded_send[...] = jnp.zeros_like(r.encoded_send)
        for m in range(blocks):
            pair = [r.grad_rows[:, m * images + i, :] for i in range(images)]
            r.encoded_send[m, 0:length] = jnp.concatenate(pair, axis=1)

    turned = r.visible[...].astype(f32).T
    none = jnp.full((rows, chips), -1.0, f32)
    turned = jnp.concatenate([none[0:2], turned, none[length:rows]], axis=0)
    r.index[...] = turned.astype(jnp.int32)

    table_copies = []
    for k in range(patches // TILE):
        table_copies.append(
            carry_local(r.table.at[k * TILE : (k + 1) * TILE], r.work_wide.at[0, k // 2, k % 2])
        )

    def pixel_copies(c):
        lanes = slice((c % 2) * depth, (c % 2 + 1) * depth)
        return [
            pltpu.make_async_copy(
                r.pixels.at[c, k * TILE : (k + 1) * TILE],
                r.work_wide.at[1, k // 2, k % 2, :, lanes],
                r.pixel_sems.at[c % 2, k],
            )
            for k in range(patches // TILE)
        ]

    for copy in pixel_copies(0):
        copy.start()
    for c in range(chips):
        if c + 1 < chips:
            for copy in pixel_copies(c + 1):
                copy.start()
        for copy in pixel_copies(c):
            copy.wait()
        hot = hot_rows(r.index[:, c : c + 1], patches)
        lanes = slice((c % 2) * depth, (c % 2 + 1) * depth)
        value = 0.0
        for k in range(patches // TILE):
            value = value + nn_dot(
                hot[:, k * TILE : (k + 1) * TILE], r.work_wide[1, k // 2, k % 2, :, lanes]
            )
        r.chosen[c] = value.astype(bf16)
        clock.work(0.7)

    for copy in narrow_copies:
        copy.wait_recv()
    r.small[...] = jnp.concatenate([r.narrow_all[m] for m in range(blocks)], axis=1)
    for m in range(blocks):
        r.small[ROW_B_UP + m : ROW_B_UP + m + 1, :] = r.bias_all[m, 0:1, :]

    for copy in table_copies:
        copy.wait()
    chip_lane = lax.broadcasted_iota(jnp.int32, (rows, chips), 1)
    index_wide = r.index[...].astype(f32)
    for i in range(images):
        mine = jnp.where(chip_lane == mp * images + i, index_wide, 0.0)
        hot = hot_rows(jnp.sum(mine, axis=1, keepdims=True).astype(jnp.int32), patches)
        value = 0.0
        for k in range(patches // TILE):
            value = value + nn_dot(
                hot[:, k * TILE : (k + 1) * TILE], r.work_wide[0, k // 2, k % 2]
            )
        r.start[span_at(i), :] = value
        token = jnp.zeros((1, width), f32)
        for k in range(r.meta.shape[1]):
            token = token + r.meta[mp * images + i, k] * small(ROW_META + k)
        line = lax.broadcasted_iota(jnp.int32, (8, width), 0)
        r.start[pl.ds(i * rows, 8), :] += jnp.where(
            line == 0, small(ROW_CLS), jnp.where(line == 1, token, 0.0)
        )
        clock.work(1.0)

    pack_grad()
    clock.work(1.5)

    clock.ensure(up_weight, 1)
    if inside:
        sensors, piece_rows = r.piece.shape[0], r.piece.shape[1]
        slots = 1 << dp_bits
        pixels_each = r.w_kernel.shape[0]
        bands = piece_rows // pixels_each
        patch_copies = []

        def patch_half(kernels, side):
            for m in range(blocks):
                pair = []
                for i in range(images):
                    tag = r.tags[m * images + i]
                    parts = [kernels[k, tag] for k in range(slots // 2)]
                    pair.append(jnp.concatenate(parts, axis=0))
                r.patch_send[m, side] = jnp.concatenate(pair, axis=1)
            for peer, m in others:
                spot = r.patch_recv.at[mp, side]
                patch_copies.append(push(r.patch_send.at[m, side], spot, peer))
            r.patch_recv[mp, side] = r.patch_send[mp, side]

        def patch_far():
            clock.ensure(gather_flow, 5)
            patch_half(r.kernels_far, 1 - dp_bit[0])

        def patch_end():
            for copy in patch_copies:
                copy.wait_recv()

        clock.ensure(gather_flow, 4)
        patch_flow = clock.add(
            [
                (lambda: patch_half(r.kernels_near, dp_bit[0]), LINK_X, 0.295 / RATE),
                (patch_far, LINK_X, 0.295 / RATE),
                (patch_end, None, 0.0),
            ]
        )
        clock.now += 0.7
        clock.ensure(patch_flow, 2)
        clock.now += 0.7
        clock.ensure(qkv_flow, 2)
        clock.ensure(out_flow, 2)
        clock.ensure(patch_flow, 3)
        for i in range(images):
            side_rows = []
            for side in range(2):
                part = [
                    r.patch_recv[m, side, :, i * block : (i + 1) * block] for m in range(blocks)
                ]
                side_rows.append(jnp.concatenate(part, axis=1).astype(f32))
            strips = []
            for b in range(bands):
                for d in range(slots):
                    first = (d // 2 * bands + b) * pixels_each
                    strips.append(side_rows[d % 2][first : first + pixels_each])
            r.patch[i] = jnp.concatenate(strips, axis=0).astype(bf16)
    clock.ensure(down_weight, 1)
    grad_flow = clock.add(
        [(grad_begin, LINK_X, 0.42 / RATE), (grad_end, None, 0.0)], at=clock.now + 8.0
    )

    for i in range(images):
        value = r.start[span_at(i), :] + nn_dot(r.chosen[mp * images + i], r.patch[i])
        r.start[span_at(i), :] = value
        scaled, _ = norm_stats(value)
        r.normed_one[span_at(i), :] = (
            scaled * small(ROW_LN1_GAIN) + small(ROW_LN1_BIAS)
        ).astype(bf16)
        clock.work(1.0)

    clock.ensure(qkv_flow, 4)
    for t in range(3):

        def project(j, carry, t=t):
            cols = tile_at(j)
            value = nt_dot(r.normed_one[...], r.wqkv[t, cols, :])
            if t == 0:
                value = value + r.small[ROW_BQ : ROW_BQ + 1, cols]
                value = value.astype(bf16).astype(f32) * (1.0 / math.sqrt(HD))
            if t == 2:
                value = value + r.small[ROW_BV : ROW_BV + 1, cols]
            r.qkv[t, :, cols] = value.astype(bf16)
            return carry

        lax.fori_loop(0, tiles, project, 0)
        clock.work(1.5)

    lane = lax.broadcasted_iota(jnp.int32, (1, LANES), 1)
    key_lane = lax.broadcasted_iota(jnp.int32, (1, rows), 1)

    def soft_copy(step, out):
        slot = step % 4
        near, distant = r.soft_slots.at[slot], r.soft.at[step]
        if out:
            return pltpu.make_async_copy(near, distant, r.soft_sems.at[0, slot])
        return pltpu.make_async_copy(distant, near, r.soft_sems.at[1, slot])

    def place_of(step):
        image, pair = step // pairs, step % pairs
        span = pl.ds(mul16(image * rows), rows)
        return span, pl.ds(pl.multiple_of(pair * LANES, LANES), LANES)

    def attend_pair(step):
        span, cols = place_of(step)
        q, k, v = r.qkv[0, span, cols], r.qkv[1, span, cols], r.qkv[2, span, cols]
        parts, softs = [], []
        for h in range(2):
            mine = (lane >= HD) if h else (lane < HD)
            scores = nt_dot(jnp.where(mine, q, jnp.zeros_like(q)), k)
            scores = jnp.where(key_lane < length, scores, -1e30)
            top = jnp.max(scores, axis=1, keepdims=True)
            power = jnp.exp(scores - top)
            soft = power * (1.0 / jnp.sum(power, axis=1, keepdims=True))
            soft = soft.astype(bf16)
            softs.append(soft)
            parts.append(nn_dot(soft, v))
        return softs, jnp.where(lane < HD, parts[0], parts[1]).astype(bf16)

    def attend(turn, carry):
        two = (2 * turn, 2 * turn + 1)

        @pl.when(turn >= 2)
        def _():
            for step in two:
                soft_copy(step - 4, True).wait()

        for step, (softs, out) in zip(two, [attend_pair(step) for step in two]):
            for h in range(2):
                r.soft_slots[step % 4, h] = softs[h]
            soft_copy(step, True).start()
            span, cols = place_of(step)
            r.attended[span, cols] = out
        return carry

    groups = 3
    count = steps_count // 2 // groups
    for g in range(groups):
        lax.fori_loop(g * count, (g + 1) * count, attend, 0)
        clock.work(4.0)
    for step in range(steps_count - 4, steps_count):
        soft_copy(step, True).wait()
    clock.ensure(out_flow, 4)

    def project_out(j, carry):
        cols = tile_at(j)
        r.middle[:, cols] = (
            r.start[:, cols]
            + nn_dot(r.attended[...], r.wout[:, cols])
            + r.small[ROW_B_OUT : ROW_B_OUT + 1, cols]
        )
        return carry

    lax.fori_loop(0, tiles, project_out, 0)
    clock.work(1.5)

    for i in range(images):
        scaled, _ = norm_stats(r.middle[span_at(i), :])
        r.normed_two[span_at(i), :] = (
            scaled * small(ROW_LN2_GAIN) + small(ROW_LN2_BIAS)
        ).astype(bf16)
        r.total[span_at(i), :] = r.middle[span_at(i), :] + small(ROW_B_DOWN)
    r.normed_flip[...] = r.normed_two[...].T
    r.back[...] = jnp.zeros_like(r.back)
    r.small_sums[0] = jnp.zeros_like(r.small_sums[0])
    clock.work(2.0)
    clock.ensure(grad_flow, 2)
    clock.ensure(up_weight, 3 + len(UP_BITS))
    clock.ensure(down_weight, 3 + len(DOWN_BITS))

    def reduction(work, recv, order, fin):
        state = Bag()
        size = work.shape[2]
        amount = size * work.shape[3] * 2 / 1e6
        split = [b for b in order if b != ACROSS][:halves]

        def half(high, bit):
            return pl.ds(mul16(bit * (high // 2)), high // 2)

        def views(level, stage):
            ref = recv[level]
            if stage == ACROSS:
                return ref.at[x_bit], ref.at[1 - x_bit], across_x
            bit, peer = dp_bit[stage], bit_peer[stage]
            if stage not in split:
                return ref, ref, peer
            lead = (slice(None),) * (len(ref.shape) - 2)
            high = ref.shape[-2]
            return ref.at[(*lead, half(high, bit))], ref.at[(*lead, half(high, 1 - bit))], peer

        def begin():
            state.copy = push(work.at[:, 1 - core_bit], recv[0], core)
            state.work = state.copy

        def step(n):
            state.copy.wait_recv()
            if n == 0:
                recv[0][...] = recv[0][...] + work[:, core_bit]
                left(state.work)
            else:
                keep, _, _ = views(n - 1, order[n - 1])
                recv[n][...] = recv[n][...] + keep[...]
            if n < len(order):
                _, give, peer = views(n, order[n])
                state.copy = push(give, recv[n + 1], peer)

        def corner(count):
            offset = 0
            for n in range(count):
                offset = offset + dp_bit[split[n]] * (size >> (n + 1))
            return pl.ds(mul16(offset), size >> count)

        def last():
            step(len(order))
            source, spot = recv[len(order)], fin(corner(halves))
            state.local = carry_local(source, spot)
            state.copy = push(source, spot, bit_peer[split[halves - 1]])

        def spread(count):
            state.copy.wait_recv()
            if count == halves - 1:
                state.local.wait()
            spot = fin(corner(count))
            state.copy = push(spot, spot, bit_peer[split[count - 1]])

        def end():
            state.copy.wait_recv()

        def link_of(stage):
            return LINK_X if stage == ACROSS else LINK_Z if stage else LINK_Y

        def hops(stage):
            return 2 if stage == 2 else 1

        steps = [(begin, LINK_CORE, amount * 2 / PAIR_RATE)]
        now = amount * 2
        for n, stage in enumerate(order):
            if stage == ACROSS or stage in split:
                now /= 2
            cost = now * hops(stage) / RATE
            steps.append((lambda n=n: step(n), link_of(stage), cost))
        for count in range(halves, 0, -1):
            stage = split[count - 1]
            action = last if count == halves else lambda c=count: spread(c)
            steps.append((action, link_of(stage), (amount / 2**count) * hops(stage) / RATE))
        steps.append((end, None, 0.0))
        return steps

    wide_flows, up_flows = [], []

    def levels_of(base):
        return [r[base + n] for n in range(2 + dp_bits)]

    def wide_flow(chunk):
        work, recv = r.work_wide.at[chunk % 2], levels_of(WIDE + 10 * chunk)
        order = order_of(dp_bits, chunk in LATE_WIDE)
        fin = r.fin_down if chunk < tiles else r.fin_inner
        wide_flows.append(
            clock.add(reduction(work, recv, order, lambda s: fin.at[chunk % tiles, s]))
        )

    def up_flow(chunk):
        cols = slice(chunk * TILE, (chunk + 1) * TILE)
        work, recv = r.work_up.at[chunk % 2], levels_of(UP + 10 * chunk)
        order = order_of(dp_bits, chunk in LATE_UP)
        up_flows.append(clock.add(reduction(work, recv, order, lambda s: r.fin_up.at[s, cols])))

    order = blocks * tiles

    def fetch(j):
        m, slot = j % blocks, j % 2
        inner = tile_at(j // blocks)
        return (
            pltpu.make_async_copy(
                r.wup.at[m, :, inner], r.up_slots.at[slot], r.slot_sems.at[0, slot]
            ),
            pltpu.make_async_copy(
                r.wdown.at[m, inner, :], r.down_slots.at[slot], r.slot_sems.at[1, slot]
            ),
        )

    for copy in fetch(0):
        copy.start()

    def feed(j, carry):
        m, slot, part = j % blocks, j % 2, (j // blocks) % 2
        inner = tile_at(j // blocks)

        @pl.when(j + 1 < order)
        def _():
            for copy in fetch(j + 1):
                copy.start()

        for copy in fetch(j):
            copy.wait()
        up, down, grad = r.up_slots[slot], r.down_slots[slot], r.grad[...]
        hidden = nn_dot(r.normed_two[...], up) + r.small[pl.ds(ROW_B_UP + m, 1), inner]
        hidden_grad = nt_dot(grad, down)
        value, slope = gelu_pair(hidden)
        value = value.astype(bf16)
        hidden_grad = (hidden_grad * slope).astype(bf16)
        r.total[...] += nn_dot(value, down)
        r.back[...] += nt_dot(hidden_grad, up)
        r.work_wide[part, m // 2, m % 2] = tn_dot(value, grad).astype(bf16)
        r.work_up[part, m // 2, m % 2] = nn_dot(r.normed_flip[...], hidden_grad).astype(bf16)
        r.small_sums[0, pl.ds(ROW_B_UP + m, 1), inner] = column_sum(hidden_grad.astype(f32))
        return carry

    for c in range(tiles):
        if c >= 2:
            clock.ensure(wide_flows[c - 2], 2)
            clock.ensure(up_flows[c - 2], 2)
        for half in range(2):
            begin = c * blocks + half * blocks // 2
            lax.fori_loop(begin, begin + blocks // 2, feed, 0)
            clock.work(5.0)
        wide_flow(c)
        up_flow(c)

    def packed(value, m, size):
        lanes = slice(m * size, (m + 1) * size)
        return jnp.concatenate([value[i][:, lanes] for i in range(images)], axis=1)

    for copy in state.grad:
        left(copy)
    total = [r.total[span_at(i), :].astype(bf16) for i in range(images)]
    for m in range(blocks):
        r.encoded_send[m, 0:rows] = packed(total, m, block)
    out_copies = []

    def encoded_begin():
        for peer, m in others:
            out_copies.append(push(r.encoded_send.at[m, 0:rows], r.encoded.at[mp], peer))

    encoded_flow = clock.add([(encoded_begin, LINK_X, 0.42 / RATE)], at=clock.now)
    encoded_own = carry_local(r.encoded_send.at[mp, 0:rows], r.encoded.at[mp])
    clock.work(1.0)

    def add_small(row, value):
        r.small_sums[0, row : row + 1, :] += value

    for i in range(images):
        span = span_at(i)
        scaled, inverse = norm_stats(r.middle[span, :])
        grad = r.back[span, :]
        out = r.grad[span, :].astype(f32)
        add_small(ROW_LN2_GAIN, column_sum(grad * scaled))
        add_small(ROW_LN2_BIAS, column_sum(grad))
        add_small(ROW_B_DOWN, column_sum(out))
        middle_grad = out + norm_back(grad, small(ROW_LN2_GAIN), scaled, inverse)
        r.middle[span, :] = middle_grad
        branch = middle_grad.astype(bf16)
        r.branch[span, :] = branch
        add_small(ROW_B_OUT, column_sum(branch.astype(f32)))
        clock.work(1.0)

    piece = block // 3

    def store_rows(t, j, value):
        for i in range(TILE // piece):
            unit = j * (TILE // piece) + i
            m, place = unit // 3, t * block + (unit % 3) * piece
            chunk, row = tiles + place // TILE, place % TILE
            clock.ensure(wide_flows[chunk - 2], 2)
            r.work_wide[chunk % 2, m // 2, m % 2, row : row + piece, :] = value[
                i * piece : (i + 1) * piece
            ].astype(bf16)

    for j in range(tiles):
        cols = slice(j * TILE, (j + 1) * TILE)
        r.gattended[:, cols] = nt_dot(r.branch[...], r.wout[cols, :]).astype(bf16)
        store_rows(0, j, tn_dot(r.attended[:, cols], r.branch[...]))
        clock.work(1.5)

    def attend_back_pair(step):
        span, cols = place_of(step)
        q, k, v = r.qkv[0, span, cols], r.qkv[1, span, cols], r.qkv[2, span, cols]
        ga = r.gattended[span, cols]
        parts = []
        for h in range(2):
            mine = (lane >= HD) if h else (lane < HD)
            soft = r.soft_slots[step % 4, h]
            soft_wide = soft.astype(f32)
            prob = nt_dot(jnp.where(mine, ga, jnp.zeros_like(ga)), v)
            delta = jnp.sum(soft_wide * prob, axis=1, keepdims=True)
            score_grad = (soft_wide * (prob - delta)).astype(bf16)
            parts.append((nn_dot(score_grad, k), tn_dot(score_grad, q), tn_dot(soft, ga)))
        one, two = parts
        gq = jnp.where(lane < HD, one[0], two[0]) * (1.0 / math.sqrt(HD))
        gk, gv = jnp.where(lane < HD, one[1], two[1]), jnp.where(lane < HD, one[2], two[2])
        return gq.astype(bf16), gk.astype(bf16), gv.astype(bf16)

    def attend_back(turn, carry):
        two = (2 * turn, 2 * turn + 1)

        @pl.when(2 * turn + 2 < steps_count)
        def _():
            for step in two:
                soft_copy(step + 2, False).start()

        for step in two:
            soft_copy(step, False).wait()
        for step, grads in zip(two, [attend_back_pair(step) for step in two]):
            span, cols = place_of(step)
            for t in range(3):
                r.qkv[t, span, cols] = grads[t]
        return carry

    soft_copy(1, False).start()
    soft_copy(0, False).start()
    for g in range(groups):
        lax.fori_loop(g * count, (g + 1) * count, attend_back, 0)
        clock.work(6.0)

    for t, row in ((0, ROW_BQ), (2, ROW_BV)):
        add_small(row, column_sum(r.qkv[t].astype(f32)))

    r.back[...] = jnp.zeros_like(r.back)
    for t in range(3):

        def project_back(j, carry, t=t):
            cols = tile_at(j)
            r.back[...] += nn_dot(r.qkv[t, :, cols], r.wqkv[t, cols, :])
            return carry

        lax.fori_loop(0, tiles, project_back, 0)
        clock.work(1.5)

    tokens = []
    for i in range(images):
        span = span_at(i)
        scaled, inverse = norm_stats(r.start[span, :])
        grad = r.back[span, :]
        add_small(ROW_LN1_GAIN, column_sum(grad * scaled))
        add_small(ROW_LN1_BIAS, column_sum(grad))
        begin = r.middle[span, :] + norm_back(grad, small(ROW_LN1_GAIN), scaled, inverse)
        add_small(ROW_CLS, begin[0:1, :])
        for k in range(r.meta.shape[1]):
            add_small(ROW_META + k, r.meta[mp * images + i, k] * begin[1:2, :])
        tokens.append(begin.astype(bf16))
    clock.ensure(encoded_flow, 1)
    encoded_own.wait()
    for copy in out_copies:
        left(copy)
    for m in range(blocks):
        r.token_send[m, 0:rows] = packed(tokens, m, block)
    token_copies = []

    def token_begin():
        for peer, m in others:
            token_copies.append(push(r.token_send.at[m, 0:rows], r.token_recv.at[mp], peer))
        r.token_recv[mp] = r.token_send[mp, 0:rows]

    def token_end():
        for copy in token_copies:
            copy.wait_recv()

    token_flow = clock.add([(token_begin, LINK_X, 0.42 / RATE), (token_end, None, 0.0)])
    clock.work(2.0)

    def all_sum(levels, out):
        state = Bag()

        def step(level):
            if level:
                state.copy.wait_recv()
                levels[level] = levels[level] + levels[level - 1]
            if level < len(peers):
                state.copy = push(levels.at[level], levels.at[level + 1], peers[level])
            else:
                out(levels[level])

        links = [LINK_CORE, LINK_X, LINK_Y] + [LINK_Z] * (dp_bits - 1) + [None]
        return [(lambda n=n: step(n), link, 1.5) for n, link in enumerate(links)]

    def store_small(value):
        narrow = jnp.zeros(r.gnarrow.shape, f32)
        bias = jnp.zeros(r.gbias.shape, f32)
        for m in range(blocks):
            narrow += jnp.where(mp == m, value[:, m * block : (m + 1) * block], 0.0)
            bias += jnp.where(mp == m, value[ROW_B_UP + m : ROW_B_UP + m + 1, :], 0.0)
        r.gnarrow[...] = narrow
        r.gbias[...] = bias

    def wave_sum():
        copies = []

        def over_mp():
            for peer, _ in others:
                copies.append(push(r.wave_parts.at[mp], r.wave_parts.at[mp], peer))

        def over_dp():
            for copy in copies:
                copy.wait_recv()
            copies.clear()
            r.wave_chips[dp] = sum(r.wave_parts[m] for m in range(blocks))
            for peer in bit_peer + mixed:
                copies.append(push(r.wave_chips.at[dp], r.wave_chips.at[dp], peer))

        def end():
            for copy in copies:
                copy.wait_recv()
            r.gwave[...] = sum(r.wave_chips[d] for d in range(1 << dp_bits))

        return [(over_mp, LINK_SMALL, 1.0), (over_dp, LINK_SMALL, 3.0), (end, None, 0.0)]

    clock.add(all_sum(r.small_sums, store_small))
    def pixel_gradient():
        pixel_back = [nt_dot(tokens[i], r.patch[i]).astype(bf16) for i in range(images)]
        for m in range(blocks):
            r.pixel_send[m] = packed(pixel_back, m, depth // blocks)

        def pixel_begin():
            for peer, m in others:
                out_copies.append(push(r.pixel_send.at[m], r.pixel_grad.at[mp], peer))

        clock.add([(pixel_begin, LINK_X, 0.28 / RATE)], at=clock.now)
        pixel_own = carry_local(r.pixel_send.at[mp], r.pixel_grad.at[mp])
        clock.work(1.5)
        return pixel_own

    def chunks_ready(count):
        while len(wide_flows) < tiles + count:
            wide_flow(len(wide_flows))

    def weight_rows(t, source):
        for j in range(tiles):
            cols = slice(j * TILE, (j + 1) * TILE)
            store_rows(t, j, tn_dot(r.qkv[source, :, cols], r.normed_one[...]))
            clock.work(0.8)
        chunks_ready((t + 1) * block // TILE)

    if inside:
        def sensor_sums():
            r.total[...] = jnp.zeros_like(r.total)
            r.back[...] = jnp.zeros_like(r.back)
            lane_block = lax.broadcasted_iota(jnp.int32, (1, width), 1) // block
            for m in range(blocks):
                for i in range(images):
                    c = m * images + i
                    part = r.token_recv[m, :, i * block : (i + 1) * block]
                    part = tn_dot(r.chosen[c], jnp.concatenate([part] * blocks, axis=1))
                    tag = r.tags[c]
                    r.total[0:depth, :] += jnp.where(lane_block == tag, part, 0.0)
                    r.back[0:depth, :] += jnp.where(lane_block + blocks == tag, part, 0.0)
                    clock.work(0.7)

            for flow in up_flows:
                clock.ensure(flow, 2)

            def slot_of(d):
                return tuple((d >> b) % 2 for b in KERNEL_ORDER)

            for s in range(sensors):
                store = r.total if s < blocks else r.back
                part = store[0:depth, s % blocks * block : (s % blocks + 1) * block]
                for d in range(slots):
                    strips = [
                        part[(b * slots + d) * pixels_each : (b * slots + d + 1) * pixels_each]
                        for b in range(bands)
                    ]
                    line = slice(s * piece_rows, (s + 1) * piece_rows)
                    r.work_up[(*slot_of(d), line, slice(0, block))] = jnp.concatenate(
                        strips, axis=0
                    ).astype(bf16)
            clock.work(1.0)

        cut = 3 * piece_rows

        def kernel_flow(half):
            here = Bag()
            order = KERNEL_ORDER
            lines = slice(cut, sensors * piece_rows) if half else slice(0, cut)

            def source(level):
                if level == 0:
                    return r.work_up.at[:, :, :, lines, :]
                return r[KERNEL + level - 1].at[(slice(None),) * (3 - level) + (lines,)]

            def step(level):
                if level:
                    target = source(level)
                    here.copy.wait_recv()
                    target[...] = target[...] + source(level - 1)[dp_bit[order[level - 1]]]
                if level < 3:
                    give = source(level).at[1 - dp_bit[order[level]]]
                    here.copy = push(give, source(level + 1), bit_peer[order[level]])
                    return
                state.shares.append(half)
                if len(state.shares) == 2:
                    kernel_end()

            steps = []
            for n, b in enumerate(order):
                cost = (0.69, 0.34, 0.17)[n] / 2 * (2 if b == 2 else 1) / RATE
                steps.append((lambda n=n: step(n), LINK_Z if b else LINK_Y, cost))
            return steps + [(lambda: step(3), None, 0.0)]

        def kernel_end():
            flat = r[KERNEL + dp_bits - 1][:, 0:block]
            r.share[...] = flat.astype(f32).reshape(r.share.shape)
            line = lax.broadcasted_iota(jnp.int32, (sensors * piece_rows, HYP), 0)
            wave = jnp.zeros((sensors * piece_rows, HYP), f32)
            for p in range(pixels_each):
                part = nn_dot(flat, r.w_kernel[p])
                wave = wave + jnp.where(line % pixels_each == p, part, 0.0)
            wave = jnp.sum(wave.reshape(sensors * bands, pixels_each, HYP), axis=1)
            r.wave_parts[mp] = wave
            clock.add(wave_sum())

        def sensor_stage():
            clock.ensure(token_flow, 2)
            sensor_sums()
            state.shares = []
            for half in range(2):
                clock.add(kernel_flow(half))

    else:

        def sensor_stage():
            clock.ensure(token_flow, 2)
            r.token_out[...] = r.token_recv[...]
            r.chosen_out[...] = r.chosen[...]

    for n, (t, source) in enumerate(((1, 2), (2, 0), (3, 1))):
        if PIXELS_AT == n:
            pixel_own = pixel_gradient()
        if SENSORS_AT == n:
            sensor_stage()
        weight_rows(t, source)
    if PIXELS_AT == 3:
        pixel_own = pixel_gradient()
    if SENSORS_AT == 3:
        sensor_stage()

    clock.drain()
    pixel_own.wait()
    for copy in out_copies:
        copy.wait_recv()
    for copy in sent:
        copy.wait_send()


def layer(length, dp_bits, inside, scalars, arrays, distant):
    piece, pixels = arrays["piece"], distant["pixels"]
    rows = -(-length // ROW_TILE) * ROW_TILE
    chips, patches, depth = pixels.shape
    block, width = distant["wout_shard"].shape
    blocks = width // block
    images = chips // blocks
    total = images * rows
    steps = images * width // LANES
    tiles = width // TILE
    halves = min(3, dp_bits)

    def vmem(*size, kind=bf16):
        return pltpu.VMEM(size, kind)

    anywhere = pl.BlockSpec(memory_space=pl.ANY)
    near = pl.BlockSpec(memory_space=pltpu.VMEM)
    scalar = pl.BlockSpec(memory_space=pltpu.SMEM)
    names, operands, in_specs = list(scalars), list(scalars.values()), [scalar] * len(scalars)
    for group, spec in ((arrays, near), (distant, anywhere)):
        names += list(group)
        operands += list(group.values())
        in_specs += [spec] * len(group)

    outs = dict(
        encoded=((blocks, rows, images * block), bf16, anywhere),
        pixel_grad=((blocks, rows, images * depth // blocks), bf16, anywhere),
        gnarrow=((SMALL_ROWS, block), f32, near),
        gbias=((1, width), f32, near),
        fin_down=((tiles, TILE, width), bf16, anywhere),
        fin_inner=((tiles, TILE, width), bf16, anywhere),
        fin_up=((width, width), bf16, anywhere),
    )
    if inside:
        sensors, piece_rows, _ = piece.shape
        outs.update(share=(piece.shape, f32, near))
        bands = piece_rows // arrays["w_kernel"].shape[0]
        outs.update(gwave=((sensors * bands, HYP), f32, near))
    else:
        outs.update(token_out=((blocks, rows, images * block), bf16, near))
        outs.update(chosen_out=((chips, rows, depth), bf16, near))
    results = list(outs)
    outs.update(wup=((blocks, width, width), bf16, anywhere))
    outs.update(wdown=((blocks, width, width), bf16, anywhere))
    outs.update(soft=((steps, 2, rows, rows), bf16, anywhere))

    scratch = dict(
        index=vmem(rows, chips, kind=jnp.int32),
        narrow=vmem(SMALL_ROWS, block, kind=f32),
        bias_up=vmem(8, width, kind=f32),
        narrow_all=vmem(blocks, SMALL_ROWS, block, kind=f32),
        bias_all=vmem(blocks, 8, width, kind=f32),
        small=vmem(SMALL_ROWS, width, kind=f32),
        grad_recv=vmem(blocks, rows, images * block),
        grad=vmem(total, width),
        chosen=vmem(chips, rows, depth),
        start=vmem(total, width, kind=f32),
        middle=vmem(total, width, kind=f32),
        normed_one=vmem(total, width),
        normed_two=vmem(total, width),
        normed_flip=vmem(width, total),
        qkv=vmem(3, total, width),
        attended=vmem(total, width),
        total=vmem(total, width, kind=f32),
        back=vmem(total, width, kind=f32),
        wqkv=vmem(3, width, width),
        wout=vmem(width, width),
        up_slots=vmem(2, width, TILE),
        down_slots=vmem(2, TILE, width),
        soft_slots=vmem(4, 2, rows, rows),
        small_sums=vmem(3 + dp_bits, SMALL_ROWS, width, kind=f32),
        work_wide=vmem(2, 2, 2, TILE, width),
        work_up=vmem(2, 2, 2, width, TILE),
        token_recv=vmem(blocks, rows, images * block),
        pixel_send=vmem(blocks, rows, images * depth // blocks),
    )
    if inside:
        scratch.update(kernels_near=vmem(1 << (dp_bits - 1), *piece.shape))
        scratch.update(kernels_far=vmem(1 << (dp_bits - 1), *piece.shape))
        for n in range(dp_bits):
            lead = (2,) * (dp_bits - 1 - n)
            scratch[KERNEL + n] = vmem(*lead, sensors * piece_rows, TILE)
        scratch.update(patch_send=vmem(blocks, 2, depth // 2, images * block))
        scratch.update(patch_recv=vmem(blocks, 2, depth // 2, images * block))
        scratch.update(encoded_send=vmem(blocks, rows, images * block))
        scratch.update(patch=vmem(images, depth, width))
        scratch.update(wave_parts=vmem(blocks, sensors * bands, HYP, kind=f32))
        scratch.update(wave_chips=vmem(1 << dp_bits, sensors * bands, HYP, kind=f32))
    else:
        scratch.update(encoded_send=vmem(blocks, rows, images * block))
        scratch.update(token_send=vmem(blocks, rows, images * block))
    for base, amount, high, wide in ((WIDE, 2 * tiles, TILE, width), (UP, tiles, width, TILE)):
        for chunk in range(amount):
            along = order_of(dp_bits, chunk in (LATE_UP if base == UP else LATE_WIDE))
            scratch[base + 10 * chunk] = vmem(2, high, wide)
            lead, now, cut = (2,), high, 0
            for n, stage in enumerate(along):
                if stage == ACROSS:
                    lead = ()
                elif cut < halves:
                    now, cut = now // 2, cut + 1
                scratch[base + 10 * chunk + 1 + n] = vmem(*lead, now, wide)
    copies = 36 + 9 * (2 + dp_bits + halves) + 2 * (2 + dp_bits) + 32 + dp_bits
    dma = pltpu.SemaphoreType.DMA
    scratch.update(local_sems=dma((24,)))
    scratch.update(send_sems=dma((copies,)))
    scratch.update(recv_sems=dma((copies,)))
    scratch.update(slot_sems=dma((2, 2)))
    scratch.update(soft_sems=dma((2, 4)))
    scratch.update(pixel_sems=dma((2, patches // TILE)))

    names += [*outs, *scratch]

    def kernel(*refs):
        labels, refs = list(names), list(refs)
        twice = dict(branch="grad", gattended="normed_two")
        if inside:
            twice.update(token_send="encoded_send")
        for second, first in twice.items():
            labels.append(second)
            refs.append(refs[names.index(first)])
        layer_kernel(labels, length, dp_bits, inside, *refs)

    values = pl.pallas_call(
        kernel,
        in_specs=in_specs,
        out_specs=[spec for _, _, spec in outs.values()],
        out_shape=[jax.ShapeDtypeStruct(size, kind) for size, kind, _ in outs.values()],
        scratch_shapes=list(scratch.values()),
        compiler_params=pltpu.CompilerParams(
            vmem_limit_bytes=VMEM_LIMIT,
            fuse_transposed_lhs_in_matmul=True,
            collective_id=0,
            has_side_effects=True,
        ),
        name="layer",
    )(*operands)
    return Refs(outs, values)


def per_device(
    dp_bits,
    pixels,
    meta,
    tags,
    visible,
    wavelength,
    w_hyp,
    b_hyp,
    w_kernel,
    w_meta,
    cls_token,
    ln1_gain,
    ln1_bias,
    w_qkv,
    b_qv,
    w_out,
    b_out,
    ln2_gain,
    ln2_bias,
    w_up,
    b_up,
    w_down,
    b_down,
    cotangent,
):
    width = w_qkv.shape[0]
    block = cls_token.shape[0]
    blocks = width // block
    sensors, bands = wavelength.shape
    chips, patches, depth = pixels.shape
    pixels_each = w_kernel.shape[1]
    length = visible.shape[1] + 2
    rows = -(-length // ROW_TILE) * ROW_TILE
    images = chips // blocks
    inside = dp_bits == 3 and bands * pixels_each % ROW_TILE == 0

    wave_table = wave_code(wavelength)
    wave_pre = jnp.einsum("sbi,ij->sbj", wave_table, w_hyp, precision=highest) + b_hyp
    wave_hidden, wave_back = jax.vjp(jax.nn.gelu, wave_pre)
    wave_low = wave_hidden.astype(bf16)
    kernel = jnp.einsum("sbj,jpf->sbpf", wave_low, w_kernel, preferred_element_type=f32)
    kernel = kernel.astype(bf16)

    scalars = dict(meta=meta, tags=tags)
    arrays = dict(
        piece=kernel.reshape(sensors, bands * pixels_each, block),
        w_meta=w_meta,
        cls=cls_token[None],
        gain_one=ln1_gain[None],
        bias_one=ln1_bias[None],
        b_qv=b_qv,
        b_out=b_out[None],
        gain_two=ln2_gain[None],
        bias_two=ln2_bias[None],
        b_down=b_down[None],
        b_up=b_up,
        w_kernel=w_kernel.transpose(1, 2, 0),
        visible=visible,
        grad_rows=cotangent.transpose(1, 0, 2),
    )
    distant = dict(
        pixels=pixels,
        table=jnp.asarray(pos_table(patches, width)),
        wqkv_shard=w_qkv.transpose(1, 2, 0),
        wout_shard=w_out,
        wup_shard=w_up,
        wdown_shard=w_down,
    )
    if not inside:
        kernel = lax.all_gather(kernel, "dp", axis=2, tiled=True)
        kernel = kernel.reshape(sensors, depth, block)
        arrays.update(patch=lax.all_to_all(kernel[tags], "mp", 0, 2, tiled=True))
    got = layer(length, dp_bits, inside, scalars, arrays, distant)

    def unpack(value, size):
        value = value.reshape(blocks, rows, images, size).transpose(0, 2, 1, 3)
        return value.reshape(chips, rows, size)

    encoded = unpack(got.encoded, block)[:, :length]
    pixel_grad = unpack(got.pixel_grad, depth // blocks)[:, 2:length]
    wave_float = wave_low.astype(f32)
    if inside:
        share = got.share.reshape(sensors, bands, pixels_each, block)
        grad_wave = got.gwave.reshape(sensors, bands, HYP)
    else:
        select = (tags[:, None] == jnp.arange(sensors, dtype=jnp.int32)[None, :]).astype(f32)
        token_grad = unpack(got.token_out, block)
        chip_grad = jnp.einsum(
            "cvk,cvf->ckf", got.chosen_out, token_grad, preferred_element_type=f32
        )
        share = jnp.einsum("cs,ckf->skf", select, chip_grad, precision=highest)
        share = share.reshape(sensors, bands, depth // bands, block)
        share = lax.psum_scatter(share, "dp", scatter_dimension=2, tiled=True)
        grad_wave = lax.psum(
            jnp.einsum("sbpf,jpf->sbj", share, w_kernel.astype(f32), precision=highest),
            ("dp", "mp"),
        )
    grad_w_kernel = jnp.einsum("sbj,sbpf->jpf", wave_float, share, precision=highest)
    grad_pre = wave_back(grad_wave)[0]
    grad_w_hyp = jnp.einsum("sbi,sbj->ij", wave_table, grad_pre, precision=highest)
    grad_b_hyp = jnp.sum(grad_pre, axis=(0, 1))

    gdown = got.fin_down.reshape(width, width).astype(f32)
    gup = got.fin_up.astype(f32)
    inner = got.fin_inner.reshape(4, block, width)
    gout = inner[0].astype(f32)
    gqkv = jnp.stack([inner[2], inner[3], inner[1]]).transpose(2, 0, 1).astype(f32)
    gnarrow = got.gnarrow
    return (
        encoded,
        pixel_grad,
        grad_w_hyp,
        grad_b_hyp,
        grad_w_kernel,
        gnarrow[ROW_META : ROW_META + w_meta.shape[0]],
        gnarrow[ROW_CLS],
        gnarrow[ROW_LN1_GAIN],
        gnarrow[ROW_LN1_BIAS],
        gqkv,
        gnarrow[ROW_BQ : ROW_BV + 1],
        gout,
        gnarrow[ROW_B_OUT],
        gnarrow[ROW_LN2_GAIN],
        gnarrow[ROW_LN2_BIAS],
        gup,
        got.gbias[0],
        gdown,
        gnarrow[ROW_B_DOWN],
    )


def solution(mesh):
    dp_bits = mesh.shape["dp"].bit_length() - 1
    return jax.shard_map(
        functools.partial(per_device, dp_bits),
        mesh=mesh,
        in_specs=(
            P("dp", None, None),
            P("dp", None),
            P("dp"),
            P("dp", None),
            P(),
            P(),
            P(),
            P(None, "dp", "mp"),
            P(None, "mp"),
            P("mp"),
            P("mp"),
            P("mp"),
            P(None, None, "mp"),
            P(None, "mp"),
            P("mp", None),
            P("mp"),
            P("mp"),
            P("mp"),
            P(None, "mp"),
            P("mp"),
            P("mp", None),
            P("mp"),
            P("dp", None, "mp"),
        ),
        out_specs=(
            P("dp", None, "mp"),
            P("dp", None, "mp"),
            P(),
            P(),
            P(None, "dp", "mp"),
            P(None, "mp"),
            P("mp"),
            P("mp"),
            P("mp"),
            P(None, None, "mp"),
            P(None, "mp"),
            P("mp", None),
            P("mp"),
            P("mp"),
            P("mp"),
            P(None, "mp"),
            P("mp"),
            P("mp", None),
            P("mp"),
        ),
        check_vma=False,
    )
```

```python
import functools
import itertools
import math

import jax
import jax.numpy as jnp
import numpy as np
from jax import lax
from jax.experimental import pallas as pl
from jax.experimental.pallas import tpu as pltpu
from jax.sharding import PartitionSpec as P

HD = 64
HYP = 128
LANES = 128
TILE = 256
ROW_TILE = 16

norm_epsilon = 1e-05
highest = lax.Precision.HIGHEST
f32 = jnp.float32
bf16 = jnp.bfloat16
VMEM_LIMIT = 62 * 1024 * 1024
MESH = pl.DeviceIdType.MESH

ROW_META = 0
ROW_CLS = 8
ROW_LN1_GAIN = 9
ROW_LN1_BIAS = 10
ROW_BQ = 11
ROW_BV = 12
ROW_B_OUT = 13
ROW_LN2_GAIN = 14
ROW_LN2_BIAS = 15
ROW_B_DOWN = 16
ROW_B_UP = 17
SMALL_ROWS = 24


def wave_code(wavelength):
    half_width = HYP // 2
    ladder = jnp.arange(half_width, dtype=f32) * (math.log(100.0) / half_width)
    angle_grid = wavelength[..., None] * jnp.exp(ladder)
    return jnp.concatenate([jnp.sin(angle_grid), jnp.cos(angle_grid)], axis=-1)


def pos_table(patch_count, width):
    index = np.arange(patch_count, dtype=np.float64)[:, None]
    feature = np.arange(width)[None, :]
    angle = index * np.exp((feature // 2) * (-2.0 * math.log(10000.0) / width))
    table = np.where(feature % 2 == 0, np.sin(angle), np.cos(angle)).astype(np.float32)
    return table.astype(jnp.bfloat16)


def nn_dot(left, right):
    return lax.dot_general(left, right, (((1,), (0,)), ((), ())), preferred_element_type=f32)


def nt_dot(left, right):
    return lax.dot_general(left, right, (((1,), (1,)), ((), ())), preferred_element_type=f32)


def tn_dot(left, right):
    return lax.dot_general(left, right, (((0,), (0,)), ((), ())), preferred_element_type=f32)


def gelu_pair(u):
    c = math.sqrt(2.0 / math.pi)
    square = u * u
    t = jnp.tanh(c * u * (1.0 + 0.044715 * square))
    half = 0.5 * (1.0 + t)
    slope = half + 0.5 * u * (1.0 - t * t) * (c * (1.0 + 3.0 * 0.044715 * square))
    return u * half, slope


def norm_stats(x):
    width = x.shape[1]
    center = jnp.sum(x, axis=1, keepdims=True) * (1.0 / width)
    square = jnp.sum(x * x, axis=1, keepdims=True) * (1.0 / width)
    inverse = lax.rsqrt(square - center * center + norm_epsilon)
    return (x - center) * inverse, inverse


def hot_rows(index, count):
    lane = lax.broadcasted_iota(jnp.int32, (index.shape[0], count), 1)
    return jnp.where(index == lane, 1.0, 0.0).astype(bf16)


def norm_back(grad, gain, scaled, inverse):
    width = grad.shape[1]
    weighted = grad * gain
    first = jnp.sum(weighted, axis=1, keepdims=True) * (1.0 / width)
    second = jnp.sum(weighted * scaled, axis=1, keepdims=True) * (1.0 / width)
    return inverse * (weighted - first - scaled * second)


def column_sum(x):
    return jnp.sum(x, axis=0, keepdims=True)


class Flow:
    def __init__(self, clock, steps, ready):
        self.clock, self.steps, self.next, self.ready = clock, steps, 0, ready

    @property
    def open(self):
        return self.next < len(self.steps)

    def due(self):
        _, link, _ = self.steps[self.next]
        return max(self.ready, self.clock.busy.get(link, 0.0) - self.clock.slack)

    def go(self):
        action, link, cost = self.steps[self.next]
        clock = self.clock
        clock.now = max(clock.now, self.ready)
        action()
        self.next += 1
        clock.now += clock.start
        begin = max(clock.now, clock.busy.get(link, 0.0))
        if link is not None:
            clock.busy[link] = begin + cost
        self.ready = begin + cost + clock.latency


class Clock:
    latency, slack, start = 1.5, 6.0, 0.3

    def __init__(self):
        self.now, self.busy, self.flows = 0.0, {}, []

    def add(self, steps, at=None):
        flow = Flow(self, steps, self.now if at is None else at)
        self.flows.append(flow)
        if at is None:
            flow.go()
        return flow

    def ensure(self, flow, count):
        if not flow.next:
            flow.ready = min(flow.ready, self.now)
        while flow.next < count:
            flow.go()

    def work(self, cost):
        self.now += cost
        self.pump()

    def pump(self):
        while True:
            due = [f for f in self.flows if f.open and f.due() <= self.now]
            if not due:
                return
            min(due, key=Flow.due).go()

    def drain(self):
        while True:
            left = [f for f in self.flows if f.open]
            if not left:
                return
            flow = min(left, key=Flow.due)
            self.now = max(self.now, flow.due())
            flow.go()


class Refs:
    def __init__(self, names, refs):
        self.named = dict(zip(names, refs, strict=True))

    def __getattr__(self, name):
        return self.named[name]

    def __getitem__(self, number):
        return self.named[number]


KERNEL, WIDE, UP = 0, 100, 200
ACROSS = -1


def order_of(dp_bits, late):
    if late:
        return [1, ACROSS, 0, *range(2, dp_bits)]
    return [ACROSS, *range(dp_bits)]


class Bag:
    pass


RATE = 0.05
PAIR_RATE = 0.3
LATE_WIDE, LATE_UP = (), ()
UP_BITS, DOWN_BITS = (0, 1), (0,)
HOLD = 18.0
UP_AT = 8.0
SENSORS_AT = 2
PIXELS_AT = 3
KERNEL_ORDER = (1, 0, 2)
HALVES = 2
LINK_CORE, LINK_X, LINK_Y, LINK_Z, LINK_SMALL = range(5)


def layer_kernel(names, length, dp_bits, inside, *refs):
    r = Refs(names, refs)
    halves = min(HALVES, dp_bits)
    rows, width = r.index.shape[0], r.start.shape[1]
    chips, patches, depth = r.pixels.shape
    blocks = r.wup.shape[0]
    images = chips // blocks
    block = width // blocks
    tiles = width // TILE
    pairs = width // LANES
    steps_count = images * pairs

    mp, dp = lax.axis_index("mp"), lax.axis_index("dp")
    core_bit, x_bit = mp % 2, mp // 2
    core_mp, x_mp = mp + 1 - 2 * core_bit, mp + 2 - 4 * x_bit
    far_mp = blocks - 1 - mp
    dp_bit = [(dp // (1 << b)) % 2 for b in range(dp_bits)]

    def flip(*bits):
        value = dp
        for b in bits:
            value = value + (1 - 2 * dp_bit[b]) * (1 << b)
        return value

    core, across_x, diagonal = {"mp": core_mp}, {"mp": x_mp}, {"mp": far_mp}
    bit_peer = [{"dp": flip(b)} for b in range(dp_bits)]
    peers = [core, across_x, *bit_peer]
    others = [(core, core_mp), (across_x, x_mp), (diagonal, far_mp)]
    greeted = peers + [diagonal]
    if inside:
        mixed = [{"dp": flip(*bits)} for bits in ((0, 1), (0, 2), (1, 2), (0, 1, 2))]
        greeted += mixed

    barrier = pltpu.get_barrier_semaphore()
    for peer in greeted:
        pl.semaphore_signal(barrier, inc=1, device_id=peer, device_id_type=MESH)
    pl.semaphore_wait(barrier, len(greeted))

    sent, numbers, local_numbers = [], itertools.count(), itertools.count()

    def push(source, target, peer):
        number = next(numbers)
        copy = pltpu.make_async_remote_copy(
            src_ref=source,
            dst_ref=target,
            send_sem=r.send_sems.at[number],
            recv_sem=r.recv_sems.at[number],
            device_id=peer,
            device_id_type=MESH,
        )
        copy.start()
        sent.append(copy)
        return copy

    def left(copy):
        copy.wait_send()
        sent[:] = [c for c in sent if c is not copy]

    def carry_local(source, target):
        copy = pltpu.make_async_copy(source, target, r.local_sems.at[next(local_numbers)])
        copy.start()
        return copy

    def mul16(value):
        return pl.multiple_of(value, ROW_TILE)

    def tile_at(j):
        return pl.ds(pl.multiple_of(j * TILE, TILE), TILE)

    def span_at(i):
        return pl.ds(i * rows, rows)

    def small(row):
        return r.small[row : row + 1, :]

    clock = Clock()

    if inside:
        place = dp // 2
        r.kernels_near[place] = r.piece[...]
        sideways = bit_peer[0]
        direct = push(r.piece, r.kernels_far.at[place], sideways)
        along = []
        for peer, bits in ((bit_peer[1], (1,)), (mixed[2], (1, 2)), (bit_peer[2], (2,))):
            along.append((push(r.piece, r.kernels_near.at[place], peer), flip(*bits) // 2))
        passed = []

        def pass_on(n):
            copy, index = along[n]
            copy.wait_recv()
            passed.append(push(r.kernels_near.at[index], r.kernels_far.at[index], sideways))

        amount = 0.172
        gather_steps = [
            (lambda: None, LINK_Z, amount / RATE),
            (lambda: pass_on(0), LINK_Y, amount * 1.5 / RATE),
            (lambda: pass_on(1), LINK_Y, amount * 1.5 / RATE),
        ]

        def halfway():
            pass_on(2)

        gather_steps.append((halfway, LINK_Y, amount / RATE))

        def gather_end():
            direct.wait_recv()
            for copy in passed:
                copy.wait_recv()

        gather_steps.append((gather_end, None, 0.0))
        gather_flow = clock.add(gather_steps)

    r.narrow[...] = jnp.zeros_like(r.narrow)
    row = 0
    for part in (r.w_meta, r.cls, r.gain_one, r.bias_one, r.b_qv, r.b_out, r.gain_two, r.bias_two):
        r.narrow[row : row + part.shape[0], :] = part[...]
        row += part.shape[0]
    r.narrow[row : row + 1, :] = r.b_down[...]
    r.bias_up[...] = jnp.broadcast_to(r.b_up[...].reshape(1, width), r.bias_up.shape)
    narrow_copies = []
    for peer, _ in others:
        narrow_copies.append(push(r.narrow, r.narrow_all.at[mp], peer))
        narrow_copies.append(push(r.bias_up, r.bias_all.at[mp], peer))
    r.narrow_all[mp] = r.narrow[...]
    r.bias_all[mp] = r.bias_up[...]

    def weight_flow(shard, full, inner, bits, at=None):
        parts = 1 << len(bits)
        high = block if inner else shard.shape[0]
        lead = (slice(None),) if len(shard.shape) == 3 else ()

        def view(m, first, count):
            place = pl.ds(mul16(first * (high // parts)), count * (high // parts))
            if inner:
                place = pl.ds(
                    mul16(m * block + first * (high // parts)), count * (high // parts)
                )
                return full.at[(*lead, place)]
            return full.at[m, place, :]

        state = Bag()
        first = 0
        for n, b in enumerate(bits):
            first = first + dp_bit[b] * (1 << n)
        state.hands = []

        def begin():
            own = shard.at[(*lead, pl.ds(mul16(first * (high // parts)), high // parts))]
            state.local = carry_local(shard, view(mp, 0, parts))
            state.copy = push(own, view(mp, first, 1), across_x)

        state.hands.append(push(shard, view(mp, 0, parts), core))

        def held(n):
            start = 0
            for k in range(n, len(bits)):
                start = start + dp_bit[bits[k]] * (1 << k)
            return start, 1 << n

        def came(n):
            start, count = held(n)
            if n:
                count //= 2
                start = start + (1 - dp_bit[bits[n - 1]]) * count
            return start, count

        def relay(n):
            state.copy.wait_recv()
            if n < len(bits):
                piece = view(x_mp, *held(n))
                state.next = push(piece, piece, bit_peer[bits[n]])
            piece = view(x_mp, *came(n))
            state.hands.append(push(piece, piece, core))
            if n < len(bits):
                state.copy = state.next

        def end():
            state.local.wait()
            for copy in state.hands:
                copy.wait_recv()

        cost = math.prod(shard.shape) * 2 / parts / 1e6
        steps = [(begin, LINK_X, cost / RATE)]
        for n in range(len(bits)):
            link = LINK_Z if bits[n] else LINK_Y
            steps.append((lambda n=n: relay(n), link, cost * (1 << n) / RATE))
        steps.append((lambda: relay(len(bits)), LINK_CORE, cost * parts / 2 / PAIR_RATE))
        steps.append((end, None, 0.0))
        return clock.add(steps, at=at)

    qkv_flow = weight_flow(r.wqkv_shard, r.wqkv, True, (0,))
    out_flow = weight_flow(r.wout_shard, r.wout, True, (0,))
    up_weight = weight_flow(r.wup_shard, r.wup, False, UP_BITS, at=UP_AT)
    down_weight = weight_flow(r.wdown_shard, r.wdown, False, DOWN_BITS, at=1000.0)
    qkv_flow.ready = out_flow.ready = HOLD

    state = Bag()

    def grad_begin():
        state.grad = [push(r.encoded_send.at[m], r.grad_recv.at[mp], p) for p, m in others]
        r.grad_recv[mp] = r.encoded_send[mp]

    def grad_end():
        for copy in state.grad:
            copy.wait_recv()
        for i in range(images):
            r.grad[span_at(i), :] = jnp.concatenate(
                [r.grad_recv[m][:, i * block : (i + 1) * block] for m in range(blocks)], axis=1
            )

    def pack_grad():
        r.encoded_send[...] = jnp.zeros_like(r.encoded_send)
        for m in range(blocks):
            pair = [r.grad_rows[:, m * images + i, :] for i in range(images)]
            r.encoded_send[m, 0:length] = jnp.concatenate(pair, axis=1)

    turned = r.visible[...].astype(f32).T
    none = jnp.full((rows, chips), -1.0, f32)
    turned = jnp.concatenate([none[0:2], turned, none[length:rows]], axis=0)
    r.index[...] = turned.astype(jnp.int32)

    table_copies = []
    for k in range(patches // TILE):
        table_copies.append(
            carry_local(r.table.at[k * TILE : (k + 1) * TILE], r.work_wide.at[0, k // 2, k % 2])
        )

    def pixel_copies(c):
        lanes = slice((c % 2) * depth, (c % 2 + 1) * depth)
        return [
            pltpu.make_async_copy(
                r.pixels.at[c, k * TILE : (k + 1) * TILE],
                r.work_wide.at[1, k // 2, k % 2, :, lanes],
                r.pixel_sems.at[c % 2, k],
            )
            for k in range(patches // TILE)
        ]

    for copy in pixel_copies(0):
        copy.start()
    for c in range(chips):
        if c + 1 < chips:
            for copy in pixel_copies(c + 1):
                copy.start()
        for copy in pixel_copies(c):
            copy.wait()
        hot = hot_rows(r.index[:, c : c + 1], patches)
        lanes = slice((c % 2) * depth, (c % 2 + 1) * depth)
        value = 0.0
        for k in range(patches // TILE):
            value = value + nn_dot(
                hot[:, k * TILE : (k + 1) * TILE], r.work_wide[1, k // 2, k % 2, :, lanes]
            )
        r.chosen[c] = value.astype(bf16)
        clock.work(0.7)

    for copy in narrow_copies:
        copy.wait_recv()
    r.small[...] = jnp.concatenate([r.narrow_all[m] for m in range(blocks)], axis=1)
    for m in range(blocks):
        r.small[ROW_B_UP + m : ROW_B_UP + m + 1, :] = r.bias_all[m, 0:1, :]

    for copy in table_copies:
        copy.wait()
    chip_lane = lax.broadcasted_iota(jnp.int32, (rows, chips), 1)
    index_wide = r.index[...].astype(f32)
    for i in range(images):
        mine = jnp.where(chip_lane == mp * images + i, index_wide, 0.0)
        hot = hot_rows(jnp.sum(mine, axis=1, keepdims=True).astype(jnp.int32), patches)
        value = 0.0
        for k in range(patches // TILE):
            value = value + nn_dot(
                hot[:, k * TILE : (k + 1) * TILE], r.work_wide[0, k // 2, k % 2]
            )
        r.start[span_at(i), :] = value
        token = jnp.zeros((1, width), f32)
        for k in range(r.meta.shape[1]):
            token = token + r.meta[mp * images + i, k] * small(ROW_META + k)
        line = lax.broadcasted_iota(jnp.int32, (8, width), 0)
        r.start[pl.ds(i * rows, 8), :] += jnp.where(
            line == 0, small(ROW_CLS), jnp.where(line == 1, token, 0.0)
        )
        clock.work(1.0)

    pack_grad()
    clock.work(1.5)

    clock.ensure(up_weight, 1)
    if inside:
        sensors, piece_rows = r.piece.shape[0], r.piece.shape[1]
        slots = 1 << dp_bits
        pixels_each = r.w_kernel.shape[0]
        bands = piece_rows // pixels_each
        patch_copies = []

        def patch_half(kernels, side):
            for m in range(blocks):
                pair = []
                for i in range(images):
                    tag = r.tags[m * images + i]
                    parts = [kernels[k, tag] for k in range(slots // 2)]
                    pair.append(jnp.concatenate(parts, axis=0))
                r.patch_send[m, side] = jnp.concatenate(pair, axis=1)
            for peer, m in others:
                spot = r.patch_recv.at[mp, side]
                patch_copies.append(push(r.patch_send.at[m, side], spot, peer))
            r.patch_recv[mp, side] = r.patch_send[mp, side]

        def patch_far():
            clock.ensure(gather_flow, 5)
            patch_half(r.kernels_far, 1 - dp_bit[0])

        def patch_end():
            for copy in patch_copies:
                copy.wait_recv()

        clock.ensure(gather_flow, 4)
        patch_flow = clock.add(
            [
                (lambda: patch_half(r.kernels_near, dp_bit[0]), LINK_X, 0.295 / RATE),
                (patch_far, LINK_X, 0.295 / RATE),
                (patch_end, None, 0.0),
            ]
        )
        clock.now += 0.7
        clock.ensure(patch_flow, 2)
        clock.now += 0.7
        clock.ensure(qkv_flow, 2)
        clock.ensure(out_flow, 2)
        clock.ensure(patch_flow, 3)
        for i in range(images):
            side_rows = []
            for side in range(2):
                part = [
                    r.patch_recv[m, side, :, i * block : (i + 1) * block] for m in range(blocks)
                ]
                side_rows.append(jnp.concatenate(part, axis=1).astype(f32))
            strips = []
            for b in range(bands):
                for d in range(slots):
                    first = (d // 2 * bands + b) * pixels_each
                    strips.append(side_rows[d % 2][first : first + pixels_each])
            r.patch[i] = jnp.concatenate(strips, axis=0).astype(bf16)
    clock.ensure(down_weight, 1)
    grad_flow = clock.add(
        [(grad_begin, LINK_X, 0.42 / RATE), (grad_end, None, 0.0)], at=clock.now + 8.0
    )

    for i in range(images):
        value = r.start[span_at(i), :] + nn_dot(r.chosen[mp * images + i], r.patch[i])
        r.start[span_at(i), :] = value
        scaled, _ = norm_stats(value)
        r.normed_one[span_at(i), :] = (
            scaled * small(ROW_LN1_GAIN) + small(ROW_LN1_BIAS)
        ).astype(bf16)
        clock.work(1.0)

    clock.ensure(qkv_flow, 4)
    for t in range(3):

        def project(j, carry, t=t):
            cols = tile_at(j)
            value = nt_dot(r.normed_one[...], r.wqkv[t, cols, :])
            if t == 0:
                value = value + r.small[ROW_BQ : ROW_BQ + 1, cols]
                value = value.astype(bf16).astype(f32) * (1.0 / math.sqrt(HD))
            if t == 2:
                value = value + r.small[ROW_BV : ROW_BV + 1, cols]
            r.qkv[t, :, cols] = value.astype(bf16)
            return carry

        lax.fori_loop(0, tiles, project, 0)
        clock.work(1.5)

    lane = lax.broadcasted_iota(jnp.int32, (1, LANES), 1)
    key_lane = lax.broadcasted_iota(jnp.int32, (1, rows), 1)

    def soft_copy(step, out):
        slot = step % 2
        near, distant = r.soft_slots.at[slot], r.soft.at[step]
        if out:
            return pltpu.make_async_copy(near, distant, r.soft_sems.at[0, slot])
        return pltpu.make_async_copy(distant, near, r.soft_sems.at[1, slot])

    def attend(step, carry):
        image = step // pairs
        pair = step % pairs
        span = pl.ds(mul16(image * rows), rows)
        cols = pl.ds(pl.multiple_of(pair * LANES, LANES), LANES)
        q, k, v = r.qkv[0, span, cols], r.qkv[1, span, cols], r.qkv[2, span, cols]

        @pl.when(step >= 2)
        def _():
            soft_copy(step - 2, True).wait()

        parts = []
        for h in range(2):
            mine = (lane >= HD) if h else (lane < HD)
            scores = nt_dot(jnp.where(mine, q, jnp.zeros_like(q)), k)
            scores = jnp.where(key_lane < length, scores, -1e30)
            top = jnp.max(scores, axis=1, keepdims=True)
            power = jnp.exp(scores - top)
            soft = power * (1.0 / jnp.sum(power, axis=1, keepdims=True))
            soft = soft.astype(bf16)
            r.soft_slots[step % 2, h] = soft
            parts.append(nn_dot(soft, v))
        soft_copy(step, True).start()
        r.attended[span, cols] = jnp.where(lane < HD, parts[0], parts[1]).astype(bf16)
        return carry

    groups = 6
    count = steps_count // groups
    for g in range(groups):
        lax.fori_loop(g * count, (g + 1) * count, attend, 0)
        clock.work(2.0)
    for step in (steps_count - 2, steps_count - 1):
        soft_copy(step, True).wait()
    clock.ensure(out_flow, 4)

    def project_out(j, carry):
        cols = tile_at(j)
        r.middle[:, cols] = (
            r.start[:, cols]
            + nn_dot(r.attended[...], r.wout[:, cols])
            + r.small[ROW_B_OUT : ROW_B_OUT + 1, cols]
        )
        return carry

    lax.fori_loop(0, tiles, project_out, 0)
    clock.work(1.5)

    for i in range(images):
        scaled, _ = norm_stats(r.middle[span_at(i), :])
        r.normed_two[span_at(i), :] = (
            scaled * small(ROW_LN2_GAIN) + small(ROW_LN2_BIAS)
        ).astype(bf16)
        r.total[span_at(i), :] = r.middle[span_at(i), :] + small(ROW_B_DOWN)
    r.normed_flip[...] = r.normed_two[...].T
    r.back[...] = jnp.zeros_like(r.back)
    r.small_sums[0] = jnp.zeros_like(r.small_sums[0])
    clock.work(2.0)
    clock.ensure(grad_flow, 2)
    clock.ensure(up_weight, 3 + len(UP_BITS))
    clock.ensure(down_weight, 3 + len(DOWN_BITS))

    def reduction(work, recv, order, fin):
        state = Bag()
        size = work.shape[2]
        amount = size * work.shape[3] * 2 / 1e6
        split = [b for b in order if b != ACROSS][:halves]

        def half(high, bit):
            return pl.ds(mul16(bit * (high // 2)), high // 2)

        def views(level, stage):
            ref = recv[level]
            if stage == ACROSS:
                return ref.at[x_bit], ref.at[1 - x_bit], across_x
            bit, peer = dp_bit[stage], bit_peer[stage]
            if stage not in split:
                return ref, ref, peer
            lead = (slice(None),) * (len(ref.shape) - 2)
            high = ref.shape[-2]
            return ref.at[(*lead, half(high, bit))], ref.at[(*lead, half(high, 1 - bit))], peer

        def begin():
            state.copy = push(work.at[:, 1 - core_bit], recv[0], core)
            state.work = state.copy

        def step(n):
            state.copy.wait_recv()
            if n == 0:
                recv[0][...] = recv[0][...] + work[:, core_bit]
                left(state.work)
            else:
                keep, _, _ = views(n - 1, order[n - 1])
                recv[n][...] = recv[n][...] + keep[...]
            if n < len(order):
                _, give, peer = views(n, order[n])
                state.copy = push(give, recv[n + 1], peer)

        def corner(count):
            offset = 0
            for n in range(count):
                offset = offset + dp_bit[split[n]] * (size >> (n + 1))
            return pl.ds(mul16(offset), size >> count)

        def last():
            step(len(order))
            source, spot = recv[len(order)], fin(corner(halves))
            state.local = carry_local(source, spot)
            state.copy = push(source, spot, bit_peer[split[halves - 1]])

        def spread(count):
            state.copy.wait_recv()
            if count == halves - 1:
                state.local.wait()
            spot = fin(corner(count))
            state.copy = push(spot, spot, bit_peer[split[count - 1]])

        def end():
            state.copy.wait_recv()

        def link_of(stage):
            return LINK_X if stage == ACROSS else LINK_Z if stage else LINK_Y

        def hops(stage):
            return 2 if stage == 2 else 1

        steps = [(begin, LINK_CORE, amount * 2 / PAIR_RATE)]
        now = amount * 2
        for n, stage in enumerate(order):
            if stage == ACROSS or stage in split:
                now /= 2
            cost = now * hops(stage) / RATE
            steps.append((lambda n=n: step(n), link_of(stage), cost))
        for count in range(halves, 0, -1):
            stage = split[count - 1]
            action = last if count == halves else lambda c=count: spread(c)
            steps.append((action, link_of(stage), (amount / 2**count) * hops(stage) / RATE))
        steps.append((end, None, 0.0))
        return steps

    wide_flows, up_flows = [], []

    def levels_of(base):
        return [r[base + n] for n in range(2 + dp_bits)]

    def wide_flow(chunk):
        work, recv = r.work_wide.at[chunk % 2], levels_of(WIDE + 10 * chunk)
        order = order_of(dp_bits, chunk in LATE_WIDE)
        fin = r.fin_down if chunk < tiles else r.fin_inner
        wide_flows.append(
            clock.add(reduction(work, recv, order, lambda s: fin.at[chunk % tiles, s]))
        )

    def up_flow(chunk):
        cols = slice(chunk * TILE, (chunk + 1) * TILE)
        work, recv = r.work_up.at[chunk % 2], levels_of(UP + 10 * chunk)
        order = order_of(dp_bits, chunk in LATE_UP)
        up_flows.append(clock.add(reduction(work, recv, order, lambda s: r.fin_up.at[s, cols])))

    order = blocks * tiles

    def fetch(j):
        m, slot = j % blocks, j % 2
        inner = tile_at(j // blocks)
        return (
            pltpu.make_async_copy(
                r.wup.at[m, :, inner], r.up_slots.at[slot], r.slot_sems.at[0, slot]
            ),
            pltpu.make_async_copy(
                r.wdown.at[m, inner, :], r.down_slots.at[slot], r.slot_sems.at[1, slot]
            ),
        )

    for copy in fetch(0):
        copy.start()

    def feed(j, carry):
        m, slot, part = j % blocks, j % 2, (j // blocks) % 2
        inner = tile_at(j // blocks)

        @pl.when(j + 1 < order)
        def _():
            for copy in fetch(j + 1):
                copy.start()

        for copy in fetch(j):
            copy.wait()
        up, down = r.up_slots[slot], r.down_slots[slot]
        hidden = nn_dot(r.normed_two[...], up)
        hidden = hidden + r.small[pl.ds(ROW_B_UP + m, 1), inner]
        value, slope = gelu_pair(hidden)
        value = value.astype(bf16)
        r.total[...] += nn_dot(value, down)
        grad = r.grad[...]
        r.work_wide[part, m // 2, m % 2] = tn_dot(value, grad).astype(bf16)
        hidden_grad = (nt_dot(grad, down) * slope).astype(bf16)
        r.small_sums[0, pl.ds(ROW_B_UP + m, 1), inner] = column_sum(hidden_grad.astype(f32))
        r.work_up[part, m // 2, m % 2] = nn_dot(r.normed_flip[...], hidden_grad).astype(bf16)
        r.back[...] += nt_dot(hidden_grad, up)
        return carry

    for c in range(tiles):
        if c >= 2:
            clock.ensure(wide_flows[c - 2], 2)
            clock.ensure(up_flows[c - 2], 2)
        for half in range(2):
            begin = c * blocks + half * blocks // 2
            lax.fori_loop(begin, begin + blocks // 2, feed, 0)
            clock.work(5.0)
        wide_flow(c)
        up_flow(c)

    def packed(value, m, size):
        lanes = slice(m * size, (m + 1) * size)
        return jnp.concatenate([value[i][:, lanes] for i in range(images)], axis=1)

    for copy in state.grad:
        left(copy)
    total = [r.total[span_at(i), :].astype(bf16) for i in range(images)]
    for m in range(blocks):
        r.encoded_send[m, 0:rows] = packed(total, m, block)
    out_copies = []

    def encoded_begin():
        for peer, m in others:
            out_copies.append(push(r.encoded_send.at[m, 0:rows], r.encoded.at[mp], peer))

    encoded_flow = clock.add([(encoded_begin, LINK_X, 0.42 / RATE)], at=clock.now)
    encoded_own = carry_local(r.encoded_send.at[mp, 0:rows], r.encoded.at[mp])
    clock.work(1.0)

    def add_small(row, value):
        r.small_sums[0, row : row + 1, :] += value

    for i in range(images):
        span = span_at(i)
        scaled, inverse = norm_stats(r.middle[span, :])
        grad = r.back[span, :]
        out = r.grad[span, :].astype(f32)
        add_small(ROW_LN2_GAIN, column_sum(grad * scaled))
        add_small(ROW_LN2_BIAS, column_sum(grad))
        add_small(ROW_B_DOWN, column_sum(out))
        middle_grad = out + norm_back(grad, small(ROW_LN2_GAIN), scaled, inverse)
        r.middle[span, :] = middle_grad
        branch = middle_grad.astype(bf16)
        r.branch[span, :] = branch
        add_small(ROW_B_OUT, column_sum(branch.astype(f32)))
        clock.work(1.0)

    piece = block // 3

    def store_rows(t, j, value):
        for i in range(TILE // piece):
            unit = j * (TILE // piece) + i
            m, place = unit // 3, t * block + (unit % 3) * piece
            chunk, row = tiles + place // TILE, place % TILE
            clock.ensure(wide_flows[chunk - 2], 2)
            r.work_wide[chunk % 2, m // 2, m % 2, row : row + piece, :] = value[
                i * piece : (i + 1) * piece
            ].astype(bf16)

    for j in range(tiles):
        cols = slice(j * TILE, (j + 1) * TILE)
        r.gattended[:, cols] = nt_dot(r.branch[...], r.wout[cols, :]).astype(bf16)
        store_rows(0, j, tn_dot(r.attended[:, cols], r.branch[...]))
        clock.work(1.5)

    def attend_back(step, carry):
        image = step // pairs
        pair = step % pairs
        span = pl.ds(mul16(image * rows), rows)
        cols = pl.ds(pl.multiple_of(pair * LANES, LANES), LANES)

        @pl.when(step + 1 < steps_count)
        def _():
            soft_copy(step + 1, False).start()

        soft_copy(step, False).wait()
        q, k, v = r.qkv[0, span, cols], r.qkv[1, span, cols], r.qkv[2, span, cols]
        ga = r.gattended[span, cols]
        parts = []
        for h in range(2):
            mine = (lane >= HD) if h else (lane < HD)
            soft = r.soft_slots[step % 2, h]
            soft_wide = soft.astype(f32)
            prob = nt_dot(jnp.where(mine, ga, jnp.zeros_like(ga)), v)
            delta = jnp.sum(soft_wide * prob, axis=1, keepdims=True)
            score_grad = (soft_wide * (prob - delta)).astype(bf16)
            parts.append((nn_dot(score_grad, k), tn_dot(score_grad, q), tn_dot(soft, ga)))
        one, two = parts
        gq = jnp.where(lane < HD, one[0], two[0]) * (1.0 / math.sqrt(HD))
        r.qkv[0, span, cols] = gq.astype(bf16)
        r.qkv[1, span, cols] = jnp.where(lane < HD, one[1], two[1]).astype(bf16)
        r.qkv[2, span, cols] = jnp.where(lane < HD, one[2], two[2]).astype(bf16)
        return carry

    soft_copy(0, False).start()
    for g in range(groups):
        lax.fori_loop(g * count, (g + 1) * count, attend_back, 0)
        clock.work(3.0)

    for t, row in ((0, ROW_BQ), (2, ROW_BV)):
        add_small(row, column_sum(r.qkv[t].astype(f32)))

    r.back[...] = jnp.zeros_like(r.back)
    for t in range(3):

        def project_back(j, carry, t=t):
            cols = tile_at(j)
            r.back[...] += nn_dot(r.qkv[t, :, cols], r.wqkv[t, cols, :])
            return carry

        lax.fori_loop(0, tiles, project_back, 0)
        clock.work(1.5)

    tokens = []
    for i in range(images):
        span = span_at(i)
        scaled, inverse = norm_stats(r.start[span, :])
        grad = r.back[span, :]
        add_small(ROW_LN1_GAIN, column_sum(grad * scaled))
        add_small(ROW_LN1_BIAS, column_sum(grad))
        begin = r.middle[span, :] + norm_back(grad, small(ROW_LN1_GAIN), scaled, inverse)
        add_small(ROW_CLS, begin[0:1, :])
        for k in range(r.meta.shape[1]):
            add_small(ROW_META + k, r.meta[mp * images + i, k] * begin[1:2, :])
        tokens.append(begin.astype(bf16))
    clock.ensure(encoded_flow, 1)
    encoded_own.wait()
    for copy in out_copies:
        left(copy)
    for m in range(blocks):
        r.token_send[m, 0:rows] = packed(tokens, m, block)
    token_copies = []

    def token_begin():
        for peer, m in others:
            token_copies.append(push(r.token_send.at[m, 0:rows], r.token_recv.at[mp], peer))
        r.token_recv[mp] = r.token_send[mp, 0:rows]

    def token_end():
        for copy in token_copies:
            copy.wait_recv()

    token_flow = clock.add([(token_begin, LINK_X, 0.42 / RATE), (token_end, None, 0.0)])
    clock.work(2.0)

    def all_sum(levels, out):
        state = Bag()

        def step(level):
            if level:
                state.copy.wait_recv()
                levels[level] = levels[level] + levels[level - 1]
            if level < len(peers):
                state.copy = push(levels.at[level], levels.at[level + 1], peers[level])
            else:
                out(levels[level])

        links = [LINK_CORE, LINK_X, LINK_Y] + [LINK_Z] * (dp_bits - 1) + [None]
        return [(lambda n=n: step(n), link, 1.5) for n, link in enumerate(links)]

    def store_small(value):
        narrow = jnp.zeros(r.gnarrow.shape, f32)
        bias = jnp.zeros(r.gbias.shape, f32)
        for m in range(blocks):
            narrow += jnp.where(mp == m, value[:, m * block : (m + 1) * block], 0.0)
            bias += jnp.where(mp == m, value[ROW_B_UP + m : ROW_B_UP + m + 1, :], 0.0)
        r.gnarrow[...] = narrow
        r.gbias[...] = bias

    def wave_sum():
        copies = []

        def over_mp():
            for peer, _ in others:
                copies.append(push(r.wave_parts.at[mp], r.wave_parts.at[mp], peer))

        def over_dp():
            for copy in copies:
                copy.wait_recv()
            copies.clear()
            r.wave_chips[dp] = sum(r.wave_parts[m] for m in range(blocks))
            for peer in bit_peer + mixed:
                copies.append(push(r.wave_chips.at[dp], r.wave_chips.at[dp], peer))

        def end():
            for copy in copies:
                copy.wait_recv()
            r.gwave[...] = sum(r.wave_chips[d] for d in range(1 << dp_bits))

        return [(over_mp, LINK_SMALL, 1.0), (over_dp, LINK_SMALL, 3.0), (end, None, 0.0)]

    clock.add(all_sum(r.small_sums, store_small))
    def pixel_gradient():
        pixel_back = [nt_dot(tokens[i], r.patch[i]).astype(bf16) for i in range(images)]
        for m in range(blocks):
            r.pixel_send[m] = packed(pixel_back, m, depth // blocks)

        def pixel_begin():
            for peer, m in others:
                out_copies.append(push(r.pixel_send.at[m], r.pixel_grad.at[mp], peer))

        clock.add([(pixel_begin, LINK_X, 0.28 / RATE)], at=clock.now)
        pixel_own = carry_local(r.pixel_send.at[mp], r.pixel_grad.at[mp])
        clock.work(1.5)
        return pixel_own

    def chunks_ready(count):
        while len(wide_flows) < tiles + count:
            wide_flow(len(wide_flows))

    def weight_rows(t, source):
        for j in range(tiles):
            cols = slice(j * TILE, (j + 1) * TILE)
            store_rows(t, j, tn_dot(r.qkv[source, :, cols], r.normed_one[...]))
            clock.work(0.8)
        chunks_ready((t + 1) * block // TILE)

    if inside:
        def sensor_sums():
            r.total[...] = jnp.zeros_like(r.total)
            r.back[...] = jnp.zeros_like(r.back)
            lane_block = lax.broadcasted_iota(jnp.int32, (1, width), 1) // block
            for m in range(blocks):
                for i in range(images):
                    c = m * images + i
                    part = r.token_recv[m, :, i * block : (i + 1) * block]
                    part = tn_dot(r.chosen[c], jnp.concatenate([part] * blocks, axis=1))
                    tag = r.tags[c]
                    r.total[0:depth, :] += jnp.where(lane_block == tag, part, 0.0)
                    r.back[0:depth, :] += jnp.where(lane_block + blocks == tag, part, 0.0)
                    clock.work(0.7)

            for flow in up_flows:
                clock.ensure(flow, 2)

            def slot_of(d):
                return tuple((d >> b) % 2 for b in KERNEL_ORDER)

            for s in range(sensors):
                store = r.total if s < blocks else r.back
                part = store[0:depth, s % blocks * block : (s % blocks + 1) * block]
                for d in range(slots):
                    strips = [
                        part[(b * slots + d) * pixels_each : (b * slots + d + 1) * pixels_each]
                        for b in range(bands)
                    ]
                    line = slice(s * piece_rows, (s + 1) * piece_rows)
                    r.work_up[(*slot_of(d), line, slice(0, block))] = jnp.concatenate(
                        strips, axis=0
                    ).astype(bf16)
            clock.work(1.0)

        cut = 3 * piece_rows

        def kernel_flow(half):
            here = Bag()
            order = KERNEL_ORDER
            lines = slice(cut, sensors * piece_rows) if half else slice(0, cut)

            def source(level):
                if level == 0:
                    return r.work_up.at[:, :, :, lines, :]
                return r[KERNEL + level - 1].at[(slice(None),) * (3 - level) + (lines,)]

            def step(level):
                if level:
                    target = source(level)
                    here.copy.wait_recv()
                    target[...] = target[...] + source(level - 1)[dp_bit[order[level - 1]]]
                if level < 3:
                    give = source(level).at[1 - dp_bit[order[level]]]
                    here.copy = push(give, source(level + 1), bit_peer[order[level]])
                    return
                state.shares.append(half)
                if len(state.shares) == 2:
                    kernel_end()

            steps = []
            for n, b in enumerate(order):
                cost = (0.69, 0.34, 0.17)[n] / 2 * (2 if b == 2 else 1) / RATE
                steps.append((lambda n=n: step(n), LINK_Z if b else LINK_Y, cost))
            return steps + [(lambda: step(3), None, 0.0)]

        def kernel_end():
            flat = r[KERNEL + dp_bits - 1][:, 0:block]
            r.share[...] = flat.astype(f32).reshape(r.share.shape)
            line = lax.broadcasted_iota(jnp.int32, (sensors * piece_rows, HYP), 0)
            wave = jnp.zeros((sensors * piece_rows, HYP), f32)
            for p in range(pixels_each):
                part = nn_dot(flat, r.w_kernel[p])
                wave = wave + jnp.where(line % pixels_each == p, part, 0.0)
            wave = jnp.sum(wave.reshape(sensors * bands, pixels_each, HYP), axis=1)
            r.wave_parts[mp] = wave
            clock.add(wave_sum())

        def sensor_stage():
            clock.ensure(token_flow, 2)
            sensor_sums()
            state.shares = []
            for half in range(2):
                clock.add(kernel_flow(half))

    else:

        def sensor_stage():
            clock.ensure(token_flow, 2)
            r.token_out[...] = r.token_recv[...]
            r.chosen_out[...] = r.chosen[...]

    for n, (t, source) in enumerate(((1, 2), (2, 0), (3, 1))):
        if PIXELS_AT == n:
            pixel_own = pixel_gradient()
        if SENSORS_AT == n:
            sensor_stage()
        weight_rows(t, source)
    if PIXELS_AT == 3:
        pixel_own = pixel_gradient()
    if SENSORS_AT == 3:
        sensor_stage()

    clock.drain()
    pixel_own.wait()
    for copy in out_copies:
        copy.wait_recv()
    for copy in sent:
        copy.wait_send()


def layer(length, dp_bits, inside, scalars, arrays, distant):
    piece, pixels = arrays["piece"], distant["pixels"]
    rows = -(-length // ROW_TILE) * ROW_TILE
    chips, patches, depth = pixels.shape
    block, width = distant["wout_shard"].shape
    blocks = width // block
    images = chips // blocks
    total = images * rows
    steps = images * width // LANES
    tiles = width // TILE
    halves = min(HALVES, dp_bits)

    def vmem(*size, kind=bf16):
        return pltpu.VMEM(size, kind)

    anywhere = pl.BlockSpec(memory_space=pl.ANY)
    near = pl.BlockSpec(memory_space=pltpu.VMEM)
    scalar = pl.BlockSpec(memory_space=pltpu.SMEM)
    names, operands, in_specs = list(scalars), list(scalars.values()), [scalar] * len(scalars)
    for group, spec in ((arrays, near), (distant, anywhere)):
        names += list(group)
        operands += list(group.values())
        in_specs += [spec] * len(group)

    outs = dict(
        encoded=((blocks, rows, images * block), bf16, anywhere),
        pixel_grad=((blocks, rows, images * depth // blocks), bf16, anywhere),
        gnarrow=((SMALL_ROWS, block), f32, near),
        gbias=((1, width), f32, near),
        fin_down=((tiles, TILE, width), bf16, anywhere),
        fin_inner=((tiles, TILE, width), bf16, anywhere),
        fin_up=((width, width), bf16, anywhere),
    )
    if inside:
        sensors, piece_rows, _ = piece.shape
        outs.update(share=(piece.shape, f32, near))
        bands = piece_rows // arrays["w_kernel"].shape[0]
        outs.update(gwave=((sensors * bands, HYP), f32, near))
    else:
        outs.update(token_out=((blocks, rows, images * block), bf16, near))
        outs.update(chosen_out=((chips, rows, depth), bf16, near))
    results = list(outs)
    outs.update(wup=((blocks, width, width), bf16, anywhere))
    outs.update(wdown=((blocks, width, width), bf16, anywhere))
    outs.update(soft=((steps, 2, rows, rows), bf16, anywhere))

    scratch = dict(
        index=vmem(rows, chips, kind=jnp.int32),
        narrow=vmem(SMALL_ROWS, block, kind=f32),
        bias_up=vmem(8, width, kind=f32),
        narrow_all=vmem(blocks, SMALL_ROWS, block, kind=f32),
        bias_all=vmem(blocks, 8, width, kind=f32),
        small=vmem(SMALL_ROWS, width, kind=f32),
        grad_recv=vmem(blocks, rows, images * block),
        grad=vmem(total, width),
        chosen=vmem(chips, rows, depth),
        start=vmem(total, width, kind=f32),
        middle=vmem(total, width, kind=f32),
        normed_one=vmem(total, width),
        normed_two=vmem(total, width),
        normed_flip=vmem(width, total),
        qkv=vmem(3, total, width),
        attended=vmem(total, width),
        total=vmem(total, width, kind=f32),
        back=vmem(total, width, kind=f32),
        wqkv=vmem(3, width, width),
        wout=vmem(width, width),
        up_slots=vmem(2, width, TILE),
        down_slots=vmem(2, TILE, width),
        soft_slots=vmem(2, 2, rows, rows),
        small_sums=vmem(3 + dp_bits, SMALL_ROWS, width, kind=f32),
        work_wide=vmem(2, 2, 2, TILE, width),
        work_up=vmem(2, 2, 2, width, TILE),
        token_recv=vmem(blocks, rows, images * block),
        pixel_send=vmem(blocks, rows, images * depth // blocks),
    )
    if inside:
        scratch.update(kernels_near=vmem(1 << (dp_bits - 1), *piece.shape))
        scratch.update(kernels_far=vmem(1 << (dp_bits - 1), *piece.shape))
        for n in range(dp_bits):
            lead = (2,) * (dp_bits - 1 - n)
            scratch[KERNEL + n] = vmem(*lead, sensors * piece_rows, TILE)
        scratch.update(patch_send=vmem(blocks, 2, depth // 2, images * block))
        scratch.update(patch_recv=vmem(blocks, 2, depth // 2, images * block))
        scratch.update(encoded_send=vmem(blocks, rows, images * block))
        scratch.update(patch=vmem(images, depth, width))
        scratch.update(wave_parts=vmem(blocks, sensors * bands, HYP, kind=f32))
        scratch.update(wave_chips=vmem(1 << dp_bits, sensors * bands, HYP, kind=f32))
    else:
        scratch.update(encoded_send=vmem(blocks, rows, images * block))
        scratch.update(token_send=vmem(blocks, rows, images * block))
    for base, amount, high, wide in ((WIDE, 2 * tiles, TILE, width), (UP, tiles, width, TILE)):
        for chunk in range(amount):
            along = order_of(dp_bits, chunk in (LATE_UP if base == UP else LATE_WIDE))
            scratch[base + 10 * chunk] = vmem(2, high, wide)
            lead, now, cut = (2,), high, 0
            for n, stage in enumerate(along):
                if stage == ACROSS:
                    lead = ()
                elif cut < halves:
                    now, cut = now // 2, cut + 1
                scratch[base + 10 * chunk + 1 + n] = vmem(*lead, now, wide)
    copies = 36 + 9 * (2 + dp_bits + halves) + 2 * (2 + dp_bits) + 32 + dp_bits
    dma = pltpu.SemaphoreType.DMA
    scratch.update(local_sems=dma((24,)))
    scratch.update(send_sems=dma((copies,)))
    scratch.update(recv_sems=dma((copies,)))
    scratch.update(slot_sems=dma((2, 2)))
    scratch.update(soft_sems=dma((2, 2)))
    scratch.update(pixel_sems=dma((2, patches // TILE)))

    names += [*outs, *scratch]

    def kernel(*refs):
        labels, refs = list(names), list(refs)
        twice = dict(branch="grad", gattended="normed_two")
        if inside:
            twice.update(token_send="encoded_send")
        for second, first in twice.items():
            labels.append(second)
            refs.append(refs[names.index(first)])
        layer_kernel(labels, length, dp_bits, inside, *refs)

    values = pl.pallas_call(
        kernel,
        in_specs=in_specs,
        out_specs=[spec for _, _, spec in outs.values()],
        out_shape=[jax.ShapeDtypeStruct(size, kind) for size, kind, _ in outs.values()],
        scratch_shapes=list(scratch.values()),
        compiler_params=pltpu.CompilerParams(
            vmem_limit_bytes=VMEM_LIMIT,
            fuse_transposed_lhs_in_matmul=True,
            collective_id=0,
            has_side_effects=True,
        ),
        name="layer",
    )(*operands)
    return Refs(outs, values)


def per_device(
    dp_bits,
    pixels,
    meta,
    tags,
    visible,
    wavelength,
    w_hyp,
    b_hyp,
    w_kernel,
    w_meta,
    cls_token,
    ln1_gain,
    ln1_bias,
    w_qkv,
    b_qv,
    w_out,
    b_out,
    ln2_gain,
    ln2_bias,
    w_up,
    b_up,
    w_down,
    b_down,
    cotangent,
):
    width = w_qkv.shape[0]
    block = cls_token.shape[0]
    blocks = width // block
    sensors, bands = wavelength.shape
    chips, patches, depth = pixels.shape
    pixels_each = w_kernel.shape[1]
    length = visible.shape[1] + 2
    rows = -(-length // ROW_TILE) * ROW_TILE
    images = chips // blocks
    inside = dp_bits == 3 and bands * pixels_each % ROW_TILE == 0

    wave_table = wave_code(wavelength)
    wave_pre = jnp.einsum("sbi,ij->sbj", wave_table, w_hyp, precision=highest) + b_hyp
    wave_hidden, wave_back = jax.vjp(jax.nn.gelu, wave_pre)
    wave_low = wave_hidden.astype(bf16)
    kernel = jnp.einsum("sbj,jpf->sbpf", wave_low, w_kernel, preferred_element_type=f32)
    kernel = kernel.astype(bf16)

    scalars = dict(meta=meta, tags=tags)
    arrays = dict(
        piece=kernel.reshape(sensors, bands * pixels_each, block),
        w_meta=w_meta,
        cls=cls_token[None],
        gain_one=ln1_gain[None],
        bias_one=ln1_bias[None],
        b_qv=b_qv,
        b_out=b_out[None],
        gain_two=ln2_gain[None],
        bias_two=ln2_bias[None],
        b_down=b_down[None],
        b_up=b_up,
        w_kernel=w_kernel.transpose(1, 2, 0),
        visible=visible,
        grad_rows=cotangent.transpose(1, 0, 2),
    )
    distant = dict(
        pixels=pixels,
        table=jnp.asarray(pos_table(patches, width)),
        wqkv_shard=w_qkv.transpose(1, 2, 0),
        wout_shard=w_out,
        wup_shard=w_up,
        wdown_shard=w_down,
    )
    if not inside:
        kernel = lax.all_gather(kernel, "dp", axis=2, tiled=True)
        kernel = kernel.reshape(sensors, depth, block)
        arrays.update(patch=lax.all_to_all(kernel[tags], "mp", 0, 2, tiled=True))
    got = layer(length, dp_bits, inside, scalars, arrays, distant)

    def unpack(value, size):
        value = value.reshape(blocks, rows, images, size).transpose(0, 2, 1, 3)
        return value.reshape(chips, rows, size)

    encoded = unpack(got.encoded, block)[:, :length]
    pixel_grad = unpack(got.pixel_grad, depth // blocks)[:, 2:length]
    wave_float = wave_low.astype(f32)
    if inside:
        share = got.share.reshape(sensors, bands, pixels_each, block)
        grad_wave = got.gwave.reshape(sensors, bands, HYP)
    else:
        select = (tags[:, None] == jnp.arange(sensors, dtype=jnp.int32)[None, :]).astype(f32)
        token_grad = unpack(got.token_out, block)
        chip_grad = jnp.einsum(
            "cvk,cvf->ckf", got.chosen_out, token_grad, preferred_element_type=f32
        )
        share = jnp.einsum("cs,ckf->skf", select, chip_grad, precision=highest)
        share = share.reshape(sensors, bands, depth // bands, block)
        share = lax.psum_scatter(share, "dp", scatter_dimension=2, tiled=True)
        grad_wave = lax.psum(
            jnp.einsum("sbpf,jpf->sbj", share, w_kernel.astype(f32), precision=highest),
            ("dp", "mp"),
        )
    grad_w_kernel = jnp.einsum("sbj,sbpf->jpf", wave_float, share, precision=highest)
    grad_pre = wave_back(grad_wave)[0]
    grad_w_hyp = jnp.einsum("sbi,sbj->ij", wave_table, grad_pre, precision=highest)
    grad_b_hyp = jnp.sum(grad_pre, axis=(0, 1))

    gdown = got.fin_down.reshape(width, width).astype(f32)
    gup = got.fin_up.astype(f32)
    inner = got.fin_inner.reshape(4, block, width)
    gout = inner[0].astype(f32)
    gqkv = jnp.stack([inner[2], inner[3], inner[1]]).transpose(2, 0, 1).astype(f32)
    gnarrow = got.gnarrow
    return (
        encoded,
        pixel_grad,
        grad_w_hyp,
        grad_b_hyp,
        grad_w_kernel,
        gnarrow[ROW_META : ROW_META + w_meta.shape[0]],
        gnarrow[ROW_CLS],
        gnarrow[ROW_LN1_GAIN],
        gnarrow[ROW_LN1_BIAS],
        gqkv,
        gnarrow[ROW_BQ : ROW_BV + 1],
        gout,
        gnarrow[ROW_B_OUT],
        gnarrow[ROW_LN2_GAIN],
        gnarrow[ROW_LN2_BIAS],
        gup,
        got.gbias[0],
        gdown,
        gnarrow[ROW_B_DOWN],
    )


def solution(mesh):
    dp_bits = mesh.shape["dp"].bit_length() - 1
    return jax.shard_map(
        functools.partial(per_device, dp_bits),
        mesh=mesh,
        in_specs=(
            P("dp", None, None),
            P("dp", None),
            P("dp"),
            P("dp", None),
            P(),
            P(),
            P(),
            P(None, "dp", "mp"),
            P(None, "mp"),
            P("mp"),
            P("mp"),
            P("mp"),
            P(None, None, "mp"),
            P(None, "mp"),
            P("mp", None),
            P("mp"),
            P("mp"),
            P("mp"),
            P(None, "mp"),
            P("mp"),
            P("mp", None),
            P("mp"),
            P("dp", None, "mp"),
        ),
        out_specs=(
            P("dp", None, "mp"),
            P("dp", None, "mp"),
            P(),
            P(),
            P(None, "dp", "mp"),
            P(None, "mp"),
            P("mp"),
            P("mp"),
            P("mp"),
            P(None, None, "mp"),
            P(None, "mp"),
            P("mp", None),
            P("mp"),
            P("mp"),
            P("mp"),
            P(None, "mp"),
            P("mp"),
            P("mp", None),
            P("mp"),
        ),
        check_vma=False,
    )
```
